32 devices in a mesh: dp: 8 (over y, x, core), rows: 4 (over z).
Axes of the slice: x: 2, y: 2, z: 4, core: 2. Of those that a mesh axis runs over, the one named last changes fastest.
Arguments:
- tokens: bfloat16 [32768, 768], P(('dp', 'rows')), may hold values from -6 to 6
- segment_ids: int32 [32768], P(('dp', 'rows')), may hold values from 0 to 8, as said below
- true_counts: int32 [32], P(('dp', 'rows')), may hold values from 213 to 1024, as said below
- regroup: int32 [32], P(('dp', 'rows')), may hold values from 0 to 31, as said below
- cotangent: bfloat16 [32768, 768], P(('dp', 'rows')), may hold values from -12 to 12
- ln1_gain: float32 [768], replicated, may hold values from 0.5 to 1.5
- ln1_bias: float32 [768], replicated, may hold values from -1.75 to 1.75
- qkv_weight: bfloat16 [768, 2304], replicated, may hold values from -0.21875 to 0.21875
- qkv_bias: float32 [2304], replicated, may hold values from -1.75 to 1.75
- out_weight: bfloat16 [768, 768], replicated, may hold values from -1.5 to 1.5
- out_bias: float32 [768], replicated, may hold values from -1.75 to 1.75
- ln2_gain: float32 [768], replicated, may hold values from 0.5 to 1.5
- ln2_bias: float32 [768], replicated, may hold values from -1.75 to 1.75
- up_weight: bfloat16 [768, 3072], replicated, may hold values from -0.21875 to 0.21875
- up_bias: float32 [3072], replicated, may hold values from -1.75 to 1.75
- down_weight: bfloat16 [3072, 768], replicated, may hold values from -0.109375 to 0.109375
- down_bias: float32 [768], replicated, may hold values from -1.75 to 1.75
Outputs:
- out: bfloat16 [32768, 768], P(('dp', 'rows'))
- input_grad: bfloat16 [32768, 768], P(('dp', 'rows'))
- grad_ln1_gain: float32 [768], replicated
- grad_ln1_bias: float32 [768], replicated
- grad_qkv_weight: float32 [768, 2304], P('dp')
- grad_qkv_bias: float32 [2304], replicated
- grad_out_weight: float32 [768, 768], P('dp')
- grad_out_bias: float32 [768], replicated
- grad_ln2_gain: float32 [768], replicated
- grad_ln2_bias: float32 [768], replicated
- grad_up_weight: float32 [768, 3072], P('dp')
- grad_up_bias: float32 [3072], replicated
- grad_down_weight: float32 [3072, 768], P(None, 'dp')
- grad_down_bias: float32 [768], replicated
The draws below stay inside these ranges and needn't reach their ends.
Inputs may be any that keep to these rules, and one draw needn't show every extreme that they name: `true_counts`: true tokens of each row; they fill its first positions, and some row is full. `segment_ids`: positions of a row carry cells 0 to 7 in order, each of 1 or more tokens, together filling the row's true count, then 8 on all padding positions. `regroup`: a permutation of the rows that maps every aligned block of 4 rows onto itself.
All inputs are finite; a program needn't handle non-finite values.
Results may differ from the reference program's by a relative error of at most 0.01.
Values may be sent and summed in bfloat16 or wider, within the bound.
A program may use at most 256 MiB of HBM per device.

```python
import jax
import jax.numpy as jnp
from jax import lax

D = 768
HEAD_DIM = 64
ROT = 16
FF = 3072
ROW_LEN = 1024
SEGS = 8
BUCKETS = 8
GROUP = 4
ROWS_ALL = 32
TOKENS = 32768


def row_layout(key):
    rows_index = jnp.arange(ROWS_ALL, dtype=jnp.int32)
    bucket = rows_index // GROUP
    base_count = ROW_LEN // 3 + (ROW_LEN - ROW_LEN // 3) * bucket // (BUCKETS - 1)
    jitter = jax.random.randint(jax.random.fold_in(key, 101), (ROWS_ALL,), 0, ROW_LEN // 8 + 1, dtype=jnp.int32)
    counts_all = jnp.where(rows_index == ROWS_ALL - 1, ROW_LEN, base_count - jitter).astype(jnp.int32)
    shares = jax.random.randint(jax.random.fold_in(key, 102), (ROWS_ALL, SEGS), 1, 9, dtype=jnp.int32)
    running = jnp.cumsum(shares, axis=1).astype(jnp.int32)
    spare = (counts_all - SEGS)[:, None]
    ending = spare * running // running[:, -1:]
    before = jnp.concatenate([jnp.zeros((ROWS_ALL, 1), jnp.int32), ending[:, :-1]], axis=1)
    lengths_all = (1 + ending - before).astype(jnp.int32)
    return (counts_all, lengths_all)


def draw_true_counts(key, part):
    return row_layout(key)[0]


def draw_segment_ids(key, part):
    lengths_all = row_layout(key)[1]
    ending = jnp.cumsum(lengths_all, axis=1).astype(jnp.int32)
    spots = jnp.arange(ROW_LEN, dtype=jnp.int32)
    labels = jnp.sum((spots[None, :, None] >= ending[:, None, :]).astype(jnp.int32), axis=2)
    return labels.reshape(TOKENS).astype(jnp.int32)


def draw_regroup(key, part):
    scores = jax.random.randint(jax.random.fold_in(key, 103), (BUCKETS, GROUP), 0, 1 << 20, dtype=jnp.int32)
    scores = scores * GROUP + jnp.arange(GROUP, dtype=jnp.int32)[None, :]
    order = jnp.argsort(scores, axis=1).astype(jnp.int32)
    return (jnp.arange(BUCKETS, dtype=jnp.int32)[:, None] * GROUP + order).reshape(ROWS_ALL).astype(jnp.int32)


def strengthened(drawn, own_key, source, target, blocks, factor):
    def block_of(position):
        return (jnp.arange(drawn.shape[position]) // (drawn.shape[position] // blocks)).reshape((-1,) + (1,) * (drawn.ndim - 1 - position))

    one_side = jax.random.permutation(own_key, blocks)[block_of(target)]
    other_side = (block_of(target) + blocks // 2) % blocks
    return jnp.where((block_of(source) == one_side) | (block_of(source) == other_side), factor * drawn, drawn)


def block_levels(own_key, shape, cuts, smallest, high):
    level = 1.0
    for axis_at, parts in cuts:
        steps = jax.random.uniform(jax.random.fold_in(jax.random.fold_in(own_key, 6), axis_at), (parts,), jnp.float32, smallest / len(cuts), high / len(cuts))
        level = level * jnp.repeat(jnp.exp(steps), shape[axis_at] // parts).reshape((-1,) + (1,) * (len(shape) - 1 - axis_at))
    return level


def bell_draw(own_key, dims, width, most, shards=(), held_as=jnp.bfloat16):
    result = jax.random.normal(own_key, dims, jnp.float32) * width
    if len(shards) > 0:
        result = block_levels(own_key, dims, shards, -0.22, 0.18) * result
    return jnp.clip(result, min=-most, max=most).astype(held_as)


def bell_draw_with(rng, shape, width, most, split, heavy, kind=jnp.bfloat16):
    drawn = width * jax.random.normal(rng, shape, jnp.float32)
    if split:
        drawn = drawn * block_levels(rng, shape, split, -0.22, 0.18)
    return jnp.clip(strengthened(drawn, jax.random.fold_in(rng, 3), *heavy), -most, most).astype(kind)


def setup_inputs(seed: int = 0) -> dict:
    splits = jax.random.split(jax.random.key(seed), 18)
    tokens = bell_draw(splits[0], (TOKENS, D), 1.0, 6.0, ((0, 32),))
    segment_ids = draw_segment_ids(jax.random.fold_in(splits[17], 71), 0)
    true_counts = draw_true_counts(jax.random.fold_in(splits[17], 71), 0)
    regroup = draw_regroup(jax.random.fold_in(splits[17], 71), 0)
    cotangent = bell_draw_with(splits[4], (TOKENS, D), 1.0, 12.0, ((0, 32),), (0, 1, 32, 2.75))
    ln1_gain = jnp.clip(1.0 + 0.1 * jax.random.normal(splits[5], (D,), jnp.float32), 0.5, 1.5)
    ln1_bias = bell_draw(splits[6], (D,), 0.3, 1.75, (), jnp.float32)
    qkv_weight = bell_draw(splits[7], (D, 3 * D), D ** -0.5, 0.21875)
    qkv_bias = bell_draw(splits[8], (3 * D,), 0.3, 1.75, (), jnp.float32)
    out_weight = bell_draw(splits[9], (D, D), (D // 48) ** -0.5, 1.5)
    out_bias = bell_draw(splits[10], (D,), 0.3, 1.75, (), jnp.float32)
    ln2_gain = jnp.clip(1.0 + 0.1 * jax.random.normal(splits[11], (D,), jnp.float32), 0.5, 1.5)
    ln2_bias = bell_draw(splits[12], (D,), 0.3, 1.75, (), jnp.float32)
    up_weight = bell_draw(splits[13], (D, FF), D ** -0.5, 0.21875)
    up_bias = bell_draw(splits[14], (FF,), 0.3, 1.75, (), jnp.float32)
    down_weight = bell_draw(splits[15], (FF, D), FF ** -0.5, 0.109375)
    down_bias = bell_draw(splits[16], (D,), 0.3, 1.75, (), jnp.float32)
    return {"tokens": tokens, "segment_ids": segment_ids, "true_counts": true_counts, "regroup": regroup, "cotangent": cotangent, "ln1_gain": ln1_gain, "ln1_bias": ln1_bias, "qkv_weight": qkv_weight, "qkv_bias": qkv_bias, "out_weight": out_weight, "out_bias": out_bias, "ln2_gain": ln2_gain, "ln2_bias": ln2_bias, "up_weight": up_weight, "up_bias": up_bias, "down_weight": down_weight, "down_bias": down_bias}


HIGHEST = lax.Precision.HIGHEST
EPSILON = 1e-05
EXCLUDED = -1e+30

@jax.custom_vjp
def low(v):
    return lax.optimization_barrier(v.astype(jnp.bfloat16)).astype(jnp.float32)

@jax.custom_vjp
def low_back(v):
    return v

def low_keep(v):
    return (low(v), None)

def low_pass(kept, grad):
    return (grad,)

def back_keep(v):
    return (v, None)

def back_low(kept, grad):
    return (low(grad),)
low.defvjp(low_keep, low_pass)
low_back.defvjp(back_keep, back_low)

def matmul(left, right):
    return jnp.dot(left, right, precision=HIGHEST, preferred_element_type=jnp.float32)

def layer_norm(tensor, scales, shifts):
    centre = lax.optimization_barrier(jnp.mean(tensor, axis=-1, keepdims=True))
    centred = tensor - centre
    spread = lax.optimization_barrier(jnp.mean(centred * centred, axis=-1, keepdims=True))
    return centred * lax.rsqrt(spread + EPSILON) * scales + shifts

def rotate(tensor, cosine, sine_table):
    halfway = ROT // 2
    moving = tensor[..., :ROT]
    turned = jnp.concatenate([-moving[..., halfway:], moving[..., :halfway]], axis=-1)
    return jnp.concatenate([moving * cosine + turned * sine_table, tensor[..., ROT:]], axis=-1)

def angles(length):
    placed = jnp.arange(length, dtype=jnp.int32).astype(jnp.float32)
    rates = jnp.exp(jnp.arange(ROT // 2, dtype=jnp.float32) * (-2.0 / ROT) * jnp.log(jnp.float32(10000.0)))
    phases = placed[:, None] * rates[None, :]
    phases = jnp.concatenate([phases, phases], axis=1)
    return (jnp.cos(phases)[:, None, :], jnp.sin(phases)[:, None, :])

def attend(query_heads, key_heads, value_heads, segment):
    length = segment.shape[0]
    span_rows = min(512, length)
    positions = jnp.arange(length, dtype=jnp.int32)

    def one_block(begin_row):
        rows_query = lax.dynamic_slice_in_dim(query_heads, begin_row, span_rows, 0)
        rows_segment = lax.dynamic_slice_in_dim(segment, begin_row, span_rows, 0)
        rows_place = lax.dynamic_slice_in_dim(positions, begin_row, span_rows, 0)
        scores = low_back(jnp.einsum('qhe,khe->hqk', rows_query, key_heads, precision=HIGHEST) * HEAD_DIM ** (-0.5))
        allowed = (rows_segment[:, None] == segment[None, :]) & (positions[None, :] <= rows_place[:, None])
        scores = jnp.where(allowed[None], scores, EXCLUDED)
        row_peak = lax.optimization_barrier(jnp.max(scores, axis=-1, keepdims=True))
        raised = jnp.exp(scores - row_peak)
        weights_soft = low(raised / lax.optimization_barrier(jnp.sum(raised, axis=-1, keepdims=True)))
        return jnp.einsum('hqk,khe->qhe', weights_soft, value_heads, precision=HIGHEST)
    begin_rows = jnp.arange(length // span_rows, dtype=jnp.int32) * span_rows
    return lax.map(jax.checkpoint(one_block), begin_rows).reshape(length, -1)

def forward(tokens_row, params, cosine, sine_table, segment):
    gain_one, shift_one, w_qkv, b_qkv, w_out, b_out, gain_two, shift_two, w_up, b_up, w_down, b_down = params
    length = tokens_row.shape[0]
    model_width = w_out.shape[0]
    head_shape = (length, model_width // HEAD_DIM, HEAD_DIM)
    normed_one = low(layer_norm(tokens_row, gain_one, shift_one))
    united_proj = low_back(matmul(normed_one, w_qkv) + b_qkv)
    query_heads = low(rotate(united_proj[:, :model_width].reshape(head_shape), cosine, sine_table))
    key_heads = low(rotate(united_proj[:, model_width:2 * model_width].reshape(head_shape), cosine, sine_table))
    value_heads = low(united_proj[:, 2 * model_width:].reshape(head_shape))
    context = low_back(low(attend(query_heads, key_heads, value_heads, segment)))
    attn_out = low_back(matmul(context, w_out) + b_out)
    normed_two = low(layer_norm(tokens_row, gain_two, shift_two))
    hidden = low_back(matmul(normed_two, w_up) + b_up)
    active = low(jax.nn.gelu(hidden, approximate=False))
    mlp_out = low_back(matmul(active, w_down) + b_down)
    return tokens_row + attn_out + mlp_out

def reference(tokens, segment_ids, true_counts, regroup, cotangent, ln1_gain, ln1_bias, qkv_weight, qkv_bias, out_weight, out_bias, ln2_gain, ln2_bias, up_weight, up_bias, down_weight, down_bias):
    params = tuple((member.astype(jnp.float32) for member in (ln1_gain, ln1_bias, qkv_weight, qkv_bias, out_weight, out_bias, ln2_gain, ln2_bias, up_weight, up_bias, down_weight, down_bias)))
    arrived = tokens.reshape(ROWS_ALL, ROW_LEN, D)[regroup].astype(jnp.float32)
    segments = segment_ids.reshape(ROWS_ALL, ROW_LEN)
    cosine, sine_table = angles(ROW_LEN)
    live_mask = (jnp.arange(ROW_LEN, dtype=jnp.int32)[None, :] < true_counts[:, None]).astype(jnp.float32)
    grad_out = cotangent.reshape(ROWS_ALL, ROW_LEN, D).astype(jnp.float32) * live_mask[:, :, None]
    rounds = ROWS_ALL // GROUP

    def grouped(array):
        return array.reshape((rounds, GROUP) + array.shape[1:])

    def one_round(totals, inputs):
        rows_in, seg_in, grad_in = inputs

        def layer_run(tokens_in, weights_in):
            return jax.vmap(forward, in_axes=(0, None, None, None, 0))(tokens_in, weights_in, cosine, sine_table, seg_in)
        layer_out, pull_back = jax.vjp(layer_run, rows_in, params)
        grad_tokens, grad_params = pull_back(grad_in)
        totals = jax.tree.map(lambda a, b: a + b, totals, grad_params)
        return (totals, (layer_out.astype(jnp.bfloat16), grad_tokens.astype(jnp.bfloat16)))
    initial = tuple((jnp.zeros_like(member) for member in params))
    grad_sums, (outputs, input_grads) = lax.scan(one_round, initial, (grouped(arrived), grouped(segments), grouped(grad_out)))
    token_total = jnp.sum(true_counts).astype(jnp.float32)
    means = tuple((member / token_total for member in grad_sums))
    return (outputs.reshape(TOKENS, D), input_grads.reshape(TOKENS, D), means[0], means[1], means[2], means[3], means[4], means[5], means[6], means[7], means[8], means[9], means[10], means[11])
```

```python
import functools
import numpy as np
import jax
import jax.numpy as jnp
from jax import lax
from jax.experimental import pallas as pl
from jax.experimental.pallas import tpu as pltpu
from jax.sharding import PartitionSpec as P

HEAD_DIM = 64
ROT = 16
PAIR = 128
EPSILON = 1e-05
EXCLUDED = -1e30
F32 = jnp.float32
BF16 = jnp.bfloat16


def nn(a, b):
    return lax.dot_general(a, b, (((1,), (0,)), ((), ())), preferred_element_type=F32)


def nt(a, b):
    return lax.dot_general(a, b, (((1,), (1,)), ((), ())), preferred_element_type=F32)


def tn(a, b):
    return lax.dot_general(a, b, (((0,), (0,)), ((), ())), preferred_element_type=F32)


def rotary_tables(length):
    half = ROT // 2
    placed = np.arange(length, dtype=np.float32)
    rates = np.exp(np.arange(half, dtype=np.float32) * np.float32(-2.0 / ROT) * np.log(np.float32(10000.0)))
    phases = placed[:, None] * rates[None, :].astype(np.float32)
    cosine = np.ones((length, HEAD_DIM), np.float32)
    sine = np.zeros((length, HEAD_DIM), np.float32)
    cosine[:, :half] = np.cos(phases)
    cosine[:, half:ROT] = np.cos(phases)
    sine[:, :half] = -np.sin(phases)
    sine[:, half:ROT] = np.sin(phases)
    return np.tile(cosine, (1, PAIR // HEAD_DIM)), np.tile(sine, (1, PAIR // HEAD_DIM))


def turned(u):
    lane = lax.broadcasted_iota(jnp.int32, u.shape, 1) % HEAD_DIM
    half = ROT // 2
    return jnp.where(lane < half, pltpu.roll(u, PAIR - half, 1), pltpu.roll(u, half, 1))


def gelu_parts(h):
    e = jnp.exp(h * h * -0.5)
    t = 1.0 / (1.0 + 0.2316418882 * jnp.abs(h))
    poly = t * (0.127414796 + t * (-0.142248368 + t * (0.7107068705 + t * (-0.7265760135 + t * 0.5307027145))))
    tail = poly * e
    phi = jnp.where(h >= 0, 1.0 - tail, tail)
    return h * phi, phi + h * (e * 0.3989422804014327)


def front_body(count_ref, x_ref, cot_ref, cos_ref, sin_ref, g1_ref, b1_ref, wqkv_ref, bqkv_ref, wout_ref, bout_ref,
               g2_ref, b2_ref, wup_ref, bup_ref, wdown_ref, bdown_ref,
               q_ref, k_ref, v_ref, gc_ref, n1_ref, n2_ref, gl_ref, act_ref, gh_ref, base_ref, t2_ref,
               gain2_ref, shift2_ref, bup_out, bout_out, *, tile):
    step = pl.program_id(0)
    rows, width = x_ref.shape
    pairs = width // PAIR
    ff = wup_ref.shape[1]
    x = x_ref[...].astype(F32)
    centred = x - jnp.mean(x, axis=1, keepdims=True)
    r = lax.rsqrt(jnp.mean(centred * centred, axis=1, keepdims=True) + EPSILON)
    n = centred * r
    n1 = (n * g1_ref[...] + b1_ref[...]).astype(BF16)
    n2 = (n * g2_ref[...] + b2_ref[...]).astype(BF16)
    n1_ref[...] = n1
    n2_ref[...] = n2
    place = step * rows + lax.broadcasted_iota(jnp.int32, (rows, 1), 0)
    gl = jnp.where(place < count_ref[0], cot_ref[...].astype(F32), 0.0)
    gl16 = gl.astype(BF16)
    gl_ref[...] = gl16

    @pl.when(step == 0)
    def _():
        gain2_ref[...] = jnp.zeros_like(gain2_ref)
        shift2_ref[...] = jnp.zeros_like(shift2_ref)
        bup_out[...] = jnp.zeros_like(bup_out)
        bout_out[...] = jnp.zeros_like(bout_out)

    bout_out[...] += jnp.sum(gl, axis=0, keepdims=True)
    cosine, sine = cos_ref[...], sin_ref[...]
    for p in range(pairs):
        cols = slice(p * PAIR, (p + 1) * PAIR)
        for which, ref in enumerate((q_ref, k_ref, v_ref)):
            wide = slice(which * width + p * PAIR, which * width + (p + 1) * PAIR)
            u = nn(n1, wqkv_ref[:, wide]) + bqkv_ref[:, wide]
            if which < 2:
                u = u * cosine + turned(u) * sine
            if which == 0:
                u = u * (HEAD_DIM ** -0.5)
            ref[p] = u.astype(BF16)
        gc_ref[p] = nt(gl16, wout_ref[cols, :]).astype(BF16)
    mlp = x + (bdown_ref[...] + bout_ref[...])
    grad_two = jnp.zeros((rows, width), F32)
    for f in range(0, ff, tile):
        cols = slice(f, f + tile)
        h = nn(n2, wup_ref[:, cols]) + bup_ref[:, cols]
        ga = nt(gl16, wdown_ref[cols, :])
        a, slope = gelu_parts(h)
        a16 = a.astype(BF16)
        gh = ga * slope
        gh16 = gh.astype(BF16)
        act_ref[:, cols] = a16
        gh_ref[:, cols] = gh16
        bup_out[:, cols] += jnp.sum(gh16.astype(F32), axis=0, keepdims=True)
        mlp = mlp + nn(a16, wdown_ref[cols, :])
        grad_two = grad_two + nt(gh16, wup_ref[:, cols])
    base_ref[...] = mlp
    t2_ref[...] = grad_two * g2_ref[...]
    gain2_ref[...] += jnp.sum(grad_two * n, axis=0, keepdims=True)
    shift2_ref[...] += jnp.sum(grad_two, axis=0, keepdims=True)


def front(count, x, cot, cosine, sine, g1, b1, wqkv, bqkv, wout, bout, g2, b2, wup, bup, wdown, bdown, rows=256, tile=512):
    length, width = x.shape
    ff = wup.shape[1]
    pairs = width // PAIR
    once = pl.Buffered(1)

    def row(cols):
        return pl.BlockSpec((rows, cols), lambda i: (i, 0))

    def whole(a):
        return pl.BlockSpec(a.shape, lambda i: (0,) * a.ndim, pipeline_mode=once)

    heads = pl.BlockSpec((pairs, rows, PAIR), lambda i: (0, i, 0))

    def vec(cols):
        return pl.BlockSpec((1, cols), lambda i: (0, 0))

    vectors = [v.reshape(1, -1) for v in (g1, b1, bqkv, bout, g2, b2, bup, bdown)]
    g1, b1, bqkv, bout, g2, b2, bup, bdown = vectors
    s = jax.ShapeDtypeStruct
    return pl.pallas_call(
        functools.partial(front_body, tile=tile),
        grid=(length // rows,),
        in_specs=[pl.BlockSpec(memory_space=pltpu.SMEM), row(width), row(width), row(PAIR), row(PAIR)]
        + [whole(a) for a in (g1, b1, wqkv, bqkv, wout, bout, g2, b2, wup, bup, wdown, bdown)],
        out_specs=[heads] * 4 + [row(width)] * 3 + [row(ff)] * 2 + [row(width)] * 2 + [vec(width), vec(width), vec(ff), vec(width)],
        out_shape=[s((pairs, length, PAIR), BF16)] * 4 + [s((length, width), BF16)] * 3 + [s((length, ff), BF16)] * 2
        + [s((length, width), F32)] * 2 + [s((1, width), F32), s((1, width), F32), s((1, ff), F32), s((1, width), F32)],
        compiler_params=pltpu.CompilerParams(vmem_limit_bytes=56 * 2**20),
        name="front",
    )(count, x, cot, cosine, sine, g1, b1, wqkv, bqkv, wout, bout, g2, b2, wup, bup, wdown, bdown)


def attention_body(first_ref, q_ref, k_ref, v_ref, gc_ref, segc_ref, segr_ref, cos_ref, sin_ref,
                   ctx_ref, gq_ref, gk_ref, gv_ref, dk_acc, dv_acc, *, rows):
    length = q_ref.shape[1]
    lane = lax.broadcasted_iota(jnp.int32, (rows, PAIR), 1)
    low = lane < HEAD_DIM
    dk_acc[...] = jnp.zeros_like(dk_acc)
    dv_acc[...] = jnp.zeros_like(dv_acc)

    def block(b, blocks):
        begin = pl.multiple_of(b * rows, rows)
        start = pl.multiple_of((b + 1 - blocks) * rows, rows)
        span = blocks * rows
        q = q_ref[0, pl.ds(begin, rows), :]
        g = gc_ref[0, pl.ds(begin, rows), :]
        zero = jnp.zeros_like(q)
        q2 = jnp.concatenate([jnp.where(low, q, zero), jnp.where(low, zero, q)], axis=0)
        g2 = jnp.concatenate([jnp.where(low, g, zero), jnp.where(low, zero, g)], axis=0)
        k = k_ref[0, pl.ds(start, span), :]
        v = v_ref[0, pl.ds(start, span), :]
        segt = segc_ref[pl.ds(begin, rows), :]
        segs = segr_ref[:, pl.ds(start, span)]
        t_at = begin + lax.broadcasted_iota(jnp.int32, (rows, span), 0)
        s_at = start + lax.broadcasted_iota(jnp.int32, (rows, span), 1)
        allowed = (segt == segs) & (s_at <= t_at)
        allowed = jnp.concatenate([allowed, allowed], axis=0)
        scores = jnp.where(allowed, nt(q2, k), EXCLUDED)
        peak = jnp.max(scores, axis=1, keepdims=True)
        e = jnp.exp(scores - peak)
        p = e * (1.0 / jnp.sum(e, axis=1, keepdims=True))
        p16 = p.astype(BF16)
        c2 = nn(p16, v)
        ctx_ref[pl.ds(begin, rows), :] = jnp.where(low, c2[:rows], c2[rows:]).astype(BF16)
        dp = nt(g2, v)
        inner = jnp.sum(p * dp, axis=1, keepdims=True)
        ds16 = (p * (dp - inner)).astype(BF16)
        d2 = nn(ds16, k)
        dq = jnp.where(low, d2[:rows], d2[rows:]) * (HEAD_DIM ** -0.5)
        cosine = cos_ref[pl.ds(begin, rows), :]
        sine = sin_ref[pl.ds(begin, rows), :]
        gq_ref[pl.ds(begin, rows), :] = (dq * cosine - turned(dq) * sine).astype(BF16)
        dk_acc[pl.ds(start, span), :] += tn(ds16, q2)
        dv_acc[pl.ds(start, span), :] += tn(p16, g2)

    total = length // rows

    def loop(b, carry):
        count = b + 1 - first_ref[b]
        for blocks in range(1, total + 1):
            @pl.when(count == blocks)
            def _():
                block(b, blocks)
        return carry

    lax.fori_loop(0, total, loop, 0)
    dk = dk_acc[...]
    gk_ref[...] = (dk * cos_ref[...] - turned(dk) * sin_ref[...]).astype(BF16)
    gv_ref[...] = dv_acc[...].astype(BF16)


def attention(q, k, v, gc, segment, cosine, sine, rows=128):
    pairs, length, _ = q.shape
    total = length // rows
    begins = jnp.sum((segment[None, :] < segment[::rows, None]).astype(jnp.int32), axis=1)
    first = begins // rows
    head = pl.BlockSpec((1, length, PAIR), lambda h, *_: (h, 0, 0))
    cols = pl.BlockSpec((length, PAIR), lambda h, *_: (0, h))
    s = jax.ShapeDtypeStruct((length, pairs * PAIR), BF16)

    def whole(shape):
        return pl.BlockSpec(shape, lambda h, *_: (0, 0), pipeline_mode=pl.Buffered(1))

    return pl.pallas_call(
        functools.partial(attention_body, rows=rows),
        grid_spec=pltpu.PrefetchScalarGridSpec(
            num_scalar_prefetch=1,
            grid=(pairs,),
            in_specs=[head] * 4 + [whole((length, 1)), whole((1, length)), whole((length, PAIR)), whole((length, PAIR))],
            out_specs=[cols] * 4,
            scratch_shapes=[pltpu.VMEM((length, PAIR), F32)] * 2,
        ),
        out_shape=[s] * 4,
        compiler_params=pltpu.CompilerParams(vmem_limit_bytes=56 * 2**20),
        name="attention",
    )(first, q, k, v, gc, segment.reshape(-1, 1), segment.reshape(1, -1), cosine, sine)


def shards(tokens, segment_ids, true_counts, regroup, cotangent, ln1_gain, ln1_bias, qkv_weight, qkv_bias, out_weight,
           out_bias, ln2_gain, ln2_bias, up_weight, up_bias, down_weight, down_bias):
    length, width = cotangent.shape
    source = regroup[0] % lax.axis_size("rows")
    piece = lax.all_gather(tokens, "rows", axis=0, tiled=True)
    arrived = lax.dynamic_slice_in_dim(piece, source * length, length, 0)
    cosine, sine = (jnp.asarray(t) for t in rotary_tables(length))
    (q, k, v, gc, n1, n2, gl, act, gh, base, t2, gain2, shift2, bias_up, bias_out) = front(
        true_counts, arrived, cotangent, cosine, sine, ln1_gain, ln1_bias, qkv_weight, qkv_bias, out_weight, out_bias,
        ln2_gain, ln2_bias, up_weight, up_bias, down_weight, down_bias)
    mlp_part = jnp.concatenate([tn(n2, gh), tn(gl, act)], axis=1).astype(BF16)
    mlp_rows = lax.psum(lax.psum_scatter(mlp_part, "dp", scatter_dimension=0, tiled=True), "rows")
    ctx, gq, gk, gv = attention(q, k, v, gc, segment_ids, cosine, sine, rows=256)
    out = (base + nn(ctx, out_weight)).astype(BF16)
    gu = jnp.concatenate([gq, gk, gv], axis=1)
    g1 = nt(gu, qkv_weight)
    x = arrived.astype(F32)
    centred = x - jnp.mean(x, axis=1, keepdims=True)
    r = lax.rsqrt(jnp.mean(centred * centred, axis=1, keepdims=True) + EPSILON)
    n = centred * r
    gain1 = jnp.sum(g1 * n, axis=0)
    shift1 = jnp.sum(g1, axis=0)
    t = g1 * ln1_gain + t2
    dx = r * (t - jnp.mean(t, axis=1, keepdims=True) - n * jnp.mean(t * n, axis=1, keepdims=True))
    input_grad = (gl.astype(F32) + dx).astype(BF16)
    attn_part = jnp.concatenate([tn(n1, gu), tn(ctx, gl)], axis=1).astype(BF16)
    attn_rows = lax.psum(lax.psum_scatter(attn_part, "dp", scatter_dimension=0, tiled=True), "rows")
    bias_qkv = jnp.sum(gu, axis=0, dtype=F32)
    packed = jnp.concatenate([gain1, shift1, bias_qkv, bias_out[0], gain2[0], shift2[0], bias_up[0], true_counts.astype(F32)])
    packed = lax.psum(packed, ("dp", "rows"))
    factor = 1.0 / packed[-1]
    cuts = np.cumsum([width, width, 3 * width, width, width, width, up_weight.shape[1]])
    vec = [part * factor for part in jnp.split(packed, cuts)[:-1]]
    mlp_rows = mlp_rows.astype(F32) * factor
    attn_rows = attn_rows.astype(F32) * factor
    ff = up_weight.shape[1]
    return (out, input_grad, vec[0], vec[1], attn_rows[:, : 3 * width], vec[2], attn_rows[:, 3 * width :], vec[3], vec[4], vec[5],
            mlp_rows[:, :ff], vec[6], mlp_rows[:, ff:].T, vec[3])


def solution(mesh):
    both = ("dp", "rows")
    placed = (P(both, None), P(both), P(both), P(both), P(both, None)) + (P(),) * 12
    return jax.shard_map(
        shards, mesh=mesh, in_specs=placed,
        out_specs=(P(both, None), P(both, None), P(), P(), P("dp", None), P(), P("dp", None), P(), P(), P(), P("dp", None), P(),
                   P(None, "dp"), P()),
        check_vma=False)
```

```python
import functools
import numpy as np
import jax
import jax.numpy as jnp
from jax import lax
from jax.experimental import pallas as pl
from jax.experimental.pallas import tpu as pltpu
from jax.sharding import PartitionSpec as P

HEAD_DIM = 64
ROT = 16
PAIR = 128
EPSILON = 1e-05
EXCLUDED = -1e30
F32 = jnp.float32
BF16 = jnp.bfloat16


def nn(a, b):
    return lax.dot_general(a, b, (((1,), (0,)), ((), ())), preferred_element_type=F32)


def nt(a, b):
    return lax.dot_general(a, b, (((1,), (1,)), ((), ())), preferred_element_type=F32)


def tn(a, b):
    return lax.dot_general(a, b, (((0,), (0,)), ((), ())), preferred_element_type=F32)


def rotary_tables(length):
    half = ROT // 2
    placed = np.arange(length, dtype=np.float32)
    rates = np.exp(np.arange(half, dtype=np.float32) * np.float32(-2.0 / ROT) * np.log(np.float32(10000.0)))
    phases = placed[:, None] * rates[None, :].astype(np.float32)
    cosine = np.ones((length, HEAD_DIM), np.float32)
    sine = np.zeros((length, HEAD_DIM), np.float32)
    cosine[:, :half] = np.cos(phases)
    cosine[:, half:ROT] = np.cos(phases)
    sine[:, :half] = -np.sin(phases)
    sine[:, half:ROT] = np.sin(phases)
    return np.tile(cosine, (1, PAIR // HEAD_DIM)), np.tile(sine, (1, PAIR // HEAD_DIM))


def turned(u):
    lane = lax.broadcasted_iota(jnp.int32, u.shape, 1) % HEAD_DIM
    half = ROT // 2
    return jnp.where(lane < half, pltpu.roll(u, PAIR - half, 1), pltpu.roll(u, half, 1))


def gelu_parts(h):
    e = jnp.exp(h * h * -0.5)
    t = 1.0 / (1.0 + 0.2316418882 * jnp.abs(h))
    poly = t * (0.127414796 + t * (-0.142248368 + t * (0.7107068705 + t * (-0.7265760135 + t * 0.5307027145))))
    tail = poly * e
    phi = jnp.where(h >= 0, 1.0 - tail, tail)
    return h * phi, phi + h * (e * 0.3989422804014327)


def front_body(count_ref, x_ref, cot_ref, cos_ref, sin_ref, g1_ref, b1_ref, wqkv_ref, bqkv_ref, wout_ref, bout_ref,
               g2_ref, b2_ref, wup_ref, bup_ref, wdown_ref, bdown_ref,
               q_ref, k_ref, v_ref, gc_ref, n1t_ref, n2t_ref, glt_ref, gl_ref, act_ref, gh_ref, base_ref, t2_ref,
               gain2_ref, shift2_ref, bup_out, bout_out, *, tile):
    step = pl.program_id(0)
    rows, width = x_ref.shape
    pairs = width // PAIR
    ff = wup_ref.shape[1]
    x = x_ref[...].astype(F32)
    centred = x - jnp.mean(x, axis=1, keepdims=True)
    r = lax.rsqrt(jnp.mean(centred * centred, axis=1, keepdims=True) + EPSILON)
    n = centred * r
    n1 = (n * g1_ref[...] + b1_ref[...]).astype(BF16)
    n2 = (n * g2_ref[...] + b2_ref[...]).astype(BF16)
    n1t_ref[...] = n1.T
    n2t_ref[...] = n2.T
    place = step * rows + lax.broadcasted_iota(jnp.int32, (rows, 1), 0)
    gl = jnp.where(place < count_ref[0], cot_ref[...].astype(F32), 0.0)
    gl16 = gl.astype(BF16)
    gl_ref[...] = gl16
    glt_ref[...] = gl16.T

    @pl.when(step == 0)
    def _():
        gain2_ref[...] = jnp.zeros_like(gain2_ref)
        shift2_ref[...] = jnp.zeros_like(shift2_ref)
        bup_out[...] = jnp.zeros_like(bup_out)
        bout_out[...] = jnp.zeros_like(bout_out)

    bout_out[...] += jnp.sum(gl, axis=0, keepdims=True)
    cosine, sine = cos_ref[...], sin_ref[...]
    for p in range(pairs):
        cols = slice(p * PAIR, (p + 1) * PAIR)
        for which, ref in enumerate((q_ref, k_ref, v_ref)):
            wide = slice(which * width + p * PAIR, which * width + (p + 1) * PAIR)
            u = nn(n1, wqkv_ref[:, wide]) + bqkv_ref[:, wide]
            if which < 2:
                u = u * cosine + turned(u) * sine
            if which == 0:
                u = u * (HEAD_DIM ** -0.5)
            ref[p] = u.astype(BF16)
        gc_ref[p] = nt(gl16, wout_ref[cols, :]).astype(BF16)
    mlp = x + (bdown_ref[...] + bout_ref[...])
    grad_two = jnp.zeros((rows, width), F32)
    for f in range(0, ff, tile):
        cols = slice(f, f + tile)
        h = nn(n2, wup_ref[:, cols]) + bup_ref[:, cols]
        ga = nt(gl16, wdown_ref[cols, :])
        a, slope = gelu_parts(h)
        a16 = a.astype(BF16)
        gh = ga * slope
        gh16 = gh.astype(BF16)
        act_ref[:, cols] = a16
        gh_ref[:, cols] = gh16
        bup_out[:, cols] += jnp.sum(gh16.astype(F32), axis=0, keepdims=True)
        mlp = mlp + nn(a16, wdown_ref[cols, :])
        grad_two = grad_two + nt(gh16, wup_ref[:, cols])
    base_ref[...] = mlp
    t2_ref[...] = grad_two * g2_ref[...]
    gain2_ref[...] += jnp.sum(grad_two * n, axis=0, keepdims=True)
    shift2_ref[...] += jnp.sum(grad_two, axis=0, keepdims=True)


def front(count, x, cot, cosine, sine, g1, b1, wqkv, bqkv, wout, bout, g2, b2, wup, bup, wdown, bdown, rows=256, tile=512):
    length, width = x.shape
    ff = wup.shape[1]
    pairs = width // PAIR
    once = pl.Buffered(1)

    def row(cols):
        return pl.BlockSpec((rows, cols), lambda i: (i, 0))

    def whole(a):
        return pl.BlockSpec(a.shape, lambda i: (0,) * a.ndim, pipeline_mode=once)

    heads = pl.BlockSpec((pairs, rows, PAIR), lambda i: (0, i, 0))

    def vec(cols):
        return pl.BlockSpec((1, cols), lambda i: (0, 0))

    vectors = [v.reshape(1, -1) for v in (g1, b1, bqkv, bout, g2, b2, bup, bdown)]
    g1, b1, bqkv, bout, g2, b2, bup, bdown = vectors
    s = jax.ShapeDtypeStruct
    return pl.pallas_call(
        functools.partial(front_body, tile=tile),
        grid=(length // rows,),
        in_specs=[pl.BlockSpec(memory_space=pltpu.SMEM), row(width), row(width), row(PAIR), row(PAIR)]
        + [whole(a) for a in (g1, b1, wqkv, bqkv, wout, bout, g2, b2, wup, bup, wdown, bdown)],
        out_specs=[heads] * 4 + [pl.BlockSpec((width, rows), lambda i: (0, i))] * 3 + [row(width)] + [row(ff)] * 2 + [row(width)] * 2 + [vec(width), vec(width), vec(ff), vec(width)],
        out_shape=[s((pairs, length, PAIR), BF16)] * 4 + [s((width, length), BF16)] * 3 + [s((length, width), BF16)] + [s((length, ff), BF16)] * 2
        + [s((length, width), F32)] * 2 + [s((1, width), F32), s((1, width), F32), s((1, ff), F32), s((1, width), F32)],
        compiler_params=pltpu.CompilerParams(vmem_limit_bytes=56 * 2**20),
        name="front",
    )(count, x, cot, cosine, sine, g1, b1, wqkv, bqkv, wout, bout, g2, b2, wup, bup, wdown, bdown)


def attention_body(first_ref, q_ref, k_ref, v_ref, gc_ref, segc_ref, segr_ref, cos_ref, sin_ref,
                   ctx_ref, ctxt_ref, gu_ref, dk_acc, dv_acc, *, rows):
    length = q_ref.shape[1]
    lane = lax.broadcasted_iota(jnp.int32, (rows, PAIR), 1)
    low = lane < HEAD_DIM
    dk_acc[...] = jnp.zeros_like(dk_acc)
    dv_acc[...] = jnp.zeros_like(dv_acc)

    def block(b, blocks):
        begin = pl.multiple_of(b * rows, rows)
        start = pl.multiple_of((b + 1 - blocks) * rows, rows)
        span = blocks * rows
        q = q_ref[0, pl.ds(begin, rows), :]
        g = gc_ref[0, pl.ds(begin, rows), :]
        zero = jnp.zeros_like(q)
        q2 = jnp.concatenate([jnp.where(low, q, zero), jnp.where(low, zero, q)], axis=0)
        g2 = jnp.concatenate([jnp.where(low, g, zero), jnp.where(low, zero, g)], axis=0)
        k = k_ref[0, pl.ds(start, span), :]
        v = v_ref[0, pl.ds(start, span), :]
        segt = segc_ref[pl.ds(begin, rows), :]
        segs = segr_ref[:, pl.ds(start, span)]
        t_at = begin + lax.broadcasted_iota(jnp.int32, (rows, span), 0)
        s_at = start + lax.broadcasted_iota(jnp.int32, (rows, span), 1)
        allowed = (segt == segs) & (s_at <= t_at)
        allowed = jnp.concatenate([allowed, allowed], axis=0)
        scores = jnp.where(allowed, nt(q2, k), EXCLUDED)
        peak = jnp.max(scores, axis=1, keepdims=True)
        e = jnp.exp(scores - peak)
        p = e * (1.0 / jnp.sum(e, axis=1, keepdims=True))
        p16 = p.astype(BF16)
        c2 = nn(p16, v)
        context = jnp.where(low, c2[:rows], c2[rows:]).astype(BF16)
        ctx_ref[pl.ds(begin, rows), :] = context
        ctxt_ref[:, pl.ds(begin, rows)] = context.T
        dp = nt(g2, v)
        inner = jnp.sum(p * dp, axis=1, keepdims=True)
        ds16 = (p * (dp - inner)).astype(BF16)
        d2 = nn(ds16, k)
        dq = jnp.where(low, d2[:rows], d2[rows:]) * (HEAD_DIM ** -0.5)
        cosine = cos_ref[pl.ds(begin, rows), :]
        sine = sin_ref[pl.ds(begin, rows), :]
        gu_ref[0, pl.ds(begin, rows), :] = (dq * cosine - turned(dq) * sine).astype(BF16)
        dk_acc[pl.ds(start, span), :] += tn(ds16, q2)
        dv_acc[pl.ds(start, span), :] += tn(p16, g2)

    total = length // rows

    def loop(b, carry):
        count = b + 1 - first_ref[b]
        for blocks in range(1, total + 1):
            @pl.when(count == blocks)
            def _():
                block(b, blocks)
        return carry

    lax.fori_loop(0, total, loop, 0)
    dk = dk_acc[...]
    gu_ref[1] = (dk * cos_ref[...] - turned(dk) * sin_ref[...]).astype(BF16)
    gu_ref[2] = dv_acc[...].astype(BF16)


def attention(q, k, v, gc, segment, cosine, sine, rows=128):
    pairs, length, _ = q.shape
    total = length // rows
    begins = jnp.sum((segment[None, :] < segment[::rows, None]).astype(jnp.int32), axis=1)
    first = begins // rows
    head = pl.BlockSpec((1, length, PAIR), lambda h, *_: (h, 0, 0))
    cols = pl.BlockSpec((length, PAIR), lambda h, *_: (0, h))
    s = jax.ShapeDtypeStruct
    width = pairs * PAIR

    def whole(shape):
        return pl.BlockSpec(shape, lambda h, *_: (0, 0), pipeline_mode=pl.Buffered(1))

    return pl.pallas_call(
        functools.partial(attention_body, rows=rows),
        grid_spec=pltpu.PrefetchScalarGridSpec(
            num_scalar_prefetch=1,
            grid=(pairs,),
            in_specs=[head] * 4 + [whole((length, 1)), whole((1, length)), whole((length, PAIR)), whole((length, PAIR))],
            out_specs=[cols, pl.BlockSpec((PAIR, length), lambda h, *_: (h, 0)), pl.BlockSpec((3, length, PAIR), lambda h, *_: (0, 0, h))],
            scratch_shapes=[pltpu.VMEM((length, PAIR), F32)] * 2,
        ),
        out_shape=[s((length, width), BF16), s((width, length), BF16), s((3, length, width), BF16)],
        compiler_params=pltpu.CompilerParams(vmem_limit_bytes=56 * 2**20),
        name="attention",
    )(first, q, k, v, gc, segment.reshape(-1, 1), segment.reshape(1, -1), cosine, sine)


MESH = pl.DeviceIdType.MESH
CHUNK = 384


class Line:
    def __init__(self):
        self.d = lax.axis_index("dp")
        self.z = lax.axis_index("rows")
        self.core = self.d % 2
        self.x = (self.d // 2) % 2
        self.y = self.d // 4
        self.over_core = (self.d + 1 - 2 * self.core, self.z)
        self.over_x = (self.d + 2 - 4 * self.x, self.z)
        self.over_y = (self.d + 4 - 8 * self.y, self.z)
        self.inner = (self.z + 1) // 2 % 2
        self.near = (self.d, self.z + 1 - 2 * (self.z % 2))
        self.far = (self.d, 3 - self.z)


def remote(src, dst, send, recv, to):
    return pltpu.make_async_remote_copy(src_ref=src, dst_ref=dst, send_sem=send, recv_sem=recv, device_id=to, device_id_type=MESH)


class Everywhere:
    HOPS = 7

    def __init__(self, at, held, come, send, recv):
        self.at, self.held, self.come, self.send, self.recv = at, held, come, send, recv

    def copy(self, hop, to):
        return remote(self.held.at[hop], self.come.at[hop], self.send.at[hop], self.recv.at[hop], to)

    def take(self, hop, to):
        self.copy(hop, to).wait()
        self.held[hop + 1] = self.held[hop] + self.come[hop]

    def hop(self, tick):
        at = self.at
        over = (at.over_core, at.over_x, at.over_y)

        @pl.when(tick == 0)
        def _():
            self.copy(0, over[0]).start()

        for j in (1, 2):
            @pl.when(tick == j)
            def _():
                self.take(j - 1, over[j - 1])
                self.copy(j, over[j]).start()

        @pl.when(tick == 3)
        def _():
            self.take(2, over[2])

            @pl.when(at.inner == 0)
            def _():
                self.copy(3, at.near).start()

        @pl.when((tick == 4) & (at.inner == 1))
        def _():
            self.copy(3, at.near).wait_recv()
            self.held[4] = self.held[3] + self.come[3]
            self.copy(4, at.far).start()

        @pl.when((tick == 4) & (at.inner == 0))
        def _():
            self.copy(3, at.near).wait_send()

        @pl.when((tick == 5) & (at.inner == 1))
        def _():
            self.take(4, at.far)
            self.copy(5, at.near).start()

        @pl.when(tick == 6)
        def _():
            @pl.when(at.inner == 1)
            def _():
                self.copy(5, at.near).wait_send()

            @pl.when(at.inner == 0)
            def _():
                self.copy(5, at.near).wait_recv()
                self.held[5] = self.come[5]


LAGS = dict(core=1, first=3, second=5, z=6, mid=8, back=9)


def reduce_body(count_ref, n1t_ref, n2t_ref, glt_ref, ctxt_ref, gh_ref, act_ref, glc_ref, guc_ref,
                x_ref, gl_ref, base_ref, t2_ref, ctx_ref, gu_ref, wqkv_ref, wout_ref, g1_ref,
                gain2_ref, shift2_ref, bup_ref, bout_ref,
                out_ref, ig_ref, grads_ref, vec_ref,
                part, from_core, from_first, from_second, zsum, from_near, from_far,
                c_send, c_recv, f_send, f_recv, s_send, s_recv, n_send, n_recv, m_send, m_recv,
                held_n, come_n, held_v, come_v, n_s, n_r, v_s, v_r, gain1, shift1, bqkv, *, cuts, row_ticks):
    tick = pl.program_id(0)
    at = Line()
    chunks = cuts[-1]
    ring = part.shape[0]
    width = wout_ref.shape[0]
    block = width // 8

    @pl.when(tick == 0)
    def _():
        barrier = pltpu.get_barrier_semaphore()
        for to in (at.over_core, at.over_x, at.over_y, at.near):
            pl.semaphore_signal(barrier, inc=1, device_id=to, device_id_type=MESH)

        @pl.when(at.inner == 1)
        def _():
            pl.semaphore_signal(barrier, inc=1, device_id=at.far, device_id_type=MESH)
            pl.semaphore_wait(barrier, 5)

        @pl.when(at.inner == 0)
        def _():
            pl.semaphore_wait(barrier, 4)

        held_n[0] = jnp.full(held_n.shape[1:], count_ref[0].astype(F32), F32)

    def places(i):
        even = 1 - i % 2
        f = at.x * even + at.y * (1 - even)
        s = at.y * even + at.x * (1 - even)
        first = (at.d + even * (2 - 4 * at.x) + (1 - even) * (4 - 8 * at.y), at.z)
        second = (at.d + even * (4 - 8 * at.y) + (1 - even) * (2 - 4 * at.x), at.z)
        return even, f, s, first, second, i % ring

    def core_copy(i):
        slot = i % ring
        return remote(part.at[slot, 1 - at.core], from_core.at[i], c_send.at[i], c_recv.at[i], at.over_core)

    def first_copy(i):
        even, f, s, first, second, slot = places(i)
        return remote(part.at[slot, at.core, 1 - f], from_first.at[i], f_send.at[i], f_recv.at[i], first)

    def second_copy(i):
        even, f, s, first, second, slot = places(i)
        return remote(part.at[slot, at.core, f, 1 - s], from_second.at[i], s_send.at[i], s_recv.at[i], second)

    def out_copy(i):
        return remote(zsum.at[i], from_near.at[i], n_send.at[i], n_recv.at[i], at.near)

    def far_copy(i):
        return remote(zsum.at[i], from_far.at[i], m_send.at[i], m_recv.at[i], at.far)

    def back_copy(i):
        return remote(from_far.at[i], from_near.at[i], n_send.at[i], n_recv.at[i], at.near)

    def plus(a, b):
        return (a.astype(F32) + b.astype(F32)).astype(BF16)

    def product(left, right):
        even = 1 - tick % 2
        slot = tick % ring
        half = width // 2
        for h in range(2):
            rows = nn(left[h * half : (h + 1) * half, :], right)
            for j in range(4):
                d = h * 4 + j
                c, x, y = d % 2, (d // 2) % 2, d // 4
                a = x * even + y * (1 - even)
                b = y * even + x * (1 - even)
                part[slot, c, a, b] = rows[j * block : (j + 1) * block].astype(BF16)
        core_copy(tick).start()

    starts = (0,) + cuts[:-1]
    operands = ((n2t_ref, gh_ref), (glt_ref, act_ref), (ctxt_ref, glc_ref), (n1t_ref, guc_ref))
    for (left, right), lo, hi in zip(operands, starts, cuts):
        @pl.when((tick >= lo) & (tick < hi))
        def _():
            product(left[...], right[0] if right is guc_ref else right[...])

    def when(lag, f):
        i = tick - lag

        @pl.when((i >= 0) & (i < chunks))
        def _():
            f(i)

    def core_step(i):
        even, f, s, first, second, slot = places(i)
        core_copy(i).wait()
        for a in range(2):
            for b in range(2):
                part[slot, at.core, a, b] = plus(part[slot, at.core, a, b], from_core[i, a, b])
        first_copy(i).start()

    def first_step(i):
        even, f, s, first, second, slot = places(i)
        first_copy(i).wait()
        for b in range(2):
            part[slot, at.core, f, b] = plus(part[slot, at.core, f, b], from_first[i, b])
        second_copy(i).start()

    def second_step(i):
        even, f, s, first, second, slot = places(i)
        second_copy(i).wait()
        zsum[i] = plus(part[slot, at.core, f, s], from_second[i])

        @pl.when(at.inner == 0)
        def _():
            out_copy(i).start()

    def near_step(i):
        @pl.when(at.inner == 1)
        def _():
            out_copy(i).wait_recv()
            zsum[i] = plus(zsum[i], from_near[i])
            far_copy(i).start()

    def far_step(i):
        @pl.when(at.inner == 1)
        def _():
            far_copy(i).wait()
            total = plus(zsum[i], from_far[i])
            from_far[i] = total
            back_copy(i).start()
            grads_ref[i] = total.astype(F32) / held_n[5, 0:1, 0:1]

        @pl.when(at.inner == 0)
        def _():
            out_copy(i).wait_send()

    def back_step(i):
        @pl.when(at.inner == 0)
        def _():
            back_copy(i).wait_recv()
            grads_ref[i] = from_near[i].astype(F32) / held_n[5, 0:1, 0:1]

        @pl.when(at.inner == 1)
        def _():
            back_copy(i).wait_send()

    when(LAGS["core"], core_step)

    @pl.when(tick == 0)
    def _():
        gain1[...] = jnp.zeros_like(gain1)
        shift1[...] = jnp.zeros_like(shift1)
        bqkv[...] = jnp.zeros_like(bqkv)

    @pl.when(tick < row_ticks)
    def _():
        out_ref[...] = (base_ref[...] + nn(ctx_ref[...], wout_ref[...])).astype(BF16)
        g1 = nt(gu_ref[0], wqkv_ref[:, :width])
        g1 = g1 + nt(gu_ref[1], wqkv_ref[:, width : 2 * width])
        g1 = g1 + nt(gu_ref[2], wqkv_ref[:, 2 * width :])
        x = x_ref[...].astype(F32)
        centred = x - jnp.mean(x, axis=1, keepdims=True)
        r = lax.rsqrt(jnp.mean(centred * centred, axis=1, keepdims=True) + EPSILON)
        n = centred * r
        gain1[...] += jnp.sum(g1 * n, axis=0, keepdims=True)
        shift1[...] += jnp.sum(g1, axis=0, keepdims=True)
        for j in range(3):
            bqkv[:, j * width : (j + 1) * width] += jnp.sum(gu_ref[j].astype(F32), axis=0, keepdims=True)
        t = g1 * g1_ref[...] + t2_ref[...]
        dx = r * (t - jnp.mean(t, axis=1, keepdims=True) - n * jnp.mean(t * n, axis=1, keepdims=True))
        ig_ref[...] = (gl_ref[...].astype(F32) + dx).astype(BF16)

    when(LAGS["first"], first_step)
    when(LAGS["second"], second_step)
    when(LAGS["z"], near_step)
    when(LAGS["mid"], far_step)
    when(LAGS["back"], back_step)

    Everywhere(at, held_n, come_n, n_s, n_r).hop(tick)

    @pl.when(tick == row_ticks)
    def _():
        held_v[0] = jnp.zeros(held_v.shape[1:], F32)
        held_v[0, 0:1, :] = bup_ref[...]
        held_v[0, 1:2, : 3 * width] = bqkv[...]
        held_v[0, 1:2, 3 * width :] = bout_ref[...]
        held_v[0, 2:3, :width] = gain1[...]
        held_v[0, 2:3, width : 2 * width] = shift1[...]
        held_v[0, 2:3, 2 * width : 3 * width] = gain2_ref[...]
        held_v[0, 2:3, 3 * width :] = shift2_ref[...]

    Everywhere(at, held_v, come_v, v_s, v_r).hop(tick - row_ticks)

    @pl.when(tick == row_ticks + 6)
    def _():
        vec_ref[...] = held_v[5] / held_n[5, 0:1, 0:1]


def reduce(count, n1t, n2t, glt, ctxt, gh, act, gl, gu, x, base, t2, ctx, wqkv, wout, g1, gain2, shift2, bup, bout):
    length, width = x.shape
    ff = gh.shape[1]
    block = width // 8
    counts = (ff // CHUNK, ff // CHUNK, width // CHUNK, 3 * width // CHUNK)
    cuts = tuple(int(c) for c in np.cumsum(counts))
    chunks = cuts[-1]
    per = width // CHUNK
    rows = 128
    row_ticks = length // rows
    ticks = chunks + LAGS["back"]
    ring = 8

    def cols(array_chunks, begin):
        return pl.BlockSpec((length, CHUNK), lambda t: (0, jnp.clip(t - begin, 0, array_chunks - 1)))

    def row(cols):
        return pl.BlockSpec((rows, cols), lambda t: (jnp.minimum(t, row_ticks - 1), 0))

    def whole(a):
        return pl.BlockSpec(a.shape, lambda t: (0,) * a.ndim, pipeline_mode=pl.Buffered(1))

    def gu_cols(t):
        j = jnp.clip(t - cuts[2], 0, counts[3] - 1)
        return (j // per, 0, j % per)

    g1 = g1.reshape(1, -1)
    s = jax.ShapeDtypeStruct
    dma = pltpu.SemaphoreType.DMA
    hops = Everywhere.HOPS
    return pl.pallas_call(
        functools.partial(reduce_body, cuts=cuts, row_ticks=row_ticks),
        grid=(ticks,),
        in_specs=[pl.BlockSpec(memory_space=pltpu.SMEM), whole(n1t), whole(n2t), whole(glt), whole(ctxt),
                  cols(counts[0], 0), cols(counts[1], cuts[0]), cols(counts[2], cuts[1]),
                  pl.BlockSpec((1, length, CHUNK), gu_cols),
                  row(width), row(width), row(width), row(width), row(width),
                  pl.BlockSpec((3, rows, width), lambda t: (0, jnp.minimum(t, row_ticks - 1), 0)),
                  whole(wqkv), whole(wout), whole(g1), whole(gain2), whole(shift2), whole(bup), whole(bout)],
        out_specs=[row(width), row(width),
                   pl.BlockSpec((chunks, block, CHUNK), lambda t: (0, 0, 0), pipeline_mode=pl.Buffered(1)),
                   pl.BlockSpec((8, ff), lambda t: (0, 0), pipeline_mode=pl.Buffered(1))],
        out_shape=[s((length, width), BF16), s((length, width), BF16), s((chunks, block, CHUNK), F32), s((8, ff), F32)],
        scratch_shapes=[
            pltpu.VMEM((ring, 2, 2, 2, block, CHUNK), BF16),
            pltpu.VMEM((chunks, 2, 2, block, CHUNK), BF16),
            pltpu.VMEM((chunks, 2, block, CHUNK), BF16),
            pltpu.VMEM((chunks, block, CHUNK), BF16),
            pltpu.VMEM((chunks, block, CHUNK), BF16),
            pltpu.VMEM((chunks, block, CHUNK), BF16),
            pltpu.VMEM((chunks, block, CHUNK), BF16),
        ] + [dma((chunks,))] * 10 + [
            pltpu.VMEM((hops, 8, 128), F32), pltpu.VMEM((hops, 8, 128), F32),
            pltpu.VMEM((hops, 8, ff), F32), pltpu.VMEM((hops, 8, ff), F32),
            dma((hops,)), dma((hops,)), dma((hops,)), dma((hops,)),
            pltpu.VMEM((1, width), F32), pltpu.VMEM((1, width), F32), pltpu.VMEM((1, 3 * width), F32),
        ],
        compiler_params=pltpu.CompilerParams(vmem_limit_bytes=60 * 2**20, collective_id=0, has_side_effects=True),
        name="reduce",
    )(count, n1t, n2t, glt, ctxt, gh, act, gl, gu, x, gl, base, t2, ctx, gu, wqkv, wout, g1, gain2, shift2, bup, bout)


def by_collectives(count, n1t, n2t, glt, ctxt, gh, act, gl, gu, x, base, t2, ctx, wqkv, wout, g1, gain2, shift2, bup, bout):
    width = x.shape[1]
    flat = jnp.concatenate([gu[0], gu[1], gu[2]], axis=1)
    out = (base + nn(ctx, wout)).astype(BF16)
    grad_one = nt(flat, wqkv)
    x = x.astype(F32)
    centred = x - jnp.mean(x, axis=1, keepdims=True)
    r = lax.rsqrt(jnp.mean(centred * centred, axis=1, keepdims=True) + EPSILON)
    n = centred * r
    t = grad_one * g1 + t2
    dx = r * (t - jnp.mean(t, axis=1, keepdims=True) - n * jnp.mean(t * n, axis=1, keepdims=True))
    input_grad = (gl.astype(F32) + dx).astype(BF16)
    packed = jnp.concatenate([bup[0], jnp.sum(flat, axis=0, dtype=F32), bout[0], jnp.sum(grad_one * n, axis=0),
                              jnp.sum(grad_one, axis=0), gain2[0], shift2[0], count.astype(F32)])
    packed = lax.psum(packed, ("dp", "rows"))
    part = jnp.concatenate([nn(n2t, gh), nn(glt, act), nn(ctxt, gl), nn(n1t, flat)], axis=1).astype(BF16)
    grads = lax.psum(lax.psum_scatter(part, "dp", scatter_dimension=0, tiled=True), "rows")
    return out, input_grad, grads.astype(F32) / packed[-1], (packed[:-1] / packed[-1]).reshape(3, -1)


def by_kernel(*operands):
    out, input_grad, grads, vec = reduce(*operands)
    grads = jnp.swapaxes(grads, 0, 1).reshape(grads.shape[1], -1)
    return out, input_grad, grads, vec


def shards(tokens, segment_ids, true_counts, regroup, cotangent, ln1_gain, ln1_bias, qkv_weight, qkv_bias, out_weight,
           out_bias, ln2_gain, ln2_bias, up_weight, up_bias, down_weight, down_bias):
    length, width = cotangent.shape
    ff = up_weight.shape[1]
    source = regroup[0] % lax.axis_size("rows")
    piece = lax.all_gather(tokens, "rows", axis=0, tiled=True)
    arrived = lax.dynamic_slice_in_dim(piece, source * length, length, 0)
    cosine, sine = (jnp.asarray(t) for t in rotary_tables(length))
    (q, k, v, gc, n1t, n2t, glt, gl, act, gh, base, t2, gain2, shift2, bias_up, bias_out) = front(
        true_counts, arrived, cotangent, cosine, sine, ln1_gain, ln1_bias, qkv_weight, qkv_bias, out_weight, out_bias,
        ln2_gain, ln2_bias, up_weight, up_bias, down_weight, down_bias)
    ctx, ctxt, gu = attention(q, k, v, gc, segment_ids, cosine, sine, rows=256)
    last = by_kernel if (lax.axis_size("dp"), lax.axis_size("rows")) == (8, 4) else by_collectives
    out, input_grad, grads, vec = last(true_counts, n1t, n2t, glt, ctxt, gh, act, gl, gu, arrived, base, t2, ctx, qkv_weight,
                                       out_weight, ln1_gain, gain2, shift2, bias_up, bias_out)
    up, down = grads[:, :ff], grads[:, ff : 2 * ff].T
    low, qkv = grads[:, 2 * ff : 2 * ff + width], grads[:, 2 * ff + width :]
    gains = vec[2].reshape(4, width)
    bias_out = vec[1, 3 * width :]
    return (out, input_grad, gains[0], gains[1], qkv, vec[1, : 3 * width], low, bias_out, gains[2], gains[3], up, vec[0], down,
            bias_out)


def solution(mesh):
    both = ("dp", "rows")
    placed = (P(both, None), P(both), P(both), P(both), P(both, None)) + (P(),) * 12
    return jax.shard_map(
        shards, mesh=mesh, in_specs=placed,
        out_specs=(P(both, None), P(both, None), P(), P(), P("dp", None), P(), P("dp", None), P(), P(), P(), P("dp", None), P(),
                   P(None, "dp"), P()),
        check_vma=False)
```

```python
import functools
import numpy as np
import jax
import jax.numpy as jnp
from jax import lax
from jax.experimental import pallas as pl
from jax.experimental.pallas import tpu as pltpu
from jax.sharding import PartitionSpec as P

HEAD_DIM = 64
ROT = 16
PAIR = 128
EPSILON = 1e-05
EXCLUDED = -1e30
F32 = jnp.float32
BF16 = jnp.bfloat16
MESH = pl.DeviceIdType.MESH


def remote(src, dst, send, recv, to):
    return pltpu.make_async_remote_copy(src_ref=src, dst_ref=dst, send_sem=send, recv_sem=recv, device_id=to, device_id_type=MESH)


def nn(a, b):
    return lax.dot_general(a, b, (((1,), (0,)), ((), ())), preferred_element_type=F32)


def nt(a, b):
    return lax.dot_general(a, b, (((1,), (1,)), ((), ())), preferred_element_type=F32)


def tn(a, b):
    return lax.dot_general(a, b, (((0,), (0,)), ((), ())), preferred_element_type=F32)


def rotary_tables(length):
    half = ROT // 2
    placed = np.arange(length, dtype=np.float32)
    rates = np.exp(np.arange(half, dtype=np.float32) * np.float32(-2.0 / ROT) * np.log(np.float32(10000.0)))
    phases = placed[:, None] * rates[None, :].astype(np.float32)
    cosine = np.ones((length, HEAD_DIM), np.float32)
    sine = np.zeros((length, HEAD_DIM), np.float32)
    cosine[:, :half] = np.cos(phases)
    cosine[:, half:ROT] = np.cos(phases)
    sine[:, :half] = -np.sin(phases)
    sine[:, half:ROT] = np.sin(phases)
    return np.tile(cosine, (1, PAIR // HEAD_DIM)), np.tile(sine, (1, PAIR // HEAD_DIM))


def turned(u):
    lane = lax.broadcasted_iota(jnp.int32, u.shape, 1) % HEAD_DIM
    half = ROT // 2
    return jnp.where(lane < half, pltpu.roll(u, PAIR - half, 1), pltpu.roll(u, half, 1))


def gelu_parts(h):
    e = jnp.exp(h * h * -0.5)
    t = 1.0 / (1.0 + 0.2316418882 * jnp.abs(h))
    poly = t * (0.127414796 + t * (-0.142248368 + t * (0.7107068705 + t * (-0.7265760135 + t * 0.5307027145))))
    tail = poly * e
    phi = jnp.where(h >= 0, 1.0 - tail, tail)
    return h * phi, phi + h * (e * 0.3989422804014327)


def front_body(count_ref, want_ref, own_ref, cot_ref, cos_ref, sin_ref, g1_ref, b1_ref, bqkv_ref, bout_ref, g2_ref, b2_ref,
               bup_ref, bdown_ref, wqkv_hbm, wout_hbm, wup_hbm, wdown_hbm,
               x_ref, q_ref, k_ref, v_ref, gc_ref, n1t_ref, n2t_ref, glt_ref, gl_ref, act_ref, gh_ref, base_ref, t2_ref,
               gain2_ref, shift2_ref, bup_out, bout_out,
               wqkv_ref, wout_ref, wup_ref, wdown_ref, wants, from_near, from_half, to_inner, to_end,
               w_sem, want_send, want_recv, near_send, near_recv, inner_send, end_send, half_recv, *, tile):
    step = pl.program_id(0)
    steps = pl.num_programs(0)
    rows, width = cot_ref.shape
    pairs = width // PAIR
    ff = wup_ref.shape[1]
    chunks = own_ref.shape[0] // rows
    d, z = lax.axis_index("dp"), lax.axis_index("rows")
    inner = (z + 1) // 2 % 2
    near = z + 1 - 2 * (z % 2)
    other_inner, other_end = 3 - z, 6 - 3 * z
    loads = [pltpu.make_async_copy(src, dst, w_sem.at[j]) for j, (src, dst) in enumerate(
        ((wqkv_hbm, wqkv_ref), (wout_hbm, wout_ref), (wup_hbm, wup_ref), (wdown_hbm, wdown_ref)))]

    def span(i):
        return pl.ds(pl.multiple_of(i * rows, rows), rows)

    def want_copy(j):
        to = lax.rem(z + j, 4)
        return remote(wants.at[0], wants.at[j], want_send.at[j], want_recv.at[j], (d, to))

    def near_copy(i):
        return remote(own_ref.at[span(i)], from_near.at[span(i)], near_send.at[i], near_recv.at[i], (d, near))

    def inner_copy(i):
        return remote(to_inner.at[span(i)], from_half.at[span(i)], inner_send.at[i], half_recv.at[i], (d, other_inner))

    def end_copy(i):
        return remote(to_end.at[span(i)], from_half.at[span(i)], end_send.at[i], half_recv.at[i], (d, other_end))

    def wanted(by):
        return wants[lax.rem(z - by + 4, 4), 0:1, 0:1]

    def relay(i):
        @pl.when(inner == 1)
        def _():
            near_copy(i).wait_recv()
            mine = own_ref[span(i), :].astype(F32)
            theirs = from_near[span(i), :].astype(F32)
            to_end[span(i), :] = jnp.where(wanted(other_end) == near, theirs, mine).astype(BF16)
            end_copy(i).start()
            to_inner[span(i), :] = jnp.where(wanted(other_inner) == near, theirs, mine).astype(BF16)
            inner_copy(i).start()

    @pl.when(step == 0)
    def _():
        barrier = pltpu.get_barrier_semaphore()
        for j in (1, 2, 3):
            pl.semaphore_signal(barrier, inc=1, device_id=(d, lax.rem(z + j, 4)), device_id_type=MESH)
        wants[0] = want_ref[...]
        pl.semaphore_wait(barrier, 3)
        for j in (1, 2, 3):
            want_copy(j).start()

        def hand(i, carry):
            near_copy(i).start()
            return carry

        lax.fori_loop(0, chunks, hand, 0)
        for load in loads:
            load.start()
        for j in (1, 2, 3):
            want_copy(j).wait()
        relay(0)
        gain2_ref[...] = jnp.zeros_like(gain2_ref)
        shift2_ref[...] = jnp.zeros_like(shift2_ref)
        bup_out[...] = jnp.zeros_like(bup_out)
        bout_out[...] = jnp.zeros_like(bout_out)

    @pl.when(step + 1 < chunks)
    def _():
        relay(step + 1)

    @pl.when(step == 0)
    def _():
        for load in loads:
            load.wait()

    place = step * rows + lax.broadcasted_iota(jnp.int32, (rows, 1), 0)
    gl = jnp.where(place < count_ref[0], cot_ref[...].astype(F32), 0.0)
    gl16 = gl.astype(BF16)
    gl_ref[...] = gl16
    glt_ref[...] = gl16.T
    bout_out[...] += jnp.sum(gl, axis=0, keepdims=True)
    for p in range(pairs):
        gc_ref[p] = nt(gl16, wout_ref[p * PAIR : (p + 1) * PAIR, :]).astype(BF16)

    @pl.when(inner == 0)
    def _():
        near_copy(step).wait_recv()

    inner_copy(step).wait_recv()
    source = wanted(z)
    x = jnp.where(source == near, from_near[span(step), :].astype(F32), from_half[span(step), :].astype(F32))
    x = jnp.where(source == z, own_ref[span(step), :].astype(F32), x)
    x_ref[...] = x.astype(BF16)
    centred = x - jnp.mean(x, axis=1, keepdims=True)
    r = lax.rsqrt(jnp.mean(centred * centred, axis=1, keepdims=True) + EPSILON)
    n = centred * r
    n1 = (n * g1_ref[...] + b1_ref[...]).astype(BF16)
    n2 = (n * g2_ref[...] + b2_ref[...]).astype(BF16)
    n1t_ref[...] = n1.T
    n2t_ref[...] = n2.T
    cosine, sine = cos_ref[...], sin_ref[...]
    for p in range(pairs):
        for which, ref in enumerate((q_ref, k_ref, v_ref)):
            wide = slice(which * width + p * PAIR, which * width + (p + 1) * PAIR)
            u = nn(n1, wqkv_ref[:, wide]) + bqkv_ref[:, wide]
            if which < 2:
                u = u * cosine + turned(u) * sine
            if which == 0:
                u = u * (HEAD_DIM ** -0.5)
            ref[p] = u.astype(BF16)
    mlp = x + (bdown_ref[...] + bout_ref[...])
    grad_two = jnp.zeros((rows, width), F32)
    for f in range(0, ff, tile):
        cols = slice(f, f + tile)
        h = nn(n2, wup_ref[:, cols]) + bup_ref[:, cols]
        ga = nt(gl16, wdown_ref[cols, :])
        a, slope = gelu_parts(h)
        a16 = a.astype(BF16)
        gh = ga * slope
        gh16 = gh.astype(BF16)
        act_ref[:, cols] = a16
        gh_ref[:, cols] = gh16
        bup_out[:, cols] += jnp.sum(gh16.astype(F32), axis=0, keepdims=True)
        mlp = mlp + nn(a16, wdown_ref[cols, :])
        grad_two = grad_two + nt(gh16, wup_ref[:, cols])
    base_ref[...] = mlp
    t2_ref[...] = grad_two * g2_ref[...]
    gain2_ref[...] += jnp.sum(grad_two * n, axis=0, keepdims=True)
    shift2_ref[...] += jnp.sum(grad_two, axis=0, keepdims=True)

    @pl.when(step == steps - 1)
    def _():
        def done(i, carry):
            near_copy(i).wait_send()

            @pl.when(inner == 1)
            def _():
                inner_copy(i).wait_send()
                end_copy(i).wait_send()
            return carry

        lax.fori_loop(0, chunks, done, 0)


def front(count, want, own, cot, cosine, sine, g1, b1, wqkv, bqkv, wout, bout, g2, b2, wup, bup, wdown, bdown, rows=128, tile=512):
    length, width = own.shape
    ff = wup.shape[1]
    pairs = width // PAIR
    chunks = length // rows

    def row(cols):
        return pl.BlockSpec((rows, cols), lambda i: (i, 0))

    def whole(a):
        return pl.BlockSpec(a.shape, lambda i: (0,) * a.ndim, pipeline_mode=pl.Buffered(1))

    heads = pl.BlockSpec((pairs, rows, PAIR), lambda i: (0, i, 0))
    down = pl.BlockSpec((width, rows), lambda i: (0, i))

    def vec(cols):
        return pl.BlockSpec((1, cols), lambda i: (0, 0))

    vectors = [v.reshape(1, -1) for v in (g1, b1, bqkv, bout, g2, b2, bup, bdown)]
    weights = (wqkv, wout, wup, wdown)
    s = jax.ShapeDtypeStruct
    dma = pltpu.SemaphoreType.DMA
    return pl.pallas_call(
        functools.partial(front_body, tile=tile),
        grid=(chunks,),
        in_specs=[pl.BlockSpec(memory_space=pltpu.SMEM), whole(want), whole(own), row(width), row(PAIR), row(PAIR)]
        + [whole(a) for a in vectors] + [pl.BlockSpec(memory_space=pl.ANY)] * 4,
        out_specs=[row(width)] + [heads] * 4 + [down] * 3 + [row(width)] + [row(ff)] * 2 + [row(width)] * 2
        + [vec(width), vec(width), vec(ff), vec(width)],
        out_shape=[s((length, width), BF16)] + [s((pairs, length, PAIR), BF16)] * 4 + [s((width, length), BF16)] * 3
        + [s((length, width), BF16)] + [s((length, ff), BF16)] * 2
        + [s((length, width), F32)] * 2 + [s((1, width), F32), s((1, width), F32), s((1, ff), F32), s((1, width), F32)],
        scratch_shapes=[pltpu.VMEM(w.shape, BF16) for w in weights]
        + [pltpu.VMEM((4, 8, 128), jnp.int32)] + [pltpu.VMEM((length, width), BF16)] * 4
        + [dma((4,)), dma((4,)), dma((4,))] + [dma((chunks,))] * 5,
        compiler_params=pltpu.CompilerParams(vmem_limit_bytes=60 * 2**20, collective_id=1, has_side_effects=True),
        name="front",
    )(count, want, own, cot, cosine, sine, *vectors, *weights)


def attention_body(first_ref, q_ref, k_ref, v_ref, gc_ref, segc_ref, segr_ref, cos_ref, sin_ref,
                   ctx_ref, ctxt_ref, gu_ref, dk_acc, dv_acc, *, rows):
    length = q_ref.shape[1]
    lane = lax.broadcasted_iota(jnp.int32, (rows, PAIR), 1)
    low = lane < HEAD_DIM
    dk_acc[...] = jnp.zeros_like(dk_acc)
    dv_acc[...] = jnp.zeros_like(dv_acc)

    def block(b, blocks):
        begin = pl.multiple_of(b * rows, rows)
        start = pl.multiple_of((b + 1 - blocks) * rows, rows)
        span = blocks * rows
        q = q_ref[0, pl.ds(begin, rows), :]
        g = gc_ref[0, pl.ds(begin, rows), :]
        zero = jnp.zeros_like(q)
        q2 = jnp.concatenate([jnp.where(low, q, zero), jnp.where(low, zero, q)], axis=0)
        g2 = jnp.concatenate([jnp.where(low, g, zero), jnp.where(low, zero, g)], axis=0)
        k = k_ref[0, pl.ds(start, span), :]
        v = v_ref[0, pl.ds(start, span), :]
        segt = segc_ref[pl.ds(begin, rows), :]
        segs = segr_ref[:, pl.ds(start, span)]
        t_at = begin + lax.broadcasted_iota(jnp.int32, (rows, span), 0)
        s_at = start + lax.broadcasted_iota(jnp.int32, (rows, span), 1)
        allowed = (segt == segs) & (s_at <= t_at)
        allowed = jnp.concatenate([allowed, allowed], axis=0)
        scores = jnp.where(allowed, nt(q2, k), EXCLUDED)
        peak = jnp.max(scores, axis=1, keepdims=True)
        e = jnp.exp(scores - peak)
        p = e * (1.0 / jnp.sum(e, axis=1, keepdims=True))
        p16 = p.astype(BF16)
        c2 = nn(p16, v)
        context = jnp.where(low, c2[:rows], c2[rows:]).astype(BF16)
        ctx_ref[pl.ds(begin, rows), :] = context
        ctxt_ref[:, pl.ds(begin, rows)] = context.T
        dp = nt(g2, v)
        inner = jnp.sum(p * dp, axis=1, keepdims=True)
        ds16 = (p * (dp - inner)).astype(BF16)
        d2 = nn(ds16, k)
        dq = jnp.where(low, d2[:rows], d2[rows:]) * (HEAD_DIM ** -0.5)
        cosine = cos_ref[pl.ds(begin, rows), :]
        sine = sin_ref[pl.ds(begin, rows), :]
        gu_ref[0, pl.ds(begin, rows), :] = (dq * cosine - turned(dq) * sine).astype(BF16)
        dk_acc[pl.ds(start, span), :] += tn(ds16, q2)
        dv_acc[pl.ds(start, span), :] += tn(p16, g2)

    total = length // rows

    def loop(b, carry):
        count = b + 1 - first_ref[b]
        for blocks in range(1, total + 1):
            @pl.when(count == blocks)
            def _():
                block(b, blocks)
        return carry

    lax.fori_loop(0, total, loop, 0)
    dk = dk_acc[...]
    gu_ref[1] = (dk * cos_ref[...] - turned(dk) * sin_ref[...]).astype(BF16)
    gu_ref[2] = dv_acc[...].astype(BF16)


def attention(q, k, v, gc, segment, cosine, sine, rows=128):
    pairs, length, _ = q.shape
    total = length // rows
    begins = jnp.sum((segment[None, :] < segment[::rows, None]).astype(jnp.int32), axis=1)
    first = begins // rows
    head = pl.BlockSpec((1, length, PAIR), lambda h, *_: (h, 0, 0))
    cols = pl.BlockSpec((length, PAIR), lambda h, *_: (0, h))
    s = jax.ShapeDtypeStruct
    width = pairs * PAIR

    def whole(shape):
        return pl.BlockSpec(shape, lambda h, *_: (0, 0), pipeline_mode=pl.Buffered(1))

    return pl.pallas_call(
        functools.partial(attention_body, rows=rows),
        grid_spec=pltpu.PrefetchScalarGridSpec(
            num_scalar_prefetch=1,
            grid=(pairs,),
            in_specs=[head] * 4 + [whole((length, 1)), whole((1, length)), whole((length, PAIR)), whole((length, PAIR))],
            out_specs=[cols, pl.BlockSpec((PAIR, length), lambda h, *_: (h, 0)), pl.BlockSpec((3, length, PAIR), lambda h, *_: (0, 0, h))],
            scratch_shapes=[pltpu.VMEM((length, PAIR), F32)] * 2,
        ),
        out_shape=[s((length, width), BF16), s((width, length), BF16), s((3, length, width), BF16)],
        compiler_params=pltpu.CompilerParams(vmem_limit_bytes=56 * 2**20),
        name="attention",
    )(first, q, k, v, gc, segment.reshape(-1, 1), segment.reshape(1, -1), cosine, sine)


CHUNK = 384


class Line:
    def __init__(self):
        self.d = lax.axis_index("dp")
        self.z = lax.axis_index("rows")
        self.core = self.d % 2
        self.x = (self.d // 2) % 2
        self.y = self.d // 4
        self.over_core = (self.d + 1 - 2 * self.core, self.z)
        self.over_x = (self.d + 2 - 4 * self.x, self.z)
        self.over_y = (self.d + 4 - 8 * self.y, self.z)
        self.inner = (self.z + 1) // 2 % 2
        self.near = (self.d, self.z + 1 - 2 * (self.z % 2))
        self.far = (self.d, 3 - self.z)


class Everywhere:
    HOPS = 7

    def __init__(self, at, held, come, send, recv):
        self.at, self.held, self.come, self.send, self.recv = at, held, come, send, recv

    def copy(self, hop, to):
        return remote(self.held.at[hop], self.come.at[hop], self.send.at[hop], self.recv.at[hop], to)

    def take(self, hop, to):
        self.copy(hop, to).wait()
        self.held[hop + 1] = self.held[hop] + self.come[hop]

    def hop(self, tick):
        at = self.at
        over = (at.over_core, at.over_x, at.over_y)

        @pl.when(tick == 0)
        def _():
            self.copy(0, over[0]).start()

        for j in (1, 2):
            @pl.when(tick == j)
            def _():
                self.take(j - 1, over[j - 1])
                self.copy(j, over[j]).start()

        @pl.when(tick == 3)
        def _():
            self.take(2, over[2])

            @pl.when(at.inner == 0)
            def _():
                self.copy(3, at.near).start()

        @pl.when((tick == 4) & (at.inner == 1))
        def _():
            self.copy(3, at.near).wait_recv()
            self.held[4] = self.held[3] + self.come[3]
            self.copy(4, at.far).start()

        @pl.when((tick == 4) & (at.inner == 0))
        def _():
            self.copy(3, at.near).wait_send()

        @pl.when((tick == 5) & (at.inner == 1))
        def _():
            self.take(4, at.far)
            self.copy(5, at.near).start()

        @pl.when(tick == 6)
        def _():
            @pl.when(at.inner == 1)
            def _():
                self.copy(5, at.near).wait_send()

            @pl.when(at.inner == 0)
            def _():
                self.copy(5, at.near).wait_recv()
                self.held[5] = self.come[5]


LAGS = dict(core=1, first=3, second=5, z=6, mid=8, back=9)


def reduce_body(count_ref, n1t_ref, n2t_ref, glt_ref, ctxt_ref, gh_ref, act_ref, glc_ref, guc_ref,
                x_ref, gl_ref, base_ref, t2_ref, ctx_ref, gu_ref, wqkv_ref, wout_ref, g1_ref,
                gain2_ref, shift2_ref, bup_ref, bout_ref,
                out_ref, ig_ref, grads_ref, vec_ref,
                part, from_core, from_first, from_second, zsum, from_near, from_far,
                c_send, c_recv, f_send, f_recv, s_send, s_recv, n_send, n_recv, m_send, m_recv,
                held_n, come_n, held_v, come_v, n_s, n_r, v_s, v_r, gain1, shift1, bqkv, *, cuts, row_ticks):
    tick = pl.program_id(0)
    at = Line()
    chunks = cuts[-1]
    ring = part.shape[0]
    width = wout_ref.shape[0]
    block = width // 8

    @pl.when(tick == 0)
    def _():
        barrier = pltpu.get_barrier_semaphore()
        for to in (at.over_core, at.over_x, at.over_y, at.near):
            pl.semaphore_signal(barrier, inc=1, device_id=to, device_id_type=MESH)

        @pl.when(at.inner == 1)
        def _():
            pl.semaphore_signal(barrier, inc=1, device_id=at.far, device_id_type=MESH)
            pl.semaphore_wait(barrier, 5)

        @pl.when(at.inner == 0)
        def _():
            pl.semaphore_wait(barrier, 4)

        held_n[0] = jnp.full(held_n.shape[1:], count_ref[0].astype(F32), F32)

    def places(i):
        even = 1 - i % 2
        f = at.x * even + at.y * (1 - even)
        s = at.y * even + at.x * (1 - even)
        first = (at.d + even * (2 - 4 * at.x) + (1 - even) * (4 - 8 * at.y), at.z)
        second = (at.d + even * (4 - 8 * at.y) + (1 - even) * (2 - 4 * at.x), at.z)
        return even, f, s, first, second, i % ring

    def core_copy(i):
        slot = i % ring
        return remote(part.at[slot, 1 - at.core], from_core.at[i], c_send.at[i], c_recv.at[i], at.over_core)

    def first_copy(i):
        even, f, s, first, second, slot = places(i)
        return remote(part.at[slot, at.core, 1 - f], from_first.at[i], f_send.at[i], f_recv.at[i], first)

    def second_copy(i):
        even, f, s, first, second, slot = places(i)
        return remote(part.at[slot, at.core, f, 1 - s], from_second.at[i], s_send.at[i], s_recv.at[i], second)

    def out_copy(i):
        return remote(zsum.at[i], from_near.at[i], n_send.at[i], n_recv.at[i], at.near)

    def far_copy(i):
        return remote(zsum.at[i], from_far.at[i], m_send.at[i], m_recv.at[i], at.far)

    def back_copy(i):
        return remote(from_far.at[i], from_near.at[i], n_send.at[i], n_recv.at[i], at.near)

    def plus(a, b):
        return (a.astype(F32) + b.astype(F32)).astype(BF16)

    def product(left, right):
        even = 1 - tick % 2
        slot = tick % ring
        half = width // 2
        for h in range(2):
            rows = nn(left[h * half : (h + 1) * half, :], right)
            for j in range(4):
                d = h * 4 + j
                c, x, y = d % 2, (d // 2) % 2, d // 4
                a = x * even + y * (1 - even)
                b = y * even + x * (1 - even)
                part[slot, c, a, b] = rows[j * block : (j + 1) * block].astype(BF16)
        core_copy(tick).start()

    starts = (0,) + cuts[:-1]
    operands = ((n2t_ref, gh_ref), (glt_ref, act_ref), (ctxt_ref, glc_ref), (n1t_ref, guc_ref))
    for (left, right), lo, hi in zip(operands, starts, cuts):
        @pl.when((tick >= lo) & (tick < hi))
        def _():
            product(left[...], right[0] if right is guc_ref else right[...])

    def when(lag, f):
        i = tick - lag

        @pl.when((i >= 0) & (i < chunks))
        def _():
            f(i)

    def core_step(i):
        even, f, s, first, second, slot = places(i)
        core_copy(i).wait()
        for a in range(2):
            for b in range(2):
                part[slot, at.core, a, b] = plus(part[slot, at.core, a, b], from_core[i, a, b])
        first_copy(i).start()

    def first_step(i):
        even, f, s, first, second, slot = places(i)
        first_copy(i).wait()
        for b in range(2):
            part[slot, at.core, f, b] = plus(part[slot, at.core, f, b], from_first[i, b])
        second_copy(i).start()

    def second_step(i):
        even, f, s, first, second, slot = places(i)
        second_copy(i).wait()
        zsum[i] = plus(part[slot, at.core, f, s], from_second[i])

        @pl.when(at.inner == 0)
        def _():
            out_copy(i).start()

    def near_step(i):
        @pl.when(at.inner == 1)
        def _():
            out_copy(i).wait_recv()
            zsum[i] = plus(zsum[i], from_near[i])
            far_copy(i).start()

    def far_step(i):
        @pl.when(at.inner == 1)
        def _():
            far_copy(i).wait()
            total = plus(zsum[i], from_far[i])
            from_far[i] = total
            back_copy(i).start()
            grads_ref[i] = total.astype(F32) / held_n[5, 0:1, 0:1]

        @pl.when(at.inner == 0)
        def _():
            out_copy(i).wait_send()

    def back_step(i):
        @pl.when(at.inner == 0)
        def _():
            back_copy(i).wait_recv()
            grads_ref[i] = from_near[i].astype(F32) / held_n[5, 0:1, 0:1]

        @pl.when(at.inner == 1)
        def _():
            back_copy(i).wait_send()

    when(LAGS["core"], core_step)

    @pl.when(tick == 0)
    def _():
        gain1[...] = jnp.zeros_like(gain1)
        shift1[...] = jnp.zeros_like(shift1)
        bqkv[...] = jnp.zeros_like(bqkv)

    @pl.when(tick < row_ticks)
    def _():
        out_ref[...] = (base_ref[...] + nn(ctx_ref[...], wout_ref[...])).astype(BF16)
        g1 = nt(gu_ref[0], wqkv_ref[:, :width])
        g1 = g1 + nt(gu_ref[1], wqkv_ref[:, width : 2 * width])
        g1 = g1 + nt(gu_ref[2], wqkv_ref[:, 2 * width :])
        x = x_ref[...].astype(F32)
        centred = x - jnp.mean(x, axis=1, keepdims=True)
        r = lax.rsqrt(jnp.mean(centred * centred, axis=1, keepdims=True) + EPSILON)
        n = centred * r
        gain1[...] += jnp.sum(g1 * n, axis=0, keepdims=True)
        shift1[...] += jnp.sum(g1, axis=0, keepdims=True)
        for j in range(3):
            bqkv[:, j * width : (j + 1) * width] += jnp.sum(gu_ref[j].astype(F32), axis=0, keepdims=True)
        t = g1 * g1_ref[...] + t2_ref[...]
        dx = r * (t - jnp.mean(t, axis=1, keepdims=True) - n * jnp.mean(t * n, axis=1, keepdims=True))
        ig_ref[...] = (gl_ref[...].astype(F32) + dx).astype(BF16)

    when(LAGS["first"], first_step)
    when(LAGS["second"], second_step)
    when(LAGS["z"], near_step)
    when(LAGS["mid"], far_step)
    when(LAGS["back"], back_step)

    Everywhere(at, held_n, come_n, n_s, n_r).hop(tick)

    @pl.when(tick == row_ticks)
    def _():
        held_v[0] = jnp.zeros(held_v.shape[1:], F32)
        held_v[0, 0:1, :] = bup_ref[...]
        held_v[0, 1:2, : 3 * width] = bqkv[...]
        held_v[0, 1:2, 3 * width :] = bout_ref[...]
        held_v[0, 2:3, :width] = gain1[...]
        held_v[0, 2:3, width : 2 * width] = shift1[...]
        held_v[0, 2:3, 2 * width : 3 * width] = gain2_ref[...]
        held_v[0, 2:3, 3 * width :] = shift2_ref[...]

    Everywhere(at, held_v, come_v, v_s, v_r).hop(tick - row_ticks)

    @pl.when(tick == row_ticks + 6)
    def _():
        vec_ref[...] = held_v[5] / held_n[5, 0:1, 0:1]


def reduce(count, n1t, n2t, glt, ctxt, gh, act, gl, gu, x, base, t2, ctx, wqkv, wout, g1, gain2, shift2, bup, bout):
    length, width = x.shape
    ff = gh.shape[1]
    block = width // 8
    counts = (ff // CHUNK, ff // CHUNK, width // CHUNK, 3 * width // CHUNK)
    cuts = tuple(int(c) for c in np.cumsum(counts))
    chunks = cuts[-1]
    per = width // CHUNK
    rows = 128
    row_ticks = length // rows
    ticks = chunks + LAGS["back"]
    ring = 8

    def cols(array_chunks, begin):
        return pl.BlockSpec((length, CHUNK), lambda t: (0, jnp.clip(t - begin, 0, array_chunks - 1)))

    def row(cols):
        return pl.BlockSpec((rows, cols), lambda t: (jnp.minimum(t, row_ticks - 1), 0))

    def whole(a):
        return pl.BlockSpec(a.shape, lambda t: (0,) * a.ndim, pipeline_mode=pl.Buffered(1))

    def gu_cols(t):
        j = jnp.clip(t - cuts[2], 0, counts[3] - 1)
        return (j // per, 0, j % per)

    g1 = g1.reshape(1, -1)
    s = jax.ShapeDtypeStruct
    dma = pltpu.SemaphoreType.DMA
    hops = Everywhere.HOPS
    return pl.pallas_call(
        functools.partial(reduce_body, cuts=cuts, row_ticks=row_ticks),
        grid=(ticks,),
        in_specs=[pl.BlockSpec(memory_space=pltpu.SMEM), whole(n1t), whole(n2t), whole(glt), whole(ctxt),
                  cols(counts[0], 0), cols(counts[1], cuts[0]), cols(counts[2], cuts[1]),
                  pl.BlockSpec((1, length, CHUNK), gu_cols),
                  row(width), row(width), row(width), row(width), row(width),
                  pl.BlockSpec((3, rows, width), lambda t: (0, jnp.minimum(t, row_ticks - 1), 0)),
                  whole(wqkv), whole(wout), whole(g1), whole(gain2), whole(shift2), whole(bup), whole(bout)],
        out_specs=[row(width), row(width),
                   pl.BlockSpec((chunks, block, CHUNK), lambda t: (0, 0, 0), pipeline_mode=pl.Buffered(1)),
                   pl.BlockSpec((8, ff), lambda t: (0, 0), pipeline_mode=pl.Buffered(1))],
        out_shape=[s((length, width), BF16), s((length, width), BF16), s((chunks, block, CHUNK), F32), s((8, ff), F32)],
        scratch_shapes=[
            pltpu.VMEM((ring, 2, 2, 2, block, CHUNK), BF16),
            pltpu.VMEM((chunks, 2, 2, block, CHUNK), BF16),
            pltpu.VMEM((chunks, 2, block, CHUNK), BF16),
            pltpu.VMEM((chunks, block, CHUNK), BF16),
            pltpu.VMEM((chunks, block, CHUNK), BF16),
            pltpu.VMEM((chunks, block, CHUNK), BF16),
            pltpu.VMEM((chunks, block, CHUNK), BF16),
        ] + [dma((chunks,))] * 10 + [
            pltpu.VMEM((hops, 8, 128), F32), pltpu.VMEM((hops, 8, 128), F32),
            pltpu.VMEM((hops, 8, ff), F32), pltpu.VMEM((hops, 8, ff), F32),
            dma((hops,)), dma((hops,)), dma((hops,)), dma((hops,)),
            pltpu.VMEM((1, width), F32), pltpu.VMEM((1, width), F32), pltpu.VMEM((1, 3 * width), F32),
        ],
        compiler_params=pltpu.CompilerParams(vmem_limit_bytes=60 * 2**20, collective_id=0, has_side_effects=True),
        name="reduce",
    )(count, n1t, n2t, glt, ctxt, gh, act, gl, gu, x, gl, base, t2, ctx, gu, wqkv, wout, g1, gain2, shift2, bup, bout)


def by_collectives(count, n1t, n2t, glt, ctxt, gh, act, gl, gu, x, base, t2, ctx, wqkv, wout, g1, gain2, shift2, bup, bout):
    width = x.shape[1]
    flat = jnp.concatenate([gu[0], gu[1], gu[2]], axis=1)
    out = (base + nn(ctx, wout)).astype(BF16)
    grad_one = nt(flat, wqkv)
    x = x.astype(F32)
    centred = x - jnp.mean(x, axis=1, keepdims=True)
    r = lax.rsqrt(jnp.mean(centred * centred, axis=1, keepdims=True) + EPSILON)
    n = centred * r
    t = grad_one * g1 + t2
    dx = r * (t - jnp.mean(t, axis=1, keepdims=True) - n * jnp.mean(t * n, axis=1, keepdims=True))
    input_grad = (gl.astype(F32) + dx).astype(BF16)
    packed = jnp.concatenate([bup[0], jnp.sum(flat, axis=0, dtype=F32), bout[0], jnp.sum(grad_one * n, axis=0),
                              jnp.sum(grad_one, axis=0), gain2[0], shift2[0], count.astype(F32)])
    packed = lax.psum(packed, ("dp", "rows"))
    part = jnp.concatenate([nn(n2t, gh), nn(glt, act), nn(ctxt, gl), nn(n1t, flat)], axis=1).astype(BF16)
    grads = lax.psum(lax.psum_scatter(part, "dp", scatter_dimension=0, tiled=True), "rows")
    return out, input_grad, grads.astype(F32) / packed[-1], (packed[:-1] / packed[-1]).reshape(3, -1)


def by_kernel(*operands):
    out, input_grad, grads, vec = reduce(*operands)
    grads = jnp.swapaxes(grads, 0, 1).reshape(grads.shape[1], -1)
    return out, input_grad, grads, vec


def shards(tokens, segment_ids, true_counts, regroup, cotangent, ln1_gain, ln1_bias, qkv_weight, qkv_bias, out_weight,
           out_bias, ln2_gain, ln2_bias, up_weight, up_bias, down_weight, down_bias):
    length, width = cotangent.shape
    ff = up_weight.shape[1]
    want = jnp.full((8, 128), regroup[0] % lax.axis_size("rows"), jnp.int32)
    cosine, sine = (jnp.asarray(t) for t in rotary_tables(length))
    (arrived, q, k, v, gc, n1t, n2t, glt, gl, act, gh, base, t2, gain2, shift2, bias_up, bias_out) = front(
        true_counts, want, tokens, cotangent, cosine, sine, ln1_gain, ln1_bias, qkv_weight, qkv_bias, out_weight, out_bias,
        ln2_gain, ln2_bias, up_weight, up_bias, down_weight, down_bias)
    ctx, ctxt, gu = attention(q, k, v, gc, segment_ids, cosine, sine, rows=256)
    last = by_kernel if (lax.axis_size("dp"), lax.axis_size("rows")) == (8, 4) else by_collectives
    out, input_grad, grads, vec = last(true_counts, n1t, n2t, glt, ctxt, gh, act, gl, gu, arrived, base, t2, ctx, qkv_weight,
                                       out_weight, ln1_gain, gain2, shift2, bias_up, bias_out)
    up, down = grads[:, :ff], grads[:, ff : 2 * ff].T
    low, qkv = grads[:, 2 * ff : 2 * ff + width], grads[:, 2 * ff + width :]
    gains = vec[2].reshape(4, width)
    bias_out = vec[1, 3 * width :]
    return (out, input_grad, gains[0], gains[1], qkv, vec[1, : 3 * width], low, bias_out, gains[2], gains[3], up, vec[0], down,
            bias_out)


def solution(mesh):
    both = ("dp", "rows")
    placed = (P(both, None), P(both), P(both), P(both), P(both, None)) + (P(),) * 12
    return jax.shard_map(
        shards, mesh=mesh, in_specs=placed,
        out_specs=(P(both, None), P(both, None), P(), P(), P("dp", None), P(), P("dp", None), P(), P(), P(), P("dp", None), P(),
                   P(None, "dp"), P()),
        check_vma=False)
```

```python
import functools
import numpy as np
import jax
import jax.numpy as jnp
from jax import lax
from jax.experimental import pallas as pl
from jax.experimental.pallas import tpu as pltpu
from jax.sharding import PartitionSpec as P

HEAD_DIM = 64
ROT = 16
PAIR = 128
EPSILON = 1e-05
EXCLUDED = -1e30
F32 = jnp.float32
BF16 = jnp.bfloat16
MESH = pl.DeviceIdType.MESH


def remote(src, dst, send, recv, to):
    return pltpu.make_async_remote_copy(src_ref=src, dst_ref=dst, send_sem=send, recv_sem=recv, device_id=to, device_id_type=MESH)


def nn(a, b):
    return lax.dot_general(a, b, (((1,), (0,)), ((), ())), preferred_element_type=F32)


def nt(a, b):
    return lax.dot_general(a, b, (((1,), (1,)), ((), ())), preferred_element_type=F32)


def tn(a, b):
    return lax.dot_general(a, b, (((0,), (0,)), ((), ())), preferred_element_type=F32)


def rotary_tables(length):
    half = ROT // 2
    placed = np.arange(length, dtype=np.float32)
    rates = np.exp(np.arange(half, dtype=np.float32) * np.float32(-2.0 / ROT) * np.log(np.float32(10000.0)))
    phases = placed[:, None] * rates[None, :].astype(np.float32)
    cosine = np.ones((length, HEAD_DIM), np.float32)
    sine = np.zeros((length, HEAD_DIM), np.float32)
    cosine[:, :half] = np.cos(phases)
    cosine[:, half:ROT] = np.cos(phases)
    sine[:, :half] = -np.sin(phases)
    sine[:, half:ROT] = np.sin(phases)
    return np.tile(cosine, (1, PAIR // HEAD_DIM)), np.tile(sine, (1, PAIR // HEAD_DIM))


def turned(u):
    lane = lax.broadcasted_iota(jnp.int32, u.shape, 1) % HEAD_DIM
    half = ROT // 2
    return jnp.where(lane < half, pltpu.roll(u, PAIR - half, 1), pltpu.roll(u, half, 1))


def gelu_parts(h):
    e = jnp.exp(h * h * -0.5)
    t = 1.0 / (1.0 + 0.2316418882 * jnp.abs(h))
    poly = t * (0.127414796 + t * (-0.142248368 + t * (0.7107068705 + t * (-0.7265760135 + t * 0.5307027145))))
    tail = poly * e
    phi = jnp.where(h >= 0, 1.0 - tail, tail)
    return h * phi, phi + h * (e * 0.3989422804014327)


def front_body(count_ref, want_ref, own_ref, cot_ref, cos_ref, sin_ref, g1_vec, b1_vec, bqkv_vec, bout_vec, g2_vec, b2_vec,
               bup_vec, bdown_vec, wqkv_hbm, wout_hbm, wup_hbm, wdown_hbm,
               x_ref, q_ref, k_ref, v_ref, gc_ref, n1t_ref, n2t_ref, glt_ref, gl_ref, act_ref, gh_ref, base_ref, t2_ref,
               gain2_ref, shift2_ref, bup_out, bout_out,
               wqkv_ref, wout_ref, wup_ref, wdown_ref, wants, from_near, from_half, to_inner, to_end,
               g1_ref, b1_ref, bqkv_ref, bout_ref, g2_ref, b2_ref, bup_ref, bdown_ref, w_sem, want_send, want_recv, near_send, near_recv, inner_send, end_send, half_recv, *, tile):
    step = pl.program_id(0)
    steps = pl.num_programs(0)
    rows, width = cot_ref.shape
    pairs = width // PAIR
    ff = wup_ref.shape[1]
    chunks = own_ref.shape[0] // rows
    d, z = lax.axis_index("dp"), lax.axis_index("rows")
    inner = (z + 1) // 2 % 2
    near = z + 1 - 2 * (z % 2)
    other_inner, other_end = 3 - z, 6 - 3 * z
    loads = [pltpu.make_async_copy(src, dst, w_sem.at[j]) for j, (src, dst) in enumerate(
        ((wqkv_hbm, wqkv_ref), (wout_hbm, wout_ref), (wup_hbm, wup_ref), (wdown_hbm, wdown_ref)))]

    def span(i):
        return pl.ds(pl.multiple_of(i * rows, rows), rows)

    def want_copy(j):
        to = lax.rem(z + j, 4)
        return remote(wants.at[0], wants.at[j], want_send.at[j], want_recv.at[j], (d, to))

    def near_copy(i):
        return remote(own_ref.at[span(i)], from_near.at[span(i)], near_send.at[i], near_recv.at[i], (d, near))

    def inner_copy(i):
        return remote(to_inner.at[span(i)], from_half.at[span(i)], inner_send.at[i], half_recv.at[i], (d, other_inner))

    def end_copy(i):
        return remote(to_end.at[span(i)], from_half.at[span(i)], end_send.at[i], half_recv.at[i], (d, other_end))

    def wanted(by):
        return wants[lax.rem(z - by + 4, 4), 0:1, 0:1]

    def relay(i):
        @pl.when(inner == 1)
        def _():
            near_copy(i).wait_recv()
            mine = own_ref[span(i), :].astype(F32)
            theirs = from_near[span(i), :].astype(F32)
            to_end[span(i), :] = jnp.where(wanted(other_end) == near, theirs, mine).astype(BF16)
            end_copy(i).start()
            to_inner[span(i), :] = jnp.where(wanted(other_inner) == near, theirs, mine).astype(BF16)
            inner_copy(i).start()

    @pl.when(step == 0)
    def _():
        barrier = pltpu.get_barrier_semaphore()
        for j in (1, 2, 3):
            pl.semaphore_signal(barrier, inc=1, device_id=(d, lax.rem(z + j, 4)), device_id_type=MESH)
        wants[0] = jnp.full(wants.shape[1:], want_ref[0] % 4, jnp.int32)
        pl.semaphore_wait(barrier, 3)
        for j in (1, 2, 3):
            want_copy(j).start()

        def hand(i, carry):
            near_copy(i).start()
            return carry

        lax.fori_loop(0, chunks, hand, 0)
        for load in loads:
            load.start()
        for j in (1, 2, 3):
            want_copy(j).wait()
        relay(0)
        for vec, ref in ((g1_vec, g1_ref), (b1_vec, b1_ref), (bqkv_vec, bqkv_ref), (bout_vec, bout_ref), (g2_vec, g2_ref),
                         (b2_vec, b2_ref), (bup_vec, bup_ref), (bdown_vec, bdown_ref)):
            ref[...] = vec[...].reshape(1, -1)
        gain2_ref[...] = jnp.zeros_like(gain2_ref)
        shift2_ref[...] = jnp.zeros_like(shift2_ref)
        bup_out[...] = jnp.zeros_like(bup_out)
        bout_out[...] = jnp.zeros_like(bout_out)

    @pl.when(step + 1 < chunks)
    def _():
        relay(step + 1)

    @pl.when(step == 0)
    def _():
        for load in loads:
            load.wait()

    place = step * rows + lax.broadcasted_iota(jnp.int32, (rows, 1), 0)
    gl = jnp.where(place < count_ref[0], cot_ref[...].astype(F32), 0.0)
    gl16 = gl.astype(BF16)
    gl_ref[...] = gl16
    glt_ref[...] = gl16.T
    bout_out[...] += jnp.sum(gl, axis=0, keepdims=True)
    for p in range(pairs):
        gc_ref[p] = nt(gl16, wout_ref[p * PAIR : (p + 1) * PAIR, :]).astype(BF16)

    @pl.when(inner == 0)
    def _():
        near_copy(step).wait_recv()

    inner_copy(step).wait_recv()
    source = wanted(z)
    x = jnp.where(source == near, from_near[span(step), :].astype(F32), from_half[span(step), :].astype(F32))
    x = jnp.where(source == z, own_ref[span(step), :].astype(F32), x)
    x_ref[...] = x.astype(BF16)
    centred = x - jnp.mean(x, axis=1, keepdims=True)
    r = lax.rsqrt(jnp.mean(centred * centred, axis=1, keepdims=True) + EPSILON)
    n = centred * r
    n1 = (n * g1_ref[...] + b1_ref[...]).astype(BF16)
    n2 = (n * g2_ref[...] + b2_ref[...]).astype(BF16)
    n1t_ref[...] = n1.T
    n2t_ref[...] = n2.T
    cosine, sine = cos_ref[...], sin_ref[...]
    for p in range(pairs):
        for which, ref in enumerate((q_ref, k_ref, v_ref)):
            wide = slice(which * width + p * PAIR, which * width + (p + 1) * PAIR)
            u = nn(n1, wqkv_ref[:, wide]) + bqkv_ref[:, wide]
            if which < 2:
                u = u * cosine + turned(u) * sine
            if which == 0:
                u = u * (HEAD_DIM ** -0.5)
            ref[p] = u.astype(BF16)
    mlp = x + (bdown_ref[...] + bout_ref[...])
    grad_two = jnp.zeros((rows, width), F32)
    for f in range(0, ff, tile):
        cols = slice(f, f + tile)
        h = nn(n2, wup_ref[:, cols]) + bup_ref[:, cols]
        ga = nt(gl16, wdown_ref[cols, :])
        a, slope = gelu_parts(h)
        a16 = a.astype(BF16)
        gh = ga * slope
        gh16 = gh.astype(BF16)
        act_ref[:, cols] = a16
        gh_ref[:, cols] = gh16
        bup_out[:, cols] += jnp.sum(gh16.astype(F32), axis=0, keepdims=True)
        mlp = mlp + nn(a16, wdown_ref[cols, :])
        grad_two = grad_two + nt(gh16, wup_ref[:, cols])
    base_ref[...] = mlp
    t2_ref[...] = grad_two * g2_ref[...]
    gain2_ref[...] += jnp.sum(grad_two * n, axis=0, keepdims=True)
    shift2_ref[...] += jnp.sum(grad_two, axis=0, keepdims=True)

    @pl.when(step == steps - 1)
    def _():
        def done(i, carry):
            near_copy(i).wait_send()

            @pl.when(inner == 1)
            def _():
                inner_copy(i).wait_send()
                end_copy(i).wait_send()
            return carry

        lax.fori_loop(0, chunks, done, 0)


def front(count, want, own, cot, cosine, sine, g1, b1, wqkv, bqkv, wout, bout, g2, b2, wup, bup, wdown, bdown, rows=128, tile=512):
    length, width = own.shape
    ff = wup.shape[1]
    pairs = width // PAIR
    chunks = length // rows

    def row(cols):
        return pl.BlockSpec((rows, cols), lambda i: (i, 0))

    def whole(a):
        return pl.BlockSpec(a.shape, lambda i: (0,) * a.ndim, pipeline_mode=pl.Buffered(1))

    heads = pl.BlockSpec((pairs, rows, PAIR), lambda i: (0, i, 0))
    down = pl.BlockSpec((width, rows), lambda i: (0, i))

    def vec(cols):
        return pl.BlockSpec((1, cols), lambda i: (0, 0))

    vectors = (g1, b1, bqkv, bout, g2, b2, bup, bdown)
    weights = (wqkv, wout, wup, wdown)
    s = jax.ShapeDtypeStruct
    dma = pltpu.SemaphoreType.DMA
    return pl.pallas_call(
        functools.partial(front_body, tile=tile),
        grid=(chunks,),
        in_specs=[pl.BlockSpec(memory_space=pltpu.SMEM), pl.BlockSpec(memory_space=pltpu.SMEM), whole(own), row(width), row(PAIR), row(PAIR)]
        + [whole(a) for a in vectors] + [pl.BlockSpec(memory_space=pl.ANY)] * 4,
        out_specs=[row(width)] + [heads] * 4 + [down] * 3 + [row(width)] + [row(ff)] * 2 + [row(width)] * 2
        + [vec(width), vec(width), vec(ff), vec(width)],
        out_shape=[s((length, width), BF16)] + [s((pairs, length, PAIR), BF16)] * 4 + [s((width, length), BF16)] * 3
        + [s((length, width), BF16)] + [s((length, ff), BF16)] * 2
        + [s((length, width), F32)] * 2 + [s((1, width), F32), s((1, width), F32), s((1, ff), F32), s((1, width), F32)],
        scratch_shapes=[pltpu.VMEM(w.shape, BF16) for w in weights]
        + [pltpu.VMEM((4, 8, 128), jnp.int32)] + [pltpu.VMEM((length, width), BF16)] * 4
        + [pltpu.VMEM((1, v.shape[0]), F32) for v in vectors] + [dma((4,)), dma((4,)), dma((4,))] + [dma((chunks,))] * 5,
        compiler_params=pltpu.CompilerParams(vmem_limit_bytes=60 * 2**20, collective_id=1, has_side_effects=True),
        name="front",
    )(count, want, own, cot, cosine, sine, *vectors, *weights)


def attention_body(q_ref, k_ref, v_ref, gc_ref, seg_ref, cos_ref, sin_ref,
                   ctx_ref, ctxt_ref, gu_ref, dk_acc, dv_acc, segc_ref, segr_ref, first_ref, *, rows):
    group, length, _ = q_ref.shape
    total = length // rows
    each = range(group)

    @pl.when(pl.program_id(0) == 0)
    def _():
        seg = seg_ref[...].reshape(1, -1)
        segr_ref[...] = seg
        segc_ref[...] = jnp.broadcast_to(seg, (8, length)).T[:, :1]
        wide = seg.astype(F32)
        for b in range(total):
            before = jnp.sum(jnp.where(wide < wide[:, b * rows : b * rows + 1], 1.0, 0.0))
            first_ref[b] = before.astype(jnp.int32) // rows

    lane = lax.broadcasted_iota(jnp.int32, (rows, PAIR), 1)
    low = lane < HEAD_DIM
    dk_acc[...] = jnp.zeros_like(dk_acc)
    dv_acc[...] = jnp.zeros_like(dv_acc)

    def both(ref, h, begin):
        t = ref[h, pl.ds(begin, rows), :]
        zero = jnp.zeros_like(t)
        return jnp.concatenate([jnp.where(low, t, zero), jnp.where(low, zero, t)], axis=0)

    def block(b, blocks):
        begin = pl.multiple_of(b * rows, rows)
        start = pl.multiple_of((b + 1 - blocks) * rows, rows)
        span = blocks * rows
        q2 = [both(q_ref, h, begin) for h in each]
        g2 = [both(gc_ref, h, begin) for h in each]
        k = [k_ref[h, pl.ds(start, span), :] for h in each]
        v = [v_ref[h, pl.ds(start, span), :] for h in each]
        segt = segc_ref[pl.ds(begin, rows), :]
        segs = segr_ref[:, pl.ds(start, span)]
        t_at = begin + lax.broadcasted_iota(jnp.int32, (rows, span), 0)
        s_at = start + lax.broadcasted_iota(jnp.int32, (rows, span), 1)
        allowed = (segt == segs) & (s_at <= t_at)
        allowed = jnp.concatenate([allowed, allowed], axis=0)
        scores = [jnp.where(allowed, nt(q2[h], k[h]), EXCLUDED) for h in each]
        dp = [nt(g2[h], v[h]) for h in each]
        e = [jnp.exp(scores[h] - jnp.max(scores[h], axis=1, keepdims=True)) for h in each]
        p = [e[h] * (1.0 / jnp.sum(e[h], axis=1, keepdims=True)) for h in each]
        p16 = [p[h].astype(BF16) for h in each]
        c2 = [nn(p16[h], v[h]) for h in each]
        for h in each:
            dv_acc[h, pl.ds(start, span), :] += tn(p16[h], g2[h])
        w = [p[h] * dp[h] for h in each]
        ds16 = [(w[h] - p[h] * jnp.sum(w[h], axis=1, keepdims=True)).astype(BF16) for h in each]
        d2 = [nn(ds16[h], k[h]) for h in each]
        for h in each:
            dk_acc[h, pl.ds(start, span), :] += tn(ds16[h], q2[h])
        cosine = cos_ref[pl.ds(begin, rows), :]
        sine = sin_ref[pl.ds(begin, rows), :]
        for h in each:
            cols = slice(h * PAIR, (h + 1) * PAIR)
            context = jnp.where(low, c2[h][:rows], c2[h][rows:]).astype(BF16)
            ctx_ref[pl.ds(begin, rows), cols] = context
            ctxt_ref[cols, pl.ds(begin, rows)] = context.T
            dq = jnp.where(low, d2[h][:rows], d2[h][rows:]) * (HEAD_DIM ** -0.5)
            gu_ref[0, pl.ds(begin, rows), cols] = (dq * cosine - turned(dq) * sine).astype(BF16)

    def loop(b, carry):
        count = b + 1 - first_ref[b]
        for blocks in range(1, total + 1):
            @pl.when(count == blocks)
            def _():
                block(b, blocks)
        return carry

    lax.fori_loop(0, total, loop, 0)
    for h in each:
        cols = slice(h * PAIR, (h + 1) * PAIR)
        dk = dk_acc[h]
        gu_ref[1, :, cols] = (dk * cos_ref[...] - turned(dk) * sin_ref[...]).astype(BF16)
        gu_ref[2, :, cols] = dv_acc[h].astype(BF16)


def attention(q, k, v, gc, segment, cosine, sine, rows=256, group=2):
    pairs, length, _ = q.shape
    head = pl.BlockSpec((group, length, PAIR), lambda h: (h, 0, 0))
    cols = pl.BlockSpec((length, group * PAIR), lambda h: (0, h))
    s = jax.ShapeDtypeStruct
    width = pairs * PAIR

    def whole(a):
        return pl.BlockSpec(a.shape, lambda h: (0,) * a.ndim, pipeline_mode=pl.Buffered(1))

    return pl.pallas_call(
        functools.partial(attention_body, rows=rows),
        grid=(pairs // group,),
        in_specs=[head] * 4 + [whole(segment), whole(cosine), whole(sine)],
        out_specs=[cols, pl.BlockSpec((group * PAIR, length), lambda h: (h, 0)),
                   pl.BlockSpec((3, length, group * PAIR), lambda h: (0, 0, h))],
        scratch_shapes=[pltpu.VMEM((group, length, PAIR), F32)] * 2
        + [pltpu.VMEM((length, 1), jnp.int32), pltpu.VMEM((1, length), jnp.int32), pltpu.SMEM((length // rows,), jnp.int32)],
        out_shape=[s((length, width), BF16), s((width, length), BF16), s((3, length, width), BF16)],
        compiler_params=pltpu.CompilerParams(vmem_limit_bytes=56 * 2**20),
        name="attention",
    )(q, k, v, gc, segment, cosine, sine)


CHUNK = 384


class Line:
    def __init__(self):
        self.d = lax.axis_index("dp")
        self.z = lax.axis_index("rows")
        self.core = self.d % 2
        self.x = (self.d // 2) % 2
        self.y = self.d // 4
        self.over_core = (self.d + 1 - 2 * self.core, self.z)
        self.over_x = (self.d + 2 - 4 * self.x, self.z)
        self.over_y = (self.d + 4 - 8 * self.y, self.z)
        self.inner = (self.z + 1) // 2 % 2
        self.near = (self.d, self.z + 1 - 2 * (self.z % 2))
        self.far = (self.d, 3 - self.z)


class Everywhere:
    HOPS = 7

    def __init__(self, at, held, come, send, recv):
        self.at, self.held, self.come, self.send, self.recv = at, held, come, send, recv

    def copy(self, hop, to):
        return remote(self.held.at[hop], self.come.at[hop], self.send.at[hop], self.recv.at[hop], to)

    def take(self, hop, to):
        self.copy(hop, to).wait()
        self.held[hop + 1] = self.held[hop] + self.come[hop]

    def hop(self, tick, spacing):
        at = self.at
        over = (at.over_core, at.over_x, at.over_y)

        @pl.when(tick == 0)
        def _():
            self.copy(0, over[0]).start()

        for j in (1, 2):
            @pl.when(tick == j * spacing)
            def _():
                self.take(j - 1, over[j - 1])
                self.copy(j, over[j]).start()

        @pl.when(tick == 3 * spacing)
        def _():
            self.take(2, over[2])

            @pl.when(at.inner == 0)
            def _():
                self.copy(3, at.near).start()

        @pl.when((tick == 4 * spacing) & (at.inner == 1))
        def _():
            self.copy(3, at.near).wait_recv()
            self.held[4] = self.held[3] + self.come[3]
            self.copy(4, at.far).start()

        @pl.when((tick == 4 * spacing) & (at.inner == 0))
        def _():
            self.copy(3, at.near).wait_send()

        @pl.when((tick == 5 * spacing) & (at.inner == 1))
        def _():
            self.take(4, at.far)
            self.copy(5, at.near).start()

        @pl.when(tick == 6 * spacing)
        def _():
            @pl.when(at.inner == 1)
            def _():
                self.copy(5, at.near).wait_send()

            @pl.when(at.inner == 0)
            def _():
                self.copy(5, at.near).wait_recv()
                self.held[5] = self.come[5]


LAGS = dict(core=1, first=4, second=7, z=9, mid=11, back=13)
SPACING = 3


def reduce_body(count_ref, gh_ref, act_ref, glc_ref, guc_ref, x_ref, gl_ref, base_ref, t2_ref, ctx_ref, gu_ref, g1_ref,
                gain2_ref, shift2_ref, bup_ref, bout_ref, n2t_hbm, wout_hbm, wqkv_hbm, glt_hbm, ctxt_hbm, n1t_hbm,
                out_ref, ig_ref, total_ref, vec_ref,
                n2t_ref, wout_ref, wqkv_ref, glt_ref, ctxt_ref, n1t_ref, load_sem, part, from_core, from_first, from_second, zsum, from_near, from_far,
                c_send, c_recv, f_send, f_recv, s_send, s_recv, n_send, n_recv, m_send, m_recv,
                held_v, come_v, v_s, v_r, gain1, shift1, bqkv, *, cuts, row_ticks):
    tick = pl.program_id(0)
    at = Line()
    chunks = cuts[-1]
    ring = part.shape[0]
    width = wout_ref.shape[0]
    block = width // 8

    loads = [pltpu.make_async_copy(src, dst, load_sem.at[j]) for j, (src, dst) in enumerate(
        ((n2t_hbm, n2t_ref), (wout_hbm, wout_ref), (wqkv_hbm, wqkv_ref), (glt_hbm, glt_ref), (ctxt_hbm, ctxt_ref),
         (n1t_hbm, n1t_ref)))]

    @pl.when(tick == 0)
    def _():
        loads[0].start()
        barrier = pltpu.get_barrier_semaphore()
        for to in (at.over_core, at.over_x, at.over_y, at.near):
            pl.semaphore_signal(barrier, inc=1, device_id=to, device_id_type=MESH)

        @pl.when(at.inner == 1)
        def _():
            pl.semaphore_signal(barrier, inc=1, device_id=at.far, device_id_type=MESH)
            pl.semaphore_wait(barrier, 5)

        @pl.when(at.inner == 0)
        def _():
            pl.semaphore_wait(barrier, 4)

        for load in loads[1:]:
            load.start()

    def places(i):
        even = 1 - i % 2
        f = at.x * even + at.y * (1 - even)
        s = at.y * even + at.x * (1 - even)
        first = (at.d + even * (2 - 4 * at.x) + (1 - even) * (4 - 8 * at.y), at.z)
        second = (at.d + even * (4 - 8 * at.y) + (1 - even) * (2 - 4 * at.x), at.z)
        return even, f, s, first, second, i % ring

    def core_copy(i):
        slot = i % ring
        return remote(part.at[slot, 1 - at.core], from_core.at[i], c_send.at[i], c_recv.at[i], at.over_core)

    def first_copy(i):
        even, f, s, first, second, slot = places(i)
        return remote(part.at[slot, at.core, 1 - f], from_first.at[i], f_send.at[i], f_recv.at[i], first)

    def second_copy(i):
        even, f, s, first, second, slot = places(i)
        return remote(part.at[slot, at.core, f, 1 - s], from_second.at[i], s_send.at[i], s_recv.at[i], second)

    def out_copy(i):
        return remote(zsum.at[i], from_near.at[i], n_send.at[i], n_recv.at[i], at.near)

    def far_copy(i):
        return remote(zsum.at[i], from_far.at[i], m_send.at[i], m_recv.at[i], at.far)

    def back_copy(i):
        return remote(from_far.at[i], from_near.at[i], n_send.at[i], n_recv.at[i], at.near)

    def plus(a, b):
        return (a.astype(F32) + b.astype(F32)).astype(BF16)

    def product(left, right):
        even = 1 - tick % 2
        slot = tick % ring
        half = width // 2
        for h in range(2):
            rows = nn(left[h * half : (h + 1) * half, :], right)
            for j in range(4):
                d = h * 4 + j
                c, x, y = d % 2, (d // 2) % 2, d // 4
                a = x * even + y * (1 - even)
                b = y * even + x * (1 - even)
                part[slot, c, a, b] = rows[j * block : (j + 1) * block].astype(BF16)
        core_copy(tick).start()

    @pl.when(tick == 0)
    def _():
        loads[0].wait()

    @pl.when(tick == 1)
    def _():
        for load in loads[1:]:
            load.wait()

    starts = (0,) + cuts[:-1]
    operands = ((n2t_ref, gh_ref), (glt_ref, act_ref), (ctxt_ref, glc_ref), (n1t_ref, guc_ref))
    for (left, right), lo, hi in zip(operands, starts, cuts):
        @pl.when((tick >= lo) & (tick < hi))
        def _():
            product(left[...], right[0] if right is guc_ref else right[...])

    def when(lag, f):
        i = tick - lag

        @pl.when((i >= 0) & (i < chunks))
        def _():
            f(i)

    def core_step(i):
        even, f, s, first, second, slot = places(i)
        core_copy(i).wait()
        for a in range(2):
            for b in range(2):
                part[slot, at.core, a, b] = plus(part[slot, at.core, a, b], from_core[i, a, b])
        first_copy(i).start()

    def first_step(i):
        even, f, s, first, second, slot = places(i)
        first_copy(i).wait()
        for b in range(2):
            part[slot, at.core, f, b] = plus(part[slot, at.core, f, b], from_first[i, b])
        second_copy(i).start()

    def second_step(i):
        even, f, s, first, second, slot = places(i)
        second_copy(i).wait()
        zsum[i] = plus(part[slot, at.core, f, s], from_second[i])

        @pl.when(at.inner == 0)
        def _():
            out_copy(i).start()

    def near_step(i):
        @pl.when(at.inner == 1)
        def _():
            out_copy(i).wait_recv()
            zsum[i] = plus(zsum[i], from_near[i])
            far_copy(i).start()

    def far_step(i):
        @pl.when(at.inner == 1)
        def _():
            far_copy(i).wait()
            total = plus(zsum[i], from_far[i])
            from_far[i] = total
            back_copy(i).start()
            total_ref[i] = total

        @pl.when(at.inner == 0)
        def _():
            out_copy(i).wait_send()

    def back_step(i):
        @pl.when(at.inner == 0)
        def _():
            back_copy(i).wait_recv()
            total_ref[i] = from_near[i]

        @pl.when(at.inner == 1)
        def _():
            back_copy(i).wait_send()

    when(LAGS["core"], core_step)

    @pl.when(tick == 0)
    def _():
        gain1[...] = jnp.zeros_like(gain1)
        shift1[...] = jnp.zeros_like(shift1)
        bqkv[...] = jnp.zeros_like(bqkv)

    @pl.when((tick >= 1) & (tick <= row_ticks))
    def _():
        out_ref[...] = (base_ref[...] + nn(ctx_ref[...], wout_ref[...])).astype(BF16)
        g1 = nt(gu_ref[0], wqkv_ref[:, :width])
        g1 = g1 + nt(gu_ref[1], wqkv_ref[:, width : 2 * width])
        g1 = g1 + nt(gu_ref[2], wqkv_ref[:, 2 * width :])
        x = x_ref[...].astype(F32)
        centred = x - jnp.mean(x, axis=1, keepdims=True)
        r = lax.rsqrt(jnp.mean(centred * centred, axis=1, keepdims=True) + EPSILON)
        n = centred * r
        gain1[...] += jnp.sum(g1 * n, axis=0, keepdims=True)
        shift1[...] += jnp.sum(g1, axis=0, keepdims=True)
        for j in range(3):
            bqkv[:, j * width : (j + 1) * width] += jnp.sum(gu_ref[j].astype(F32), axis=0, keepdims=True)
        t = g1 * g1_ref[...].reshape(1, -1) + t2_ref[...]
        dx = r * (t - jnp.mean(t, axis=1, keepdims=True) - n * jnp.mean(t * n, axis=1, keepdims=True))
        ig_ref[...] = (gl_ref[...].astype(F32) + dx).astype(BF16)

    when(LAGS["first"], first_step)
    when(LAGS["second"], second_step)
    when(LAGS["z"], near_step)
    when(LAGS["mid"], far_step)
    when(LAGS["back"], back_step)

    @pl.when(tick == row_ticks + 1)
    def _():
        held_v[0] = jnp.zeros(held_v.shape[1:], F32)
        held_v[0, 0:1, :] = bup_ref[...]
        held_v[0, 1:2, : 3 * width] = bqkv[...]
        held_v[0, 1:2, 3 * width :] = bout_ref[...]
        held_v[0, 2:3, :width] = gain1[...]
        held_v[0, 2:3, width : 2 * width] = shift1[...]
        held_v[0, 2:3, 2 * width : 3 * width] = gain2_ref[...]
        held_v[0, 2:3, 3 * width :] = shift2_ref[...]
        held_v[0, 3:4, :] = jnp.full((1, held_v.shape[2]), count_ref[0].astype(F32), F32)

    begin = row_ticks + 1
    Everywhere(at, held_v, come_v, v_s, v_r).hop(tick - begin, SPACING)

    @pl.when(tick == begin + 6 * SPACING)
    def _():
        vec_ref[...] = held_v[5]


def reduce(count, n1t, n2t, glt, ctxt, gh, act, gl, gu, x, base, t2, ctx, wqkv, wout, g1, gain2, shift2, bup, bout):
    length, width = x.shape
    ff = gh.shape[1]
    block = width // 8
    counts = (ff // CHUNK, ff // CHUNK, width // CHUNK, 3 * width // CHUNK)
    cuts = tuple(int(c) for c in np.cumsum(counts))
    chunks = cuts[-1]
    per = width // CHUNK
    rows = 128
    row_ticks = length // rows
    ticks = chunks + LAGS["back"]
    assert ticks > row_ticks + 1 + 6 * SPACING
    ring = 8

    def cols(array_chunks, begin):
        return pl.BlockSpec((length, CHUNK), lambda t: (0, jnp.clip(t - begin, 0, array_chunks - 1)))

    def row(cols):
        return pl.BlockSpec((rows, cols), lambda t: (jnp.clip(t - 1, 0, row_ticks - 1), 0))

    def whole(a):
        return pl.BlockSpec(a.shape, lambda t: (0,) * a.ndim, pipeline_mode=pl.Buffered(1))

    def gu_cols(t):
        j = jnp.clip(t - cuts[2], 0, counts[3] - 1)
        return (j // per, 0, j % per)

    loaded = (n2t, wout, wqkv, glt, ctxt, n1t)
    s = jax.ShapeDtypeStruct
    dma = pltpu.SemaphoreType.DMA
    hops = Everywhere.HOPS
    return pl.pallas_call(
        functools.partial(reduce_body, cuts=cuts, row_ticks=row_ticks),
        grid=(ticks,),
        in_specs=[pl.BlockSpec(memory_space=pltpu.SMEM),
                  cols(counts[0], 0), cols(counts[1], cuts[0]), cols(counts[2], cuts[1]),
                  pl.BlockSpec((1, length, CHUNK), gu_cols),
                  row(width), row(width), row(width), row(width), row(width),
                  pl.BlockSpec((3, rows, width), lambda t: (0, jnp.clip(t - 1, 0, row_ticks - 1), 0)),
                  whole(g1), whole(gain2), whole(shift2), whole(bup), whole(bout)] + [pl.BlockSpec(memory_space=pl.ANY)] * 6,
        out_specs=[row(width), row(width),
                   pl.BlockSpec((chunks, block, CHUNK), lambda t: (0, 0, 0), pipeline_mode=pl.Buffered(1)),
                   pl.BlockSpec((8, ff), lambda t: (0, 0), pipeline_mode=pl.Buffered(1))],
        out_shape=[s((length, width), BF16), s((length, width), BF16), s((chunks, block, CHUNK), BF16), s((8, ff), F32)],
        scratch_shapes=[pltpu.VMEM(a.shape, BF16) for a in loaded] + [
            dma((len(loaded),)),
            pltpu.VMEM((ring, 2, 2, 2, block, CHUNK), BF16),
            pltpu.VMEM((chunks, 2, 2, block, CHUNK), BF16),
            pltpu.VMEM((chunks, 2, block, CHUNK), BF16),
            pltpu.VMEM((chunks, block, CHUNK), BF16),
            pltpu.VMEM((chunks, block, CHUNK), BF16),
            pltpu.VMEM((chunks, block, CHUNK), BF16),
            pltpu.VMEM((chunks, block, CHUNK), BF16),
        ] + [dma((chunks,))] * 10 + [
            pltpu.VMEM((hops, 8, ff), F32), pltpu.VMEM((hops, 8, ff), F32),
            dma((hops,)), dma((hops,)),
            pltpu.VMEM((1, width), F32), pltpu.VMEM((1, width), F32), pltpu.VMEM((1, 3 * width), F32),
        ],
        compiler_params=pltpu.CompilerParams(vmem_limit_bytes=60 * 2**20, collective_id=0, has_side_effects=True),
        name="reduce",
    )(count, gh, act, gl, gu, x, gl, base, t2, ctx, gu, g1, gain2, shift2, bup, bout, *loaded)


def finish_body(out_hbm, ig_hbm, total_ref, vec_ref, out_to, ig_to, up_ref, down_ref, low_ref, qkv_ref,
                gain1_ref, shift1_ref, bqkv_ref, bout_ref, gain2_ref, shift2_ref, bup_ref, bdown_ref, sem):
    copies = [pltpu.make_async_copy(out_hbm, out_to, sem.at[0]), pltpu.make_async_copy(ig_hbm, ig_to, sem.at[1])]
    for copy in copies:
        copy.start()
    width, ff = gain1_ref.shape[0], bup_ref.shape[0]
    factor = 1.0 / vec_ref[3:4, 0:1]
    n_up, n_low = ff // CHUNK, width // CHUNK
    for i in range(total_ref.shape[0]):
        grad = total_ref[i].astype(F32) * factor
        if i < n_up:
            up_ref[:, i * CHUNK : (i + 1) * CHUNK] = grad
        elif i < 2 * n_up:
            down_ref[:, (i - n_up) * CHUNK : (i - n_up + 1) * CHUNK] = grad
        elif i < 2 * n_up + n_low:
            j = i - 2 * n_up
            low_ref[:, j * CHUNK : (j + 1) * CHUNK] = grad
        else:
            j = i - 2 * n_up - n_low
            qkv_ref[:, j * CHUNK : (j + 1) * CHUNK] = grad
    vec = vec_ref[...] * factor
    bup_ref[...] = vec[0]
    bqkv_ref[...] = vec[1, : 3 * width]
    bout_ref[...] = vec[1, 3 * width :]
    bdown_ref[...] = vec[1, 3 * width :]
    for j, ref in enumerate((gain1_ref, shift1_ref, gain2_ref, shift2_ref)):
        ref[...] = vec[2, j * width : (j + 1) * width]
    for copy in copies:
        copy.wait()


def finish(out, ig, total, vec):
    length, width = out.shape
    block, ff = total.shape[1], vec.shape[1]
    s = jax.ShapeDtypeStruct
    hbm, vmem = pl.BlockSpec(memory_space=pltpu.HBM), pl.BlockSpec(memory_space=pltpu.VMEM)
    vectors = (width, width, 3 * width, width, width, width, ff, width)
    return pl.pallas_call(
        finish_body,
        in_specs=[hbm, hbm, vmem, vmem],
        out_specs=[hbm, hbm] + [vmem] * 12,
        out_shape=[s(out.shape, BF16), s(ig.shape, BF16), s((block, ff), F32), s((block, ff), F32), s((block, width), F32),
                   s((block, 3 * width), F32)] + [s((n,), F32) for n in vectors],
        scratch_shapes=[pltpu.SemaphoreType.DMA((2,))],
        compiler_params=pltpu.CompilerParams(vmem_limit_bytes=40 * 2**20),
        name="finish",
    )(out, ig, total, vec)


def by_collectives(count, n1t, n2t, glt, ctxt, gh, act, gl, gu, x, base, t2, ctx, wqkv, wout, g1, gain2, shift2, bup, bout):
    width = x.shape[1]
    flat = jnp.concatenate([gu[0], gu[1], gu[2]], axis=1)
    out = (base + nn(ctx, wout)).astype(BF16)
    grad_one = nt(flat, wqkv)
    x = x.astype(F32)
    centred = x - jnp.mean(x, axis=1, keepdims=True)
    r = lax.rsqrt(jnp.mean(centred * centred, axis=1, keepdims=True) + EPSILON)
    n = centred * r
    t = grad_one * g1 + t2
    dx = r * (t - jnp.mean(t, axis=1, keepdims=True) - n * jnp.mean(t * n, axis=1, keepdims=True))
    input_grad = (gl.astype(F32) + dx).astype(BF16)
    packed = jnp.concatenate([bup[0], jnp.sum(flat, axis=0, dtype=F32), bout[0], jnp.sum(grad_one * n, axis=0),
                              jnp.sum(grad_one, axis=0), gain2[0], shift2[0],
                              jnp.full(bup.shape[1], count[0].astype(F32))])
    packed = lax.psum(packed, ("dp", "rows"))
    part = jnp.concatenate([nn(n2t, gh), nn(glt, act), nn(ctxt, gl), nn(n1t, flat)], axis=1).astype(BF16)
    grads = lax.psum(lax.psum_scatter(part, "dp", scatter_dimension=0, tiled=True), "rows")
    total = jnp.swapaxes(grads.reshape(grads.shape[0], -1, CHUNK), 0, 1)
    return out, input_grad, total, packed.reshape(4, -1)


def shards(tokens, segment_ids, true_counts, regroup, cotangent, ln1_gain, ln1_bias, qkv_weight, qkv_bias, out_weight,
           out_bias, ln2_gain, ln2_bias, up_weight, up_bias, down_weight, down_bias):
    length, width = cotangent.shape
    ff = up_weight.shape[1]
    cosine, sine = (jnp.asarray(t) for t in rotary_tables(length))
    (arrived, q, k, v, gc, n1t, n2t, glt, gl, act, gh, base, t2, gain2, shift2, bias_up, bias_out) = front(
        true_counts, regroup, tokens, cotangent, cosine, sine, ln1_gain, ln1_bias, qkv_weight, qkv_bias, out_weight, out_bias,
        ln2_gain, ln2_bias, up_weight, up_bias, down_weight, down_bias)
    ctx, ctxt, gu = attention(q, k, v, gc, segment_ids, cosine, sine)
    last = reduce if (lax.axis_size("dp"), lax.axis_size("rows")) == (8, 4) else by_collectives
    out, input_grad, total, vec = last(true_counts, n1t, n2t, glt, ctxt, gh, act, gl, gu, arrived, base, t2, ctx, qkv_weight,
                                       out_weight, ln1_gain, gain2, shift2, bias_up, bias_out)
    (out, input_grad, up, down, low, qkv, gain1, shift1, bias_qkv, bias_out, gain2, shift2, bias_up, bias_down) = finish(
        out, input_grad, total, vec)
    return (out, input_grad, gain1, shift1, qkv, bias_qkv, low, bias_out, gain2, shift2, up, bias_up, down.T, bias_down)


def solution(mesh):
    both = ("dp", "rows")
    placed = (P(both, None), P(both), P(both), P(both), P(both, None)) + (P(),) * 12
    return jax.shard_map(
        shards, mesh=mesh, in_specs=placed,
        out_specs=(P(both, None), P(both, None), P(), P(), P("dp", None), P(), P("dp", None), P(), P(), P(), P("dp", None), P(),
                   P(None, "dp"), P()),
        check_vma=False)
```

```python
import functools
import numpy as np
import jax
import jax.numpy as jnp
from jax import lax
from jax.experimental import pallas as pl
from jax.experimental.pallas import tpu as pltpu
from jax.sharding import PartitionSpec as P

HEAD_DIM = 64
ROT = 16
PAIR = 128
EPSILON = 1e-05
EXCLUDED = -1e30
F32 = jnp.float32
BF16 = jnp.bfloat16
MESH = pl.DeviceIdType.MESH


def remote(src, dst, send, recv, to):
    return pltpu.make_async_remote_copy(src_ref=src, dst_ref=dst, send_sem=send, recv_sem=recv, device_id=to, device_id_type=MESH)


def nn(a, b):
    return lax.dot_general(a, b, (((1,), (0,)), ((), ())), preferred_element_type=F32)


def nt(a, b):
    return lax.dot_general(a, b, (((1,), (1,)), ((), ())), preferred_element_type=F32)


def tn(a, b):
    return lax.dot_general(a, b, (((0,), (0,)), ((), ())), preferred_element_type=F32)


def rotary_tables(length):
    half = ROT // 2
    placed = np.arange(length, dtype=np.float32)
    rates = np.exp(np.arange(half, dtype=np.float32) * np.float32(-2.0 / ROT) * np.log(np.float32(10000.0)))
    phases = placed[:, None] * rates[None, :].astype(np.float32)
    cosine = np.ones((length, HEAD_DIM), np.float32)
    sine = np.zeros((length, HEAD_DIM), np.float32)
    cosine[:, :half] = np.cos(phases)
    cosine[:, half:ROT] = np.cos(phases)
    sine[:, :half] = -np.sin(phases)
    sine[:, half:ROT] = np.sin(phases)
    return np.tile(cosine, (1, PAIR // HEAD_DIM)), np.tile(sine, (1, PAIR // HEAD_DIM))


def turned(u):
    lane = lax.broadcasted_iota(jnp.int32, u.shape, 1) % HEAD_DIM
    half = ROT // 2
    return jnp.where(lane < half, pltpu.roll(u, PAIR - half, 1), pltpu.roll(u, half, 1))


def gelu_parts(h):
    e = jnp.exp(h * h * -0.5)
    t = 1.0 / (1.0 + 0.2316418882 * jnp.abs(h))
    poly = t * (0.127414796 + t * (-0.142248368 + t * (0.7107068705 + t * (-0.7265760135 + t * 0.5307027145))))
    tail = poly * e
    phi = jnp.where(h >= 0, 1.0 - tail, tail)
    return h * phi, phi + h * (e * 0.3989422804014327)


def front_body(count_ref, want_ref, own_ref, cot_ref, cos_ref, sin_ref, g1_vec, b1_vec, bqkv_vec, bout_vec, g2_vec, b2_vec,
               bup_vec, bdown_vec, wqkv_hbm, wout_hbm, wup_hbm, wdown_hbm,
               x_ref, q_ref, k_ref, v_ref, gc_ref, n1t_ref, n2t_ref, glt_ref, gl_ref, mlp_ref, base_ref, t2_ref,
               gain2_ref, shift2_ref, bup_out, bout_out,
               wqkv_ref, wout_ref, wup_ref, wdown_ref, wants, from_near, from_half, to_inner, to_end,
               g1_ref, b1_ref, bqkv_ref, bout_ref, g2_ref, b2_ref, bup_ref, bdown_ref, w_sem, want_send, want_recv, near_send, near_recv, inner_send, end_send, half_recv, *, tile):
    step = pl.program_id(0)
    steps = pl.num_programs(0)
    rows, width = cot_ref.shape
    pairs = width // PAIR
    ff = wup_ref.shape[1]
    chunks = own_ref.shape[0] // rows
    d, z = lax.axis_index("dp"), lax.axis_index("rows")
    inner = (z + 1) // 2 % 2
    near = z + 1 - 2 * (z % 2)
    other_inner, other_end = 3 - z, 6 - 3 * z
    loads = [pltpu.make_async_copy(src, dst, w_sem.at[j]) for j, (src, dst) in enumerate(
        ((wqkv_hbm, wqkv_ref), (wout_hbm, wout_ref), (wup_hbm, wup_ref), (wdown_hbm, wdown_ref)))]

    def span(i):
        return pl.ds(pl.multiple_of(i * rows, rows), rows)

    def want_copy(j):
        to = lax.rem(z + j, 4)
        return remote(wants.at[0], wants.at[j], want_send.at[j], want_recv.at[j], (d, to))

    def near_copy(i):
        return remote(own_ref.at[span(i)], from_near.at[span(i)], near_send.at[i], near_recv.at[i], (d, near))

    def inner_copy(i):
        return remote(to_inner.at[span(i)], from_half.at[span(i)], inner_send.at[i], half_recv.at[i], (d, other_inner))

    def end_copy(i):
        return remote(to_end.at[span(i)], from_half.at[span(i)], end_send.at[i], half_recv.at[i], (d, other_end))

    def wanted(by):
        return wants[lax.rem(z - by + 4, 4), 0:1, 0:1]

    def relay(i):
        @pl.when(inner == 1)
        def _():
            near_copy(i).wait_recv()
            mine = own_ref[span(i), :].astype(F32)
            theirs = from_near[span(i), :].astype(F32)
            to_end[span(i), :] = jnp.where(wanted(other_end) == near, theirs, mine).astype(BF16)
            end_copy(i).start()
            to_inner[span(i), :] = jnp.where(wanted(other_inner) == near, theirs, mine).astype(BF16)
            inner_copy(i).start()

    @pl.when(step == 0)
    def _():
        barrier = pltpu.get_barrier_semaphore()
        for j in (1, 2, 3):
            pl.semaphore_signal(barrier, inc=1, device_id=(d, lax.rem(z + j, 4)), device_id_type=MESH)
        wants[0] = jnp.full(wants.shape[1:], want_ref[0] % 4, jnp.int32)
        pl.semaphore_wait(barrier, 3)
        for j in (1, 2, 3):
            want_copy(j).start()

        def hand(i, carry):
            near_copy(i).start()
            return carry

        lax.fori_loop(0, chunks, hand, 0)
        for load in loads:
            load.start()
        for j in (1, 2, 3):
            want_copy(j).wait()
        relay(0)
        for vec, ref in ((g1_vec, g1_ref), (b1_vec, b1_ref), (bqkv_vec, bqkv_ref), (bout_vec, bout_ref), (g2_vec, g2_ref),
                         (b2_vec, b2_ref), (bup_vec, bup_ref), (bdown_vec, bdown_ref)):
            ref[...] = vec[...].reshape(1, -1)
        gain2_ref[...] = jnp.zeros_like(gain2_ref)
        shift2_ref[...] = jnp.zeros_like(shift2_ref)
        bup_out[...] = jnp.zeros_like(bup_out)
        bout_out[...] = jnp.zeros_like(bout_out)

    @pl.when(step + 1 < chunks)
    def _():
        relay(step + 1)

    @pl.when(step == 0)
    def _():
        for load in loads:
            load.wait()

    place = step * rows + lax.broadcasted_iota(jnp.int32, (rows, 1), 0)
    gl = jnp.where(place < count_ref[0], cot_ref[...].astype(F32), 0.0)
    gl16 = gl.astype(BF16)
    for j in range(gl_ref.shape[0]):
        gl_ref[j] = gl16[:, j * PIECE : (j + 1) * PIECE]
    glt_ref[...] = gl16.T
    bout_out[...] += jnp.sum(gl, axis=0, keepdims=True)
    for p in range(pairs):
        gc_ref[p] = nt(gl16, wout_ref[p * PAIR : (p + 1) * PAIR, :]).astype(BF16)

    @pl.when(inner == 0)
    def _():
        near_copy(step).wait_recv()

    inner_copy(step).wait_recv()
    source = wanted(z)
    x = jnp.where(source == near, from_near[span(step), :].astype(F32), from_half[span(step), :].astype(F32))
    x = jnp.where(source == z, own_ref[span(step), :].astype(F32), x)
    x_ref[...] = x.astype(BF16)
    centred = x - jnp.mean(x, axis=1, keepdims=True)
    r = lax.rsqrt(jnp.mean(centred * centred, axis=1, keepdims=True) + EPSILON)
    n = centred * r
    n1 = (n * g1_ref[...] + b1_ref[...]).astype(BF16)
    n2 = (n * g2_ref[...] + b2_ref[...]).astype(BF16)
    n1t_ref[...] = n1.T
    n2t_ref[...] = n2.T
    cosine, sine = cos_ref[...], sin_ref[...]
    for p in range(pairs):
        for which, ref in enumerate((q_ref, k_ref, v_ref)):
            wide = slice(which * width + p * PAIR, which * width + (p + 1) * PAIR)
            u = nn(n1, wqkv_ref[:, wide]) + bqkv_ref[:, wide]
            if which < 2:
                u = u * cosine + turned(u) * sine
            if which == 0:
                u = u * (HEAD_DIM ** -0.5)
            ref[p] = u.astype(BF16)
    mlp = x + (bdown_ref[...] + bout_ref[...])
    grad_two = jnp.zeros((rows, width), F32)
    for f in range(0, ff, tile):
        cols = slice(f, f + tile)
        h = nn(n2, wup_ref[:, cols]) + bup_ref[:, cols]
        ga = nt(gl16, wdown_ref[cols, :])
        a, slope = gelu_parts(h)
        a16 = a.astype(BF16)
        gh = ga * slope
        gh16 = gh.astype(BF16)
        mlp_ref[:, cols] = gh16
        mlp_ref[:, ff + f : ff + f + tile] = a16
        bup_out[:, cols] += jnp.sum(gh16.astype(F32), axis=0, keepdims=True)
        mlp = mlp + nn(a16, wdown_ref[cols, :])
        grad_two = grad_two + nt(gh16, wup_ref[:, cols])
    base_ref[...] = mlp
    t2_ref[...] = grad_two * g2_ref[...]
    gain2_ref[...] += jnp.sum(grad_two * n, axis=0, keepdims=True)
    shift2_ref[...] += jnp.sum(grad_two, axis=0, keepdims=True)

    @pl.when(step == steps - 1)
    def _():
        def done(i, carry):
            near_copy(i).wait_send()

            @pl.when(inner == 1)
            def _():
                inner_copy(i).wait_send()
                end_copy(i).wait_send()
            return carry

        lax.fori_loop(0, chunks, done, 0)


def front(count, want, own, cot, cosine, sine, g1, b1, wqkv, bqkv, wout, bout, g2, b2, wup, bup, wdown, bdown, rows=128, tile=512):
    length, width = own.shape
    ff = wup.shape[1]
    pairs = width // PAIR
    chunks = length // rows

    def row(cols):
        return pl.BlockSpec((rows, cols), lambda i: (i, 0))

    def whole(a):
        return pl.BlockSpec(a.shape, lambda i: (0,) * a.ndim, pipeline_mode=pl.Buffered(1))

    heads = pl.BlockSpec((pairs, rows, PAIR), lambda i: (0, i, 0))
    down = pl.BlockSpec((width, rows), lambda i: (0, i))

    def vec(cols):
        return pl.BlockSpec((1, cols), lambda i: (0, 0))

    vectors = (g1, b1, bqkv, bout, g2, b2, bup, bdown)
    weights = (wqkv, wout, wup, wdown)
    s = jax.ShapeDtypeStruct
    dma = pltpu.SemaphoreType.DMA
    return pl.pallas_call(
        functools.partial(front_body, tile=tile),
        grid=(chunks,),
        in_specs=[pl.BlockSpec(memory_space=pltpu.SMEM), pl.BlockSpec(memory_space=pltpu.SMEM), whole(own), row(width), row(PAIR), row(PAIR)]
        + [whole(a) for a in vectors] + [pl.BlockSpec(memory_space=pl.ANY)] * 4,
        out_specs=[row(width)] + [heads] * 4 + [down] * 3
        + [pl.BlockSpec((width // PIECE, rows, PIECE), lambda i: (0, i, 0)), row(2 * ff)] + [row(width)] * 2
        + [vec(width), vec(width), vec(ff), vec(width)],
        out_shape=[s((length, width), BF16)] + [s((pairs, length, PAIR), BF16)] * 4 + [s((width, length), BF16)] * 3
        + [s((width // PIECE, length, PIECE), BF16), s((length, 2 * ff), BF16)]
        + [s((length, width), F32)] * 2 + [s((1, width), F32), s((1, width), F32), s((1, ff), F32), s((1, width), F32)],
        scratch_shapes=[pltpu.VMEM(w.shape, BF16) for w in weights]
        + [pltpu.VMEM((4, 8, 128), jnp.int32)] + [pltpu.VMEM((length, width), BF16)] * 4
        + [pltpu.VMEM((1, v.shape[0]), F32) for v in vectors] + [dma((4,)), dma((4,)), dma((4,))] + [dma((chunks,))] * 5,
        compiler_params=pltpu.CompilerParams(vmem_limit_bytes=60 * 2**20, collective_id=1, has_side_effects=True),
        name="front",
    )(count, want, own, cot, cosine, sine, *vectors, *weights)


def attention_body(q_ref, k_ref, v_ref, gc_ref, seg_ref, cos_ref, sin_ref,
                   ctx_ref, ctxt_ref, gu_ref, dk_acc, dv_acc, segc_ref, segr_ref, first_ref, *, rows):
    group, length, _ = q_ref.shape
    total = length // rows
    each = range(group)

    @pl.when(pl.program_id(0) == 0)
    def _():
        seg = seg_ref[...].reshape(1, -1)
        segr_ref[...] = seg
        segc_ref[...] = jnp.broadcast_to(seg, (8, length)).T[:, :1]
        wide = seg.astype(F32)
        for b in range(total):
            before = jnp.sum(jnp.where(wide < wide[:, b * rows : b * rows + 1], 1.0, 0.0))
            first_ref[b] = before.astype(jnp.int32) // rows

    lane = lax.broadcasted_iota(jnp.int32, (rows, PAIR), 1)
    low = lane < HEAD_DIM
    dk_acc[...] = jnp.zeros_like(dk_acc)
    dv_acc[...] = jnp.zeros_like(dv_acc)

    def both(ref, h, begin):
        t = ref[h, pl.ds(begin, rows), :]
        zero = jnp.zeros_like(t)
        return jnp.concatenate([jnp.where(low, t, zero), jnp.where(low, zero, t)], axis=0)

    def block(b, blocks):
        begin = pl.multiple_of(b * rows, rows)
        start = pl.multiple_of((b + 1 - blocks) * rows, rows)
        span = blocks * rows
        q2 = [both(q_ref, h, begin) for h in each]
        g2 = [both(gc_ref, h, begin) for h in each]
        k = [k_ref[h, pl.ds(start, span), :] for h in each]
        v = [v_ref[h, pl.ds(start, span), :] for h in each]
        segt = segc_ref[pl.ds(begin, rows), :]
        segs = segr_ref[:, pl.ds(start, span)]
        t_at = begin + lax.broadcasted_iota(jnp.int32, (rows, span), 0)
        s_at = start + lax.broadcasted_iota(jnp.int32, (rows, span), 1)
        allowed = (segt == segs) & (s_at <= t_at)
        allowed = jnp.concatenate([allowed, allowed], axis=0)
        scores = [jnp.where(allowed, nt(q2[h], k[h]), EXCLUDED) for h in each]
        dp = [nt(g2[h], v[h]) for h in each]
        e = [jnp.exp(scores[h] - jnp.max(scores[h], axis=1, keepdims=True)) for h in each]
        p = [e[h] * (1.0 / jnp.sum(e[h], axis=1, keepdims=True)) for h in each]
        p16 = [p[h].astype(BF16) for h in each]
        c2 = [nn(p16[h], v[h]) for h in each]
        for h in each:
            dv_acc[h, pl.ds(start, span), :] += tn(p16[h], g2[h])
        w = [p[h] * dp[h] for h in each]
        ds16 = [(w[h] - p[h] * jnp.sum(w[h], axis=1, keepdims=True)).astype(BF16) for h in each]
        d2 = [nn(ds16[h], k[h]) for h in each]
        for h in each:
            dk_acc[h, pl.ds(start, span), :] += tn(ds16[h], q2[h])
        cosine = cos_ref[pl.ds(begin, rows), :]
        sine = sin_ref[pl.ds(begin, rows), :]
        for h in each:
            cols = slice(h * PAIR, (h + 1) * PAIR)
            context = jnp.where(low, c2[h][:rows], c2[h][rows:]).astype(BF16)
            ctx_ref[pl.ds(begin, rows), cols] = context
            ctxt_ref[cols, pl.ds(begin, rows)] = context.T
            dq = jnp.where(low, d2[h][:rows], d2[h][rows:]) * (HEAD_DIM ** -0.5)
            gu_ref[0, pl.ds(begin, rows), cols] = (dq * cosine - turned(dq) * sine).astype(BF16)

    def loop(b, carry):
        count = b + 1 - first_ref[b]
        for blocks in range(1, total + 1):
            @pl.when(count == blocks)
            def _():
                block(b, blocks)
        return carry

    lax.fori_loop(0, total, loop, 0)
    for h in each:
        cols = slice(h * PAIR, (h + 1) * PAIR)
        dk = dk_acc[h]
        gu_ref[1, :, cols] = (dk * cos_ref[...] - turned(dk) * sin_ref[...]).astype(BF16)
        gu_ref[2, :, cols] = dv_acc[h].astype(BF16)


def attention(q, k, v, gc, segment, cosine, sine, rows=256, group=2):
    pairs, length, _ = q.shape
    head = pl.BlockSpec((group, length, PAIR), lambda h: (h, 0, 0))
    cols = pl.BlockSpec((length, group * PAIR), lambda h: (0, h))
    s = jax.ShapeDtypeStruct
    width = pairs * PAIR

    def whole(a):
        return pl.BlockSpec(a.shape, lambda h: (0,) * a.ndim, pipeline_mode=pl.Buffered(1))

    return pl.pallas_call(
        functools.partial(attention_body, rows=rows),
        grid=(pairs // group,),
        in_specs=[head] * 4 + [whole(segment), whole(cosine), whole(sine)],
        out_specs=[cols, pl.BlockSpec((group * PAIR, length), lambda h: (h, 0)),
                   pl.BlockSpec((3, length, group * PAIR), lambda h: (0, 0, h))],
        scratch_shapes=[pltpu.VMEM((group, length, PAIR), F32)] * 2
        + [pltpu.VMEM((length, 1), jnp.int32), pltpu.VMEM((1, length), jnp.int32), pltpu.SMEM((length // rows,), jnp.int32)],
        out_shape=[s((length, width), BF16), s((width, length), BF16), s((3, length, width), BF16)],
        compiler_params=pltpu.CompilerParams(vmem_limit_bytes=56 * 2**20),
        name="attention",
    )(q, k, v, gc, segment, cosine, sine)


CHUNK = 512
PIECE = 256
GROUP = 2


class Line:
    def __init__(self):
        self.d = lax.axis_index("dp")
        self.z = lax.axis_index("rows")
        self.core = self.d % 2
        self.x = (self.d // 2) % 2
        self.y = self.d // 4
        self.over_core = (self.d + 1 - 2 * self.core, self.z)
        self.over_x = (self.d + 2 - 4 * self.x, self.z)
        self.over_y = (self.d + 4 - 8 * self.y, self.z)
        self.inner = (self.z + 1) // 2 % 2
        self.near = (self.d, self.z + 1 - 2 * (self.z % 2))
        self.far = (self.d, 3 - self.z)


class Everywhere:
    HOPS = 7

    def __init__(self, at, held, come, send, recv):
        self.at, self.held, self.come, self.send, self.recv = at, held, come, send, recv

    def copy(self, hop, to):
        return remote(self.held.at[hop], self.come.at[hop], self.send.at[hop], self.recv.at[hop], to)

    def take(self, hop, to):
        self.copy(hop, to).wait()
        self.held[hop + 1] = self.held[hop] + self.come[hop]

    def hop(self, tick, spacing):
        at = self.at
        over = (at.over_core, at.over_x, at.over_y)

        @pl.when(tick == 0)
        def _():
            self.copy(0, over[0]).start()

        for j in (1, 2):
            @pl.when(tick == j * spacing)
            def _():
                self.take(j - 1, over[j - 1])
                self.copy(j, over[j]).start()

        @pl.when(tick == 3 * spacing)
        def _():
            self.take(2, over[2])

            @pl.when(at.inner == 0)
            def _():
                self.copy(3, at.near).start()

        @pl.when((tick == 4 * spacing) & (at.inner == 1))
        def _():
            self.copy(3, at.near).wait_recv()
            self.held[4] = self.held[3] + self.come[3]
            self.copy(4, at.far).start()

        @pl.when((tick == 4 * spacing) & (at.inner == 0))
        def _():
            self.copy(3, at.near).wait_send()

        @pl.when((tick == 5 * spacing) & (at.inner == 1))
        def _():
            self.take(4, at.far)
            self.copy(5, at.near).start()

        @pl.when(tick == 6 * spacing)
        def _():
            @pl.when(at.inner == 1)
            def _():
                self.copy(5, at.near).wait_send()

            @pl.when(at.inner == 0)
            def _():
                self.copy(5, at.near).wait_recv()
                self.held[5] = self.come[5]

LAGS = dict(core=1, first=3, second=5, z=7, mid=9, back=10)
RING, CORE_RING, LINK_RING = 7, 6, 8


def chunk_columns(i, groups, per_group):
    period = per_group + 1
    if i < groups * period and i % period < per_group:
        return "mlp", per_group * (i // period) + i % period
    j = i // period if i < groups * period else i - groups * per_group
    return "rest", 2 * j, 2 * j + 1


def back_body(count_ref, seg_ref, mlp_ref, q_ref, k_ref, v_ref, gc_ref, x_ref, base_ref, t2_ref, cos_ref, sin_ref, g1_ref,
              gain2_ref, shift2_ref, bup_ref, bout_ref, n2t_hbm, glt_hbm, n1t_hbm, gl_hbm, wout_hbm, wqkv_hbm,
              out_ref, ig_ref, total_ref, vec_ref,
              left_mlp, left_rest, rhs, wout_ref, wqkv_ref, load_sem, ctx, dk_acc, dv_acc, begin_ref,
              part, from_core, from_first, from_second, from_near, from_far,
              c_send, c_recv, f_send, f_recv, s_send, s_recv, n_send, n_recv, m_send, m_recv,
              held_v, come_v, v_s, v_r, gain1, shift1, bqkv, *, rows, row_ticks):
    tick = pl.program_id(0)
    at = Line()
    chunks, block = total_ref.shape[0], total_ref.shape[1]
    length, width = seg_ref.shape[0], wout_ref.shape[0]
    groups = width // PIECE
    per_group = length // rows
    period = per_group + 1
    busy = groups * period
    g = jnp.minimum(tick // period, groups - 1)
    spot = tick % period
    first_need = (pltpu.make_async_copy(n2t_hbm, left_mlp.at[0], load_sem.at[0]),)
    later_need = [pltpu.make_async_copy(src, dst, load_sem.at[1 + j]) for j, (src, dst) in enumerate(
        ((glt_hbm, left_mlp.at[1]), (n1t_hbm, left_rest.at[0]), (gl_hbm, rhs.at[pl.ds(3 * groups, groups)]),
         (wout_hbm, wout_ref), (wqkv_hbm, wqkv_ref)))]

    @pl.when(tick == 0)
    def _():
        first_need[0].start()
        barrier = pltpu.get_barrier_semaphore()
        for to in (at.over_core, at.over_x, at.over_y, at.near):
            pl.semaphore_signal(barrier, inc=1, device_id=to, device_id_type=MESH)

        @pl.when(at.inner == 1)
        def _():
            pl.semaphore_signal(barrier, inc=1, device_id=at.far, device_id_type=MESH)
            pl.semaphore_wait(barrier, 5)

        @pl.when(at.inner == 0)
        def _():
            pl.semaphore_wait(barrier, 4)

        for load in later_need:
            load.start()
        wide = jnp.broadcast_to(seg_ref[...].reshape(1, -1), (8, length)).astype(F32)
        tall = wide.T[:, :1]
        for b in range(0, length, PAIR):
            earlier = jnp.where(wide[:1] < tall[b : b + PAIR], 1.0, 0.0)
            begin_ref[b : b + PAIR, :] = jnp.sum(earlier, axis=1, keepdims=True).astype(jnp.int32)
        gain1[...] = jnp.zeros_like(gain1)
        shift1[...] = jnp.zeros_like(shift1)
        bqkv[...] = jnp.zeros_like(bqkv)
        first_need[0].wait()

    @pl.when(tick == 1)
    def _():
        for load in later_need:
            load.wait()

    def places(i):
        even = 1 - i % 2
        f = at.x * even + at.y * (1 - even)
        s = at.y * even + at.x * (1 - even)
        first = (at.d + even * (2 - 4 * at.x) + (1 - even) * (4 - 8 * at.y), at.z)
        second = (at.d + even * (4 - 8 * at.y) + (1 - even) * (2 - 4 * at.x), at.z)
        return f, s, first, second, i % RING

    def core_copy(i):
        return remote(part.at[i % RING, 1 - at.core], from_core.at[i % CORE_RING], c_send.at[i], c_recv.at[i], at.over_core)

    def first_copy(i):
        f, s, first, second, slot = places(i)
        return remote(part.at[slot, at.core, 1 - f], from_first.at[i % LINK_RING], f_send.at[i], f_recv.at[i], first)

    def second_copy(i):
        f, s, first, second, slot = places(i)
        return remote(part.at[slot, at.core, f, 1 - s], from_second.at[i % LINK_RING], s_send.at[i], s_recv.at[i], second)

    def out_copy(i):
        return remote(total_ref.at[i], from_near.at[i % LINK_RING], n_send.at[i], n_recv.at[i], at.near)

    def far_copy(i):
        return remote(total_ref.at[i], from_far.at[i % LINK_RING], m_send.at[i], m_recv.at[i], at.far)

    def plus(a, b):
        return (a.astype(F32) + b.astype(F32)).astype(BF16)

    def put(h, half, cols, rows_of):
        even = 1 - tick % 2
        for j in range(4):
            d = h * 4 + j
            c, x, y = d % 2, (d // 2) % 2, d // 4
            a = x * even + y * (1 - even)
            b = y * even + x * (1 - even)
            part[tick % RING, c, a, b, :, cols] = rows_of[j * block : (j + 1) * block].astype(BF16)

    half = width // 2
    is_mlp = (tick < busy) & (spot < per_group)

    @pl.when(is_mlp)
    def _():
        left = (per_group * g + spot) // (groups * per_group // 2)
        for h in range(2):
            put(h, half, slice(0, CHUNK), nn(left_mlp[left, h * half : (h + 1) * half, :], mlp_ref[...]))
        core_copy(tick).start()

    @pl.when((tick < chunks) & jnp.logical_not(is_mlp))
    def _():
        j = (tick // period) * (1 - tick // busy) + (tick - groups * per_group) * (tick // busy)
        for e in range(2):
            s = 2 * j + e
            for h in range(2):
                put(h, half, slice(e * PIECE, (e + 1) * PIECE),
                    nn(left_rest[s // (3 * groups), h * half : (h + 1) * half, :], rhs[s]))
        core_copy(tick).start()

    def when(lag, f):
        i = tick - lag

        @pl.when((i >= 0) & (i < chunks))
        def _():
            f(i)

    def core_step(i):
        f, s, first, second, slot = places(i)
        core_copy(i).wait()
        for a in range(2):
            for b in range(2):
                part[slot, at.core, a, b] = plus(part[slot, at.core, a, b], from_core[i % CORE_RING, a, b])
        first_copy(i).start()

    def first_step(i):
        f, s, first, second, slot = places(i)
        first_copy(i).wait()
        for b in range(2):
            part[slot, at.core, f, b] = plus(part[slot, at.core, f, b], from_first[i % LINK_RING, b])
        second_copy(i).start()

    def second_step(i):
        f, s, first, second, slot = places(i)
        second_copy(i).wait()
        total_ref[i] = plus(part[slot, at.core, f, s], from_second[i % LINK_RING])

        @pl.when(at.inner == 0)
        def _():
            out_copy(i).start()

    def near_step(i):
        @pl.when(at.inner == 1)
        def _():
            out_copy(i).wait_recv()
            total_ref[i] = plus(total_ref[i], from_near[i % LINK_RING])
            far_copy(i).start()

    def far_step(i):
        @pl.when(at.inner == 1)
        def _():
            far_copy(i).wait()
            total_ref[i] = plus(total_ref[i], from_far[i % LINK_RING])
            out_copy(i).start()

        @pl.when(at.inner == 0)
        def _():
            out_copy(i).wait_send()

    def back_step(i):
        @pl.when(at.inner == 0)
        def _():
            out_copy(i).wait_recv()
            total_ref[i] = from_near[i % LINK_RING]

        @pl.when(at.inner == 1)
        def _():
            out_copy(i).wait_send()

    when(LAGS["core"], core_step)
    when(LAGS["first"], first_step)
    when(LAGS["second"], second_step)
    when(LAGS["z"], near_step)
    when(LAGS["mid"], far_step)
    when(LAGS["back"], back_step)

    each = range(GROUP)
    low = lax.broadcasted_iota(jnp.int32, (rows, PAIR), 1) < HEAD_DIM

    def unit(b):
        span = (b + 1) * rows
        mine = slice(b * rows, span)

        def both(ref, h):
            t = ref[h, mine, :]
            zero = jnp.zeros_like(t)
            return jnp.concatenate([jnp.where(low, t, zero), jnp.where(low, zero, t)], axis=0)

        q2 = [both(q_ref, h) for h in each]
        g2 = [both(gc_ref, h) for h in each]
        k = [k_ref[h, :span, :] for h in each]
        v = [v_ref[h, :span, :] for h in each]
        s_at = lax.broadcasted_iota(jnp.int32, (rows, span), 1)
        t_at = b * rows + lax.broadcasted_iota(jnp.int32, (rows, span), 0)
        allowed = (s_at >= begin_ref[mine, :]) & (s_at <= t_at)
        allowed = jnp.concatenate([allowed, allowed], axis=0)
        scores = [jnp.where(allowed, nt(q2[h], k[h]), EXCLUDED) for h in each]
        dp = [nt(g2[h], v[h]) for h in each]
        e = [jnp.exp(scores[h] - jnp.max(scores[h], axis=1, keepdims=True)) for h in each]
        p = [e[h] * (1.0 / jnp.sum(e[h], axis=1, keepdims=True)) for h in each]
        p16 = [p[h].astype(BF16) for h in each]
        c2 = [nn(p16[h], v[h]) for h in each]
        for h in each:
            dv_acc[h, :span, :] += tn(p16[h], g2[h])
        w = [p[h] * dp[h] for h in each]
        ds16 = [(w[h] - p[h] * jnp.sum(w[h], axis=1, keepdims=True)).astype(BF16) for h in each]
        d2 = [nn(ds16[h], k[h]) for h in each]
        for h in each:
            dk_acc[h, :span, :] += tn(ds16[h], q2[h])
        for h in each:
            cols = slice(h * PAIR, (h + 1) * PAIR)
            context = jnp.where(low, c2[h][:rows], c2[h][rows:]).astype(BF16)
            ctx[g, mine, cols] = context
            left_rest[1, pl.ds(pl.multiple_of(g * PIECE + h * PAIR, PAIR), PAIR), mine] = context.T
            dq = jnp.where(low, d2[h][:rows], d2[h][rows:]) * (HEAD_DIM ** -0.5)
            rhs[3 * g, mine, cols] = (dq * cos_ref[mine, :] - turned(dq) * sin_ref[mine, :]).astype(BF16)

    @pl.when((tick < busy) & (spot == 0))
    def _():
        dk_acc[...] = jnp.zeros_like(dk_acc)
        dv_acc[...] = jnp.zeros_like(dv_acc)

    for b in range(per_group):
        @pl.when((tick < busy) & (spot == b))
        def _():
            unit(b)

    @pl.when((tick < busy) & (spot == per_group - 1))
    def _():
        for h in each:
            cols = slice(h * PAIR, (h + 1) * PAIR)
            dk = dk_acc[h]
            rhs[3 * g + 1, :, cols] = (dk * cos_ref[...] - turned(dk) * sin_ref[...]).astype(BF16)
            rhs[3 * g + 2, :, cols] = dv_acc[h].astype(BF16)

    @pl.when((tick >= busy) & (tick < busy + row_ticks))
    def _():
        n_rows = x_ref.shape[0]
        here = pl.ds(pl.multiple_of((tick - busy) * n_rows, n_rows), n_rows)
        attn = base_ref[...]
        for j in range(groups):
            attn = attn + nn(ctx[j, here, :], wout_ref[j * PIECE : (j + 1) * PIECE, :])
        out_ref[...] = attn.astype(BF16)
        g1 = jnp.zeros(attn.shape, F32)
        for s in range(3 * groups):
            cols = slice((s % 3) * width + (s // 3) * PIECE, (s % 3) * width + (s // 3 + 1) * PIECE)
            grads = rhs[s, here, :]
            g1 = g1 + nt(grads, wqkv_ref[:, cols])
            bqkv[:, cols] += jnp.sum(grads.astype(F32), axis=0, keepdims=True)
        x = x_ref[...].astype(F32)
        centred = x - jnp.mean(x, axis=1, keepdims=True)
        r = lax.rsqrt(jnp.mean(centred * centred, axis=1, keepdims=True) + EPSILON)
        n = centred * r
        gain1[...] += jnp.sum(g1 * n, axis=0, keepdims=True)
        shift1[...] += jnp.sum(g1, axis=0, keepdims=True)
        t = g1 * g1_ref[...].reshape(1, -1) + t2_ref[...]
        dx = r * (t - jnp.mean(t, axis=1, keepdims=True) - n * jnp.mean(t * n, axis=1, keepdims=True))
        gl = jnp.concatenate([rhs[3 * groups + j, here, :] for j in range(groups)], axis=1)
        ig_ref[...] = (gl.astype(F32) + dx).astype(BF16)

    begin = busy + row_ticks

    @pl.when(tick == begin)
    def _():
        held_v[0] = jnp.zeros(held_v.shape[1:], F32)
        held_v[0, 0:1, :] = bup_ref[...]
        held_v[0, 1:2, : 3 * width] = bqkv[...]
        held_v[0, 1:2, 3 * width :] = bout_ref[...]
        held_v[0, 2:3, :width] = gain1[...]
        held_v[0, 2:3, width : 2 * width] = shift1[...]
        held_v[0, 2:3, 2 * width : 3 * width] = gain2_ref[...]
        held_v[0, 2:3, 3 * width :] = shift2_ref[...]
        held_v[0, 3:4, :] = jnp.full((1, held_v.shape[2]), count_ref[0].astype(F32), F32)

    Everywhere(at, held_v, come_v, v_s, v_r).hop(tick - begin, 1)

    @pl.when(tick == begin + 6)
    def _():
        vec_ref[...] = held_v[5]


def back(count, segment, mlp, q, k, v, gc, x, base, t2, cosine, sine, g1, gain2, shift2, bup, bout, n2t, glt, n1t, gl, wout, wqkv,
         rows=256):
    length, width = x.shape
    ff = bup.shape[1]
    block = width // 8
    groups = width // PIECE
    chunks = (2 * ff + 4 * width) // CHUNK
    period = length // rows + 1
    busy = groups * period
    row_ticks = length // rows
    ticks = max(chunks + LAGS["back"], busy + row_ticks + 7)
    n_mlp = 2 * ff // CHUNK

    def row(cols):
        return pl.BlockSpec((rows, cols), lambda t: (jnp.clip(t - busy, 0, row_ticks - 1), 0))

    def whole(a):
        return pl.BlockSpec(a.shape, lambda t: (0,) * a.ndim, pipeline_mode=pl.Buffered(1))

    def mlp_cols(t):
        return (0, jnp.minimum((period - 1) * (t // period) + jnp.minimum(t % period, period - 2), n_mlp - 1))

    heads = pl.BlockSpec((GROUP, length, PAIR), lambda t: (jnp.minimum(t // period, groups - 1), 0, 0))
    s = jax.ShapeDtypeStruct
    dma = pltpu.SemaphoreType.DMA
    hops = Everywhere.HOPS
    loaded = (n2t, glt, n1t, gl, wout, wqkv)
    return pl.pallas_call(
        functools.partial(back_body, rows=rows, row_ticks=row_ticks),
        grid=(ticks,),
        in_specs=[pl.BlockSpec(memory_space=pltpu.SMEM), whole(segment), pl.BlockSpec((length, CHUNK), mlp_cols)]
        + [heads] * 4 + [row(width)] * 3
        + [whole(a) for a in (cosine, sine, g1, gain2, shift2, bup, bout)] + [pl.BlockSpec(memory_space=pl.ANY)] * 6,
        out_specs=[row(width), row(width),
                   pl.BlockSpec((chunks, block, CHUNK), lambda t: (0, 0, 0), pipeline_mode=pl.Buffered(1)),
                   pl.BlockSpec((8, ff), lambda t: (0, 0), pipeline_mode=pl.Buffered(1))],
        out_shape=[s((length, width), BF16), s((length, width), BF16), s((chunks, block, CHUNK), BF16), s((8, ff), F32)],
        scratch_shapes=[
            pltpu.VMEM((2, width, length), BF16),
            pltpu.VMEM((2, width, length), BF16),
            pltpu.VMEM((4 * groups, length, PIECE), BF16),
            pltpu.VMEM(wout.shape, BF16),
            pltpu.VMEM(wqkv.shape, BF16),
            dma((6,)),
            pltpu.VMEM((groups, length, PIECE), BF16),
            pltpu.VMEM((GROUP, length, PAIR), F32),
            pltpu.VMEM((GROUP, length, PAIR), F32),
            pltpu.VMEM((length, 1), jnp.int32),
            pltpu.VMEM((RING, 2, 2, 2, block, CHUNK), BF16),
            pltpu.VMEM((CORE_RING, 2, 2, block, CHUNK), BF16),
            pltpu.VMEM((LINK_RING, 2, block, CHUNK), BF16),
            pltpu.VMEM((LINK_RING, block, CHUNK), BF16),
            pltpu.VMEM((LINK_RING, block, CHUNK), BF16),
            pltpu.VMEM((LINK_RING, block, CHUNK), BF16),
        ] + [dma((chunks,))] * 10 + [
            pltpu.VMEM((hops, 8, ff), F32), pltpu.VMEM((hops, 8, ff), F32),
            dma((hops,)), dma((hops,)),
            pltpu.VMEM((1, width), F32), pltpu.VMEM((1, width), F32), pltpu.VMEM((1, 3 * width), F32),
        ],
        compiler_params=pltpu.CompilerParams(vmem_limit_bytes=60 * 2**20, collective_id=0, has_side_effects=True),
        name="back",
    )(count, segment, mlp, q, k, v, gc, x, base, t2, cosine, sine, g1, gain2, shift2, bup, bout, *loaded)


def finish_body(out_hbm, ig_hbm, total_ref, vec_ref, out_to, ig_to, up_ref, down_ref, low_ref, qkv_ref,
                gain1_ref, shift1_ref, bqkv_ref, bout_ref, gain2_ref, shift2_ref, bup_ref, bdown_ref, sem):
    copies = [pltpu.make_async_copy(out_hbm, out_to, sem.at[0]), pltpu.make_async_copy(ig_hbm, ig_to, sem.at[1])]
    for copy in copies:
        copy.start()
    width, ff = gain1_ref.shape[0], bup_ref.shape[0]
    factor = 1.0 / vec_ref[3:4, 0:1]
    groups = width // PIECE
    n_up = ff // CHUNK
    for i in range(total_ref.shape[0]):
        grad = total_ref[i].astype(F32) * factor
        kind, *what = chunk_columns(i, groups, 2 * n_up // groups)
        if kind == "mlp":
            ref, j = (up_ref, what[0]) if what[0] < n_up else (down_ref, what[0] - n_up)
            ref[:, j * CHUNK : (j + 1) * CHUNK] = grad
            continue
        for e, s in enumerate(what):
            ref, col = (qkv_ref, (s % 3) * width + (s // 3) * PIECE) if s < 3 * groups else (low_ref, (s - 3 * groups) * PIECE)
            ref[:, col : col + PIECE] = grad[:, e * PIECE : (e + 1) * PIECE]
    vec = vec_ref[...] * factor
    bup_ref[...] = vec[0]
    bqkv_ref[...] = vec[1, : 3 * width]
    bout_ref[...] = vec[1, 3 * width :]
    bdown_ref[...] = vec[1, 3 * width :]
    for j, ref in enumerate((gain1_ref, shift1_ref, gain2_ref, shift2_ref)):
        ref[...] = vec[2, j * width : (j + 1) * width]
    for copy in copies:
        copy.wait()


def finish(out, ig, total, vec):
    length, width = out.shape
    block, ff = total.shape[1], vec.shape[1]
    s = jax.ShapeDtypeStruct
    hbm, vmem = pl.BlockSpec(memory_space=pltpu.HBM), pl.BlockSpec(memory_space=pltpu.VMEM)
    vectors = (width, width, 3 * width, width, width, width, ff, width)
    return pl.pallas_call(
        finish_body,
        in_specs=[hbm, hbm, vmem, vmem],
        out_specs=[hbm, hbm] + [vmem] * 12,
        out_shape=[s(out.shape, BF16), s(ig.shape, BF16), s((block, ff), F32), s((block, ff), F32), s((block, width), F32),
                   s((block, 3 * width), F32)] + [s((n,), F32) for n in vectors],
        scratch_shapes=[pltpu.SemaphoreType.DMA((2,))],
        compiler_params=pltpu.CompilerParams(vmem_limit_bytes=40 * 2**20),
        name="finish",
    )(out, ig, total, vec)


def by_collectives(count, segment, mlp, q, k, v, gc, x, base, t2, cosine, sine, g1, gain2, shift2, bup, bout, n2t, glt, n1t, gl,
                   wout, wqkv):
    width, ff = x.shape[1], bup.shape[1]
    ctx, ctxt, gu = attention(q, k, v, gc, segment, cosine, sine)
    flat = jnp.concatenate([gu[0], gu[1], gu[2]], axis=1)
    low = jnp.concatenate(list(gl), axis=1)
    out = (base + nn(ctx, wout)).astype(BF16)
    grad_one = nt(flat, wqkv)
    x = x.astype(F32)
    centred = x - jnp.mean(x, axis=1, keepdims=True)
    r = lax.rsqrt(jnp.mean(centred * centred, axis=1, keepdims=True) + EPSILON)
    n = centred * r
    t = grad_one * g1 + t2
    dx = r * (t - jnp.mean(t, axis=1, keepdims=True) - n * jnp.mean(t * n, axis=1, keepdims=True))
    input_grad = (low.astype(F32) + dx).astype(BF16)
    packed = jnp.concatenate([bup[0], jnp.sum(flat, axis=0, dtype=F32), bout[0], jnp.sum(grad_one * n, axis=0),
                              jnp.sum(grad_one, axis=0), gain2[0], shift2[0], jnp.full(ff, count[0].astype(F32))])
    packed = lax.psum(packed, ("dp", "rows"))
    mlp_part = jnp.concatenate([nn(n2t, mlp[:, :ff]), nn(glt, mlp[:, ff:])], axis=1)
    rest = [nn(n1t, gu[s % 3, :, (s // 3) * PIECE : (s // 3 + 1) * PIECE]) for s in range(3 * width // PIECE)]
    rest = jnp.concatenate(rest + [nn(ctxt, low)], axis=1)
    columns = []
    for i in range((mlp_part.shape[1] + rest.shape[1]) // CHUNK):
        kind, j, *_ = chunk_columns(i, width // PIECE, 2 * ff // CHUNK * PIECE // width)
        begin = j * (CHUNK if kind == "mlp" else PIECE)
        columns.append((mlp_part if kind == "mlp" else rest)[:, begin : begin + CHUNK])
    part = jnp.stack(columns, axis=1).astype(BF16)
    grads = lax.psum(lax.psum_scatter(part, "dp", scatter_dimension=0, tiled=True), "rows")
    return out, input_grad, jnp.swapaxes(grads, 0, 1), packed.reshape(4, -1)


def shards(tokens, segment_ids, true_counts, regroup, cotangent, ln1_gain, ln1_bias, qkv_weight, qkv_bias, out_weight,
           out_bias, ln2_gain, ln2_bias, up_weight, up_bias, down_weight, down_bias):
    length, width = cotangent.shape
    ff = up_weight.shape[1]
    cosine, sine = (jnp.asarray(t) for t in rotary_tables(length))
    (arrived, q, k, v, gc, n1t, n2t, glt, gl, mlp, base, t2, gain2, shift2, bias_up, bias_out) = front(
        true_counts, regroup, tokens, cotangent, cosine, sine, ln1_gain, ln1_bias, qkv_weight, qkv_bias, out_weight, out_bias,
        ln2_gain, ln2_bias, up_weight, up_bias, down_weight, down_bias)
    last = back if (lax.axis_size("dp"), lax.axis_size("rows")) == (8, 4) else by_collectives
    out, input_grad, total, vec = last(true_counts, segment_ids, mlp, q, k, v, gc, arrived, base, t2, cosine, sine, ln1_gain, gain2,
                                       shift2, bias_up, bias_out, n2t, glt, n1t, gl, out_weight, qkv_weight)
    (out, input_grad, up, down, low, qkv, gain1, shift1, bias_qkv, bias_out, gain2, shift2, bias_up, bias_down) = finish(
        out, input_grad, total, vec)
    return (out, input_grad, gain1, shift1, qkv, bias_qkv, low, bias_out, gain2, shift2, up, bias_up, down.T, bias_down)


def solution(mesh):
    both = ("dp", "rows")
    placed = (P(both, None), P(both), P(both), P(both), P(both, None)) + (P(),) * 12
    return jax.shard_map(
        shards, mesh=mesh, in_specs=placed,
        out_specs=(P(both, None), P(both, None), P(), P(), P("dp", None), P(), P("dp", None), P(), P(), P(), P("dp", None), P(),
                   P(None, "dp"), P()),
        check_vma=False)
```

```python
import functools
import numpy as np
import jax
import jax.numpy as jnp
from jax import lax
from jax.experimental import pallas as pl
from jax.experimental.pallas import tpu as pltpu
from jax.sharding import PartitionSpec as P

HEAD_DIM = 64
ROT = 16
PAIR = 128
CHUNK = 512
PIECE = 256
GROUP = 2
SPAN = 256
EPSILON = 1e-05
EXCLUDED = -1e30
F32 = jnp.float32
BF16 = jnp.bfloat16
MESH = pl.DeviceIdType.MESH


def remote(src, dst, send, recv, to):
    return pltpu.make_async_remote_copy(src_ref=src, dst_ref=dst, send_sem=send, recv_sem=recv, device_id=to, device_id_type=MESH)


def nn(a, b):
    return lax.dot_general(a, b, (((1,), (0,)), ((), ())), preferred_element_type=F32)


def nt(a, b):
    return lax.dot_general(a, b, (((1,), (1,)), ((), ())), preferred_element_type=F32)


def tn(a, b):
    return lax.dot_general(a, b, (((0,), (0,)), ((), ())), preferred_element_type=F32)


def rotary_tables(length):
    half = ROT // 2
    placed = np.arange(length, dtype=np.float32)
    rates = np.exp(np.arange(half, dtype=np.float32) * np.float32(-2.0 / ROT) * np.log(np.float32(10000.0)))
    phases = placed[:, None] * rates[None, :].astype(np.float32)
    cosine = np.ones((length, HEAD_DIM), np.float32)
    sine = np.zeros((length, HEAD_DIM), np.float32)
    cosine[:, :half] = np.cos(phases)
    cosine[:, half:ROT] = np.cos(phases)
    sine[:, :half] = -np.sin(phases)
    sine[:, half:ROT] = np.sin(phases)
    return np.tile(cosine, (1, PAIR // HEAD_DIM)), np.tile(sine, (1, PAIR // HEAD_DIM))


def turned(u):
    lane = lax.broadcasted_iota(jnp.int32, u.shape, 1) % HEAD_DIM
    half = ROT // 2
    return jnp.where(lane < half, pltpu.roll(u, PAIR - half, 1), pltpu.roll(u, half, 1))


def gelu_parts(h):
    e = jnp.exp(h * h * -0.5)
    t = 1.0 / (1.0 + 0.2316418882 * jnp.abs(h))
    poly = t * (0.127414796 + t * (-0.142248368 + t * (0.7107068705 + t * (-0.7265760135 + t * 0.5307027145))))
    tail = poly * e
    phi = jnp.where(h >= 0, 1.0 - tail, tail)
    return h * phi, phi + h * (e * 0.3989422804014327)


def attend(q, k, v, gc, begins, t_first):
    each, rows, span = range(len(q)), q[0].shape[0], k[0].shape[0]
    low = lax.broadcasted_iota(jnp.int32, (rows, PAIR), 1) < HEAD_DIM

    def both(t):
        zero = jnp.zeros_like(t)
        return jnp.concatenate([jnp.where(low, t, zero), jnp.where(low, zero, t)], axis=0)

    q2, g2 = [both(t) for t in q], [both(t) for t in gc]
    s_at = lax.broadcasted_iota(jnp.int32, (rows, span), 1)
    t_at = t_first + lax.broadcasted_iota(jnp.int32, (rows, span), 0)
    allowed = (s_at >= begins) & (s_at <= t_at)
    allowed = jnp.concatenate([allowed, allowed], axis=0)
    scores = [jnp.where(allowed, nt(q2[h], k[h]), EXCLUDED) for h in each]
    dp = [nt(g2[h], v[h]) for h in each]
    e = [jnp.exp(scores[h] - jnp.max(scores[h], axis=1, keepdims=True)) for h in each]
    p = [e[h] * (1.0 / jnp.sum(e[h], axis=1, keepdims=True)) for h in each]
    p16 = [p[h].astype(BF16) for h in each]
    c2 = [nn(p16[h], v[h]) for h in each]
    dv = [tn(p16[h], g2[h]) for h in each]
    w = [p[h] * dp[h] for h in each]
    ds16 = [(w[h] - p[h] * jnp.sum(w[h], axis=1, keepdims=True)).astype(BF16) for h in each]
    d2 = [nn(ds16[h], k[h]) for h in each]
    dk = [tn(ds16[h], q2[h]) for h in each]
    context = [jnp.where(low, c2[h][:rows], c2[h][rows:]).astype(BF16) for h in each]
    dq = [jnp.where(low, d2[h][:rows], d2[h][rows:]) * (HEAD_DIM ** -0.5) for h in each]
    return context, dq, dk, dv


def front_body(count_ref, want_ref, own_ref, cot_ref, cos_ref, sin_ref, g1_vec, b1_vec, bqkv_vec, bout_vec, g2_vec, b2_vec,
               bup_vec, bdown_vec, wqkv_hbm, wout_hbm, wup_hbm, wdown_hbm,
               x_ref, q_ref, k_ref, v_ref, gc_ref, n1t_ref, n2t_ref, glt_ref, gl_ref, mlp_ref, base_ref, t2_ref,
               gain2_ref, shift2_ref, bup_out, bout_out,
               wqkv_ref, wout_ref, wup_ref, wdown_ref, wants, from_near, from_half, to_inner, to_end,
               g1_ref, b1_ref, bqkv_ref, bout_ref, g2_ref, b2_ref, bup_ref, bdown_ref, gl_all, ga_all, gc_all, w_sem, want_send, want_recv, near_send, near_recv, inner_send, end_send, half_recv, *, tile):
    step = pl.program_id(0)
    steps = pl.num_programs(0)
    length, width = cot_ref.shape
    rows = x_ref.shape[0]
    pairs = width // PAIR
    ff = wup_ref.shape[1]
    chunks = length // rows
    part = rows // 2
    parts = length // part
    d, z = lax.axis_index("dp"), lax.axis_index("rows")
    inner = (z + 1) // 2 % 2
    near = z + 1 - 2 * (z % 2)
    other_inner, other_end = 3 - z, 6 - 3 * z
    loads = [pltpu.make_async_copy(src, dst, w_sem.at[j]) for j, (src, dst) in enumerate(
        ((wdown_hbm, wdown_ref), (wout_hbm, wout_ref), (wqkv_hbm, wqkv_ref), (wup_hbm, wup_ref)))]

    def span(i):
        return pl.ds(pl.multiple_of(i * rows, rows), rows)

    def bit(i):
        return pl.ds(pl.multiple_of(i * part, part), part)

    def want_copy(j):
        to = lax.rem(z + j, 4)
        return remote(wants.at[0], wants.at[j], want_send.at[j], want_recv.at[j], (d, to))

    def near_copy(i):
        return remote(own_ref.at[bit(i)], from_near.at[bit(i)], near_send.at[i], near_recv.at[i], (d, near))

    def inner_copy(i):
        return remote(to_inner.at[bit(i)], from_half.at[bit(i)], inner_send.at[i], half_recv.at[i], (d, other_inner))

    def end_copy(i):
        return remote(to_end.at[bit(i)], from_half.at[bit(i)], end_send.at[i], half_recv.at[i], (d, other_end))

    def wanted(by):
        return wants[lax.rem(z - by + 4, 4), 0:1, 0:1]

    def relay(i):
        @pl.when(inner == 1)
        def _():
            near_copy(i).wait_recv()
            mine = own_ref[bit(i), :].astype(F32)
            theirs = from_near[bit(i), :].astype(F32)
            to_end[bit(i), :] = jnp.where(wanted(other_end) == near, theirs, mine).astype(BF16)
            end_copy(i).start()
            to_inner[bit(i), :] = jnp.where(wanted(other_inner) == near, theirs, mine).astype(BF16)
            inner_copy(i).start()

    @pl.when(step == 0)
    def _():
        barrier = pltpu.get_barrier_semaphore()
        for j in (1, 2, 3):
            pl.semaphore_signal(barrier, inc=1, device_id=(d, lax.rem(z + j, 4)), device_id_type=MESH)
        wants[0] = jnp.full(wants.shape[1:], want_ref[0] % 4, jnp.int32)
        pl.semaphore_wait(barrier, 3)
        for j in (1, 2, 3):
            want_copy(j).start()

        def hand(i, carry):
            near_copy(i).start()
            return carry

        lax.fori_loop(0, parts, hand, 0)
        for load in loads:
            load.start()
        for vec, ref in ((g1_vec, g1_ref), (b1_vec, b1_ref), (bqkv_vec, bqkv_ref), (bout_vec, bout_ref), (g2_vec, g2_ref),
                         (b2_vec, b2_ref), (bup_vec, bup_ref), (bdown_vec, bdown_ref)):
            ref[...] = vec[...].reshape(1, -1)
        gain2_ref[...] = jnp.zeros_like(gain2_ref)
        shift2_ref[...] = jnp.zeros_like(shift2_ref)
        bup_out[...] = jnp.zeros_like(bup_out)
        place = lax.broadcasted_iota(jnp.int32, (length, 1), 0)
        masked = jnp.where(place < count_ref[0], cot_ref[...].astype(F32), 0.0)
        gl_all[...] = masked.astype(BF16)
        bout_out[...] = jnp.sum(masked, axis=0, keepdims=True)

        def active(f):
            ga_all[f] = nt(gl_all[...], wdown_ref[f * tile : (f + 1) * tile, :])

        tiles = ff // tile
        loads[0].wait()
        for f in range(2):
            active(f)
        for j in (1, 2, 3):
            want_copy(j).wait()
        relay(0)
        relay(1)
        for f in range(2, tiles - 1):
            active(f)
        relay(2)
        relay(3)
        active(tiles - 1)
        loads[1].wait()
        for p in range(pairs):
            gc_all[p] = nt(gl_all[...], wout_ref[p * PAIR : (p + 1) * PAIR, :]).astype(BF16)
        for load in loads[2:]:
            load.wait()

    @pl.when((step > 0) & (step + 1 < chunks))
    def _():
        relay(2 * step + 2)
        relay(2 * step + 3)

    gl16 = gl_all[span(step), :]
    for j in range(gl_ref.shape[0]):
        gl_ref[j] = gl16[:, j * PIECE : (j + 1) * PIECE]
    glt_ref[...] = gl16.T
    for p in range(pairs):
        gc_ref[p] = gc_all[p, span(step), :]

    @pl.when(inner == 0)
    def _():
        for j in range(2):
            near_copy(2 * step + j).wait_recv()

    for j in range(2):
        inner_copy(2 * step + j).wait_recv()
    source = wanted(z)
    x = jnp.where(source == near, from_near[span(step), :].astype(F32), from_half[span(step), :].astype(F32))
    x = jnp.where(source == z, own_ref[span(step), :].astype(F32), x)
    x_ref[...] = x.astype(BF16)
    centred = x - jnp.mean(x, axis=1, keepdims=True)
    r = lax.rsqrt(jnp.mean(centred * centred, axis=1, keepdims=True) + EPSILON)
    n = centred * r
    n1 = (n * g1_ref[...] + b1_ref[...]).astype(BF16)
    n2 = (n * g2_ref[...] + b2_ref[...]).astype(BF16)
    n1t_ref[...] = n1.T
    n2t_ref[...] = n2.T
    cosine, sine = cos_ref[...], sin_ref[...]
    for p in range(pairs):
        for which, ref in enumerate((q_ref, k_ref, v_ref)):
            wide = slice(which * width + p * PAIR, which * width + (p + 1) * PAIR)
            u = nn(n1, wqkv_ref[:, wide]) + bqkv_ref[:, wide]
            if which < 2:
                u = u * cosine + turned(u) * sine
            if which == 0:
                u = u * (HEAD_DIM ** -0.5)
            ref[p] = u.astype(BF16)
    mlp = x + (bdown_ref[...] + bout_ref[...])
    grad_two = jnp.zeros((rows, width), F32)
    for f in range(0, ff, tile):
        cols = slice(f, f + tile)
        h = nn(n2, wup_ref[:, cols]) + bup_ref[:, cols]
        ga = ga_all[f // tile, span(step), :]
        a, slope = gelu_parts(h)
        a16 = a.astype(BF16)
        gh = ga * slope
        gh16 = gh.astype(BF16)
        mlp_ref[:, cols] = gh16
        mlp_ref[:, ff + f : ff + f + tile] = a16
        bup_out[:, cols] += jnp.sum(gh16.astype(F32), axis=0, keepdims=True)
        mlp = mlp + nn(a16, wdown_ref[cols, :])
        grad_two = grad_two + nt(gh16, wup_ref[:, cols])
    base_ref[...] = mlp
    t2_ref[...] = grad_two * g2_ref[...]
    gain2_ref[...] += jnp.sum(grad_two * n, axis=0, keepdims=True)
    shift2_ref[...] += jnp.sum(grad_two, axis=0, keepdims=True)

    @pl.when(step == steps - 1)
    def _():
        def done(i, carry):
            near_copy(i).wait_send()

            @pl.when(inner == 1)
            def _():
                inner_copy(i).wait_send()
                end_copy(i).wait_send()
            return carry

        lax.fori_loop(0, parts, done, 0)


def front(count, want, own, cot, cosine, sine, g1, b1, wqkv, bqkv, wout, bout, g2, b2, wup, bup, wdown, bdown, rows=128, tile=512):
    length, width = own.shape
    ff = wup.shape[1]
    pairs = width // PAIR
    chunks = length // rows

    def row(cols):
        return pl.BlockSpec((rows, cols), lambda i: (i, 0))

    def whole(a):
        return pl.BlockSpec(a.shape, lambda i: (0,) * a.ndim, pipeline_mode=pl.Buffered(1))

    heads = pl.BlockSpec((pairs, rows, PAIR), lambda i: (0, i, 0))
    down = pl.BlockSpec((width, rows), lambda i: (0, i))

    def vec(cols):
        return pl.BlockSpec((1, cols), lambda i: (0, 0))

    vectors = (g1, b1, bqkv, bout, g2, b2, bup, bdown)
    weights = (wqkv, wout, wup, wdown)
    s = jax.ShapeDtypeStruct
    dma = pltpu.SemaphoreType.DMA
    return pl.pallas_call(
        functools.partial(front_body, tile=tile),
        grid=(chunks,),
        in_specs=[pl.BlockSpec(memory_space=pltpu.SMEM), pl.BlockSpec(memory_space=pltpu.SMEM), whole(own), whole(cot), row(PAIR), row(PAIR)]
        + [whole(a) for a in vectors] + [pl.BlockSpec(memory_space=pl.ANY)] * 4,
        out_specs=[row(width)] + [heads] * 4 + [down] * 3
        + [pl.BlockSpec((width // PIECE, rows, PIECE), lambda i: (0, i, 0)), row(2 * ff)] + [row(width)] * 2
        + [vec(width), vec(width), vec(ff), vec(width)],
        out_shape=[s((length, width), BF16)] + [s((pairs, length, PAIR), BF16)] * 4 + [s((width, length), BF16)] * 3
        + [s((width // PIECE, length, PIECE), BF16), s((length, 2 * ff), BF16)]
        + [s((length, width), F32)] * 2 + [s((1, width), F32), s((1, width), F32), s((1, ff), F32), s((1, width), F32)],
        scratch_shapes=[pltpu.VMEM(w.shape, BF16) for w in weights]
        + [pltpu.VMEM((4, 8, 128), jnp.int32)] + [pltpu.VMEM((length, width), BF16)] * 4
        + [pltpu.VMEM((1, v.shape[0]), F32) for v in vectors]
        + [pltpu.VMEM((length, width), BF16), pltpu.VMEM((ff // tile, length, tile), F32), pltpu.VMEM((pairs, length, PAIR), BF16)]
        + [dma((4,)), dma((4,)), dma((4,))] + [dma((2 * chunks,))] * 5,
        compiler_params=pltpu.CompilerParams(vmem_limit_bytes=60 * 2**20, collective_id=1, has_side_effects=True),
        name="front",
    )(count, want, own, cot, cosine, sine, *vectors, *weights)


def attention_body(q_ref, k_ref, v_ref, gc_ref, seg_ref, cos_ref, sin_ref,
                   ctx_ref, ctxt_ref, gu_ref, dk_acc, dv_acc, segc_ref, segr_ref, first_ref, *, rows):
    group, length, _ = q_ref.shape
    total = length // rows
    each = range(group)

    @pl.when(pl.program_id(0) == 0)
    def _():
        seg = seg_ref[...].reshape(1, -1)
        segr_ref[...] = seg
        segc_ref[...] = jnp.broadcast_to(seg, (8, length)).T[:, :1]
        wide = seg.astype(F32)
        for b in range(total):
            before = jnp.sum(jnp.where(wide < wide[:, b * rows : b * rows + 1], 1.0, 0.0))
            first_ref[b] = before.astype(jnp.int32) // rows

    lane = lax.broadcasted_iota(jnp.int32, (rows, PAIR), 1)
    low = lane < HEAD_DIM
    dk_acc[...] = jnp.zeros_like(dk_acc)
    dv_acc[...] = jnp.zeros_like(dv_acc)

    def both(ref, h, begin):
        t = ref[h, pl.ds(begin, rows), :]
        zero = jnp.zeros_like(t)
        return jnp.concatenate([jnp.where(low, t, zero), jnp.where(low, zero, t)], axis=0)

    def block(b, blocks):
        begin = pl.multiple_of(b * rows, rows)
        start = pl.multiple_of((b + 1 - blocks) * rows, rows)
        span = blocks * rows
        q2 = [both(q_ref, h, begin) for h in each]
        g2 = [both(gc_ref, h, begin) for h in each]
        k = [k_ref[h, pl.ds(start, span), :] for h in each]
        v = [v_ref[h, pl.ds(start, span), :] for h in each]
        segt = segc_ref[pl.ds(begin, rows), :]
        segs = segr_ref[:, pl.ds(start, span)]
        t_at = begin + lax.broadcasted_iota(jnp.int32, (rows, span), 0)
        s_at = start + lax.broadcasted_iota(jnp.int32, (rows, span), 1)
        allowed = (segt == segs) & (s_at <= t_at)
        allowed = jnp.concatenate([allowed, allowed], axis=0)
        scores = [jnp.where(allowed, nt(q2[h], k[h]), EXCLUDED) for h in each]
        dp = [nt(g2[h], v[h]) for h in each]
        e = [jnp.exp(scores[h] - jnp.max(scores[h], axis=1, keepdims=True)) for h in each]
        p = [e[h] * (1.0 / jnp.sum(e[h], axis=1, keepdims=True)) for h in each]
        p16 = [p[h].astype(BF16) for h in each]
        c2 = [nn(p16[h], v[h]) for h in each]
        for h in each:
            dv_acc[h, pl.ds(start, span), :] += tn(p16[h], g2[h])
        w = [p[h] * dp[h] for h in each]
        ds16 = [(w[h] - p[h] * jnp.sum(w[h], axis=1, keepdims=True)).astype(BF16) for h in each]
        d2 = [nn(ds16[h], k[h]) for h in each]
        for h in each:
            dk_acc[h, pl.ds(start, span), :] += tn(ds16[h], q2[h])
        cosine = cos_ref[pl.ds(begin, rows), :]
        sine = sin_ref[pl.ds(begin, rows), :]
        for h in each:
            cols = slice(h * PAIR, (h + 1) * PAIR)
            context = jnp.where(low, c2[h][:rows], c2[h][rows:]).astype(BF16)
            ctx_ref[pl.ds(begin, rows), cols] = context
            ctxt_ref[cols, pl.ds(begin, rows)] = context.T
            dq = jnp.where(low, d2[h][:rows], d2[h][rows:]) * (HEAD_DIM ** -0.5)
            gu_ref[0, pl.ds(begin, rows), cols] = (dq * cosine - turned(dq) * sine).astype(BF16)

    def loop(b, carry):
        count = b + 1 - first_ref[b]
        for blocks in range(1, total + 1):
            @pl.when(count == blocks)
            def _():
                block(b, blocks)
        return carry

    lax.fori_loop(0, total, loop, 0)
    for h in each:
        cols = slice(h * PAIR, (h + 1) * PAIR)
        dk = dk_acc[h]
        gu_ref[1, :, cols] = (dk * cos_ref[...] - turned(dk) * sin_ref[...]).astype(BF16)
        gu_ref[2, :, cols] = dv_acc[h].astype(BF16)


def attention(q, k, v, gc, segment, cosine, sine, rows=256, group=2):
    pairs, length, _ = q.shape
    head = pl.BlockSpec((group, length, PAIR), lambda h: (h, 0, 0))
    cols = pl.BlockSpec((length, group * PAIR), lambda h: (0, h))
    s = jax.ShapeDtypeStruct
    width = pairs * PAIR

    def whole(a):
        return pl.BlockSpec(a.shape, lambda h: (0,) * a.ndim, pipeline_mode=pl.Buffered(1))

    return pl.pallas_call(
        functools.partial(attention_body, rows=rows),
        grid=(pairs // group,),
        in_specs=[head] * 4 + [whole(segment), whole(cosine), whole(sine)],
        out_specs=[cols, pl.BlockSpec((group * PAIR, length), lambda h: (h, 0)),
                   pl.BlockSpec((3, length, group * PAIR), lambda h: (0, 0, h))],
        scratch_shapes=[pltpu.VMEM((group, length, PAIR), F32)] * 2
        + [pltpu.VMEM((length, 1), jnp.int32), pltpu.VMEM((1, length), jnp.int32), pltpu.SMEM((length // rows,), jnp.int32)],
        out_shape=[s((length, width), BF16), s((width, length), BF16), s((3, length, width), BF16)],
        compiler_params=pltpu.CompilerParams(vmem_limit_bytes=56 * 2**20),
        name="attention",
    )(q, k, v, gc, segment, cosine, sine)


class Line:
    def __init__(self):
        self.d = lax.axis_index("dp")
        self.z = lax.axis_index("rows")
        self.core = self.d % 2
        self.x = (self.d // 2) % 2
        self.y = self.d // 4
        self.over_core = (self.d + 1 - 2 * self.core, self.z)
        self.over_x = (self.d + 2 - 4 * self.x, self.z)
        self.over_y = (self.d + 4 - 8 * self.y, self.z)
        self.inner = (self.z + 1) // 2 % 2
        self.near = (self.d, self.z + 1 - 2 * (self.z % 2))
        self.far = (self.d, 3 - self.z)


class Everywhere:
    def __init__(self, at, of_dp, of_rows, send, recv):
        self.at, self.of_dp, self.of_rows, self.send, self.recv = at, of_dp, of_rows, send, recv
        self.devices, self.lines = of_dp.shape[0], of_rows.shape[0]

    def over_dp(self, j):
        at = self.at
        mine = self.of_dp.at[at.d]
        return remote(mine, mine, self.send.at[j], self.recv.at[j], (lax.rem(at.d + j, self.devices), at.z))

    def over_rows(self, j):
        at, sem = self.at, self.devices + j
        mine = self.of_rows.at[at.z]
        return remote(mine, mine, self.send.at[sem], self.recv.at[sem], (at.d, lax.rem(at.z + j, self.lines)))

    def begin(self, rows):
        self.of_dp[self.at.d] = jnp.concatenate(rows, axis=0)
        for j in range(1, self.devices):
            self.over_dp(j).start()

    def turn(self):
        for j in range(1, self.devices):
            self.over_dp(j).wait()
        total = self.of_dp[0]
        for j in range(1, self.devices):
            total = total + self.of_dp[j]
        self.of_rows[self.at.z] = total
        for j in range(1, self.lines):
            self.over_rows(j).start()

    def end(self):
        for j in range(1, self.lines):
            self.over_rows(j).wait()
        total = self.of_rows[0]
        for j in range(1, self.lines):
            total = total + self.of_rows[j]
        return total


LAGS = dict(core=1, first=3, second=5, z=7, mid=9, back=10)
RING, CORE_RING, LINK_RING = 7, 6, 8


def chunk_columns(i, n_mlp, pieces, per_group):
    period = per_group + 1
    busy = n_mlp // per_group * period
    if i < busy and i % period < per_group:
        return "mlp", per_group * (i // period) + i % period
    j = i // period if i < busy else i - n_mlp
    wide = pieces // 3
    return ("rest", 2 * j, 2 * j + 1) if j < wide else ("rest", j + wide)


def back_body(count_ref, seg_ref, mlp_ref, q_ref, k_ref, v_ref, gc_ref, x_ref, base_ref, t2_ref, cos_ref, sin_ref, g1_ref,
              gain2_ref, shift2_ref, bup_ref, bout_ref, n2t_hbm, glt_hbm, n1t_hbm, gl_hbm, wout_hbm, wqkv_hbm,
              out_ref, ig_ref, total_ref, vec_ref,
              left_mlp, left_rest, rhs, wout_ref, wqkv_ref, load_sem, ctx, dk_acc, dv_acc, begin_ref,
              part, from_core, from_first, from_second, from_near, from_far,
              c_send, c_recv, f_send, f_recv, s_send, s_recv, n_send, n_recv, m_send, m_recv,
              dp_e, rows_e, dp_l, rows_l, e_send, e_recv, l_send, l_recv, gain1, shift1, bqkv, *, rows, row_ticks):
    tick = pl.program_id(0)
    at = Line()
    chunks, block = total_ref.shape[0], total_ref.shape[1]
    length, width = seg_ref.shape[0], wout_ref.shape[0]
    groups = width // PIECE
    per_group = length // rows
    n_mlp, pieces = 2 * bup_ref.shape[1] // CHUNK, 4 * groups
    n_wide = n_mlp + pieces // 3
    period = per_group + 1
    busy = groups * period
    g, spot = jnp.minimum(tick // period, groups - 1), tick % period
    attending = (tick < busy) & (spot < per_group)
    first_need = (pltpu.make_async_copy(n2t_hbm, left_mlp.at[0], load_sem.at[0]),)
    later_need = [pltpu.make_async_copy(src, dst, load_sem.at[1 + j]) for j, (src, dst) in enumerate(
        ((glt_hbm, left_mlp.at[1]), (n1t_hbm, left_rest.at[0]), (gl_hbm, rhs.at[pl.ds(3 * groups, groups)]),
         (wout_hbm, wout_ref), (wqkv_hbm, wqkv_ref)))]

    @pl.when(tick == 0)
    def _():
        first_need[0].start()
        barrier = pltpu.get_barrier_semaphore()
        for j in range(1, 8):
            pl.semaphore_signal(barrier, inc=1, device_id=(lax.rem(at.d + j, 8), at.z), device_id_type=MESH)
        for j in range(1, 4):
            pl.semaphore_signal(barrier, inc=1, device_id=(at.d, lax.rem(at.z + j, 4)), device_id_type=MESH)
        pl.semaphore_wait(barrier, 10)
        for load in later_need:
            load.start()
        wide = jnp.broadcast_to(seg_ref[...].reshape(1, -1), (8, length)).astype(F32)
        tall = wide.T[:, :1]
        for b in range(0, length, PAIR):
            earlier = jnp.where(wide[:1] < tall[b : b + PAIR], 1.0, 0.0)
            begin_ref[b : b + PAIR, :] = jnp.sum(earlier, axis=1, keepdims=True).astype(jnp.int32)
        gain1[...] = jnp.zeros_like(gain1)
        shift1[...] = jnp.zeros_like(shift1)
        bqkv[...] = jnp.zeros_like(bqkv)
        first_need[0].wait()

    @pl.when(tick == 1)
    def _():
        for load in later_need:
            load.wait()

    def places(i):
        even = 1 - i % 2
        f = at.x * even + at.y * (1 - even)
        s = at.y * even + at.x * (1 - even)
        first = (at.d + even * (2 - 4 * at.x) + (1 - even) * (4 - 8 * at.y), at.z)
        second = (at.d + even * (4 - 8 * at.y) + (1 - even) * (2 - 4 * at.x), at.z)
        return f, s, first, second, i % RING

    def core_copy(i, w):
        lanes = pl.ds(0, w)
        return remote(part.at[i % RING, 1 - at.core, :, :, :, lanes], from_core.at[i % CORE_RING, :, :, :, lanes],
                      c_send.at[i], c_recv.at[i], at.over_core)

    def first_copy(i, w):
        f, s, first, second, slot = places(i)
        lanes = pl.ds(0, w)
        return remote(part.at[slot, at.core, 1 - f, :, :, lanes], from_first.at[i % LINK_RING, :, :, lanes],
                      f_send.at[i], f_recv.at[i], first)

    def second_copy(i, w):
        f, s, first, second, slot = places(i)
        lanes = pl.ds(0, w)
        return remote(part.at[slot, at.core, f, 1 - s, :, lanes], from_second.at[i % LINK_RING, :, lanes],
                      s_send.at[i], s_recv.at[i], second)

    def out_copy(i, w):
        lanes = pl.ds(0, w)
        return remote(total_ref.at[i, :, lanes], from_near.at[i % LINK_RING, :, lanes], n_send.at[i], n_recv.at[i], at.near)

    def far_copy(i, w):
        lanes = pl.ds(0, w)
        return remote(total_ref.at[i, :, lanes], from_far.at[i % LINK_RING, :, lanes], m_send.at[i], m_recv.at[i], at.far)

    def plus(a, b):
        return (a.astype(F32) + b.astype(F32)).astype(BF16)

    def put(h, half, cols, rows_of):
        even = 1 - tick % 2
        for j in range(4):
            d = h * 4 + j
            c, x, y = d % 2, (d // 2) % 2, d // 4
            a = x * even + y * (1 - even)
            b = y * even + x * (1 - even)
            part[tick % RING, c, a, b, :, cols] = rows_of[j * block : (j + 1) * block].astype(BF16)

    half = width // 2

    @pl.when(attending)
    def _():
        left = (per_group * g + spot) // (n_mlp // 2)
        for h in range(2):
            put(h, half, slice(0, CHUNK), nn(left_mlp[left, h * half : (h + 1) * half, :], mlp_ref[...]))
        core_copy(tick, CHUNK).start()

    def rest(s, e):
        for h in range(2):
            put(h, half, slice(e * PIECE, (e + 1) * PIECE),
                nn(left_rest[s // (3 * groups), h * half : (h + 1) * half, :], rhs[s]))

    @pl.when((tick < n_wide) & jnp.logical_not(attending))
    def _():
        late = tick // busy
        j = (tick // period) * (1 - late) + (tick - n_mlp) * late
        for e in range(2):
            rest(2 * j + e, e)
        core_copy(tick, CHUNK).start()

    @pl.when((tick >= n_wide) & (tick < chunks))
    def _():
        rest(tick - n_wide + 2 * (n_wide - n_mlp), 0)
        core_copy(tick, PIECE).start()

    def when(lag, f):
        i = tick - lag

        @pl.when((i >= 0) & (i < n_wide))
        def _():
            f(i, CHUNK)

        @pl.when((i >= n_wide) & (i < chunks))
        def _():
            f(i, PIECE)

    def core_step(i, w):
        f, s, first, second, slot = places(i)
        core_copy(i, w).wait()
        for a in range(2):
            for b in range(2):
                part[slot, at.core, a, b, :, :w] = plus(part[slot, at.core, a, b, :, :w], from_core[i % CORE_RING, a, b, :, :w])
        first_copy(i, w).start()

    def first_step(i, w):
        f, s, first, second, slot = places(i)
        first_copy(i, w).wait()
        for b in range(2):
            part[slot, at.core, f, b, :, :w] = plus(part[slot, at.core, f, b, :, :w], from_first[i % LINK_RING, b, :, :w])
        second_copy(i, w).start()

    def second_step(i, w):
        f, s, first, second, slot = places(i)
        second_copy(i, w).wait()
        total_ref[i, :, :w] = plus(part[slot, at.core, f, s, :, :w], from_second[i % LINK_RING, :, :w])

        @pl.when(at.inner == 0)
        def _():
            out_copy(i, w).start()

    def near_step(i, w):
        @pl.when(at.inner == 1)
        def _():
            out_copy(i, w).wait_recv()
            total_ref[i, :, :w] = plus(total_ref[i, :, :w], from_near[i % LINK_RING, :, :w])
            far_copy(i, w).start()

    def far_step(i, w):
        @pl.when(at.inner == 1)
        def _():
            far_copy(i, w).wait()
            total_ref[i, :, :w] = plus(total_ref[i, :, :w], from_far[i % LINK_RING, :, :w])
            out_copy(i, w).start()

        @pl.when(at.inner == 0)
        def _():
            out_copy(i, w).wait_send()

    def back_step(i, w):
        @pl.when(at.inner == 0)
        def _():
            out_copy(i, w).wait_recv()
            total_ref[i, :, :w] = from_near[i % LINK_RING, :, :w]

        @pl.when(at.inner == 1)
        def _():
            out_copy(i, w).wait_send()

    when(LAGS["core"], core_step)
    when(LAGS["first"], first_step)
    when(LAGS["second"], second_step)
    when(LAGS["z"], near_step)
    when(LAGS["mid"], far_step)
    when(LAGS["back"], back_step)

    each = range(GROUP)

    def unit(b):
        span = (b + 1) * rows
        mine = slice(b * rows, span)
        context, dq, dk, dv = attend([q_ref[h, mine, :] for h in each], [k_ref[h, :span, :] for h in each],
                                     [v_ref[h, :span, :] for h in each], [gc_ref[h, mine, :] for h in each],
                                     begin_ref[mine, :], b * rows)
        for h in each:
            cols = slice(h * PAIR, (h + 1) * PAIR)
            dk_acc[h, :span, :] += dk[h]
            dv_acc[h, :span, :] += dv[h]
            ctx[g, mine, cols] = context[h]
            left_rest[1, pl.ds(pl.multiple_of(g * PIECE + h * PAIR, PAIR), PAIR), mine] = context[h].T
            rhs[3 * g, mine, cols] = (dq[h] * cos_ref[mine, :] - turned(dq[h]) * sin_ref[mine, :]).astype(BF16)

    @pl.when(attending & (spot == 0))
    def _():
        dk_acc[...] = jnp.zeros_like(dk_acc)
        dv_acc[...] = jnp.zeros_like(dv_acc)

    for b in range(per_group):
        @pl.when(attending & (spot == b))
        def _():
            unit(b)

    @pl.when(attending & (spot == per_group - 1))
    def _():
        for h in each:
            cols = slice(h * PAIR, (h + 1) * PAIR)
            dk = dk_acc[h]
            rhs[3 * g + 1, :, cols] = (dk * cos_ref[...] - turned(dk) * sin_ref[...]).astype(BF16)
            rhs[3 * g + 2, :, cols] = dv_acc[h].astype(BF16)

    @pl.when((tick >= busy) & (tick < busy + row_ticks))
    def _():
        n_rows = x_ref.shape[0]
        here = pl.ds(pl.multiple_of((tick - busy) * n_rows, n_rows), n_rows)
        attn = base_ref[...]
        for j in range(groups):
            attn = attn + nn(ctx[j, here, :], wout_ref[j * PIECE : (j + 1) * PIECE, :])
        out_ref[...] = attn.astype(BF16)
        g1 = jnp.zeros(attn.shape, F32)
        for s in range(3 * groups):
            cols = slice((s % 3) * width + (s // 3) * PIECE, (s % 3) * width + (s // 3 + 1) * PIECE)
            grads = rhs[s, here, :]
            g1 = g1 + nt(grads, wqkv_ref[:, cols])
            bqkv[:, cols] += jnp.sum(grads.astype(F32), axis=0, keepdims=True)
        x = x_ref[...].astype(F32)
        centred = x - jnp.mean(x, axis=1, keepdims=True)
        r = lax.rsqrt(jnp.mean(centred * centred, axis=1, keepdims=True) + EPSILON)
        n = centred * r
        gain1[...] += jnp.sum(g1 * n, axis=0, keepdims=True)
        shift1[...] += jnp.sum(g1, axis=0, keepdims=True)
        t = g1 * g1_ref[...].reshape(1, -1) + t2_ref[...]
        dx = r * (t - jnp.mean(t, axis=1, keepdims=True) - n * jnp.mean(t * n, axis=1, keepdims=True))
        gl = jnp.concatenate([rhs[3 * groups + j, here, :] for j in range(groups)], axis=1)
        ig_ref[...] = (gl.astype(F32) + dx).astype(BF16)

    def lines(ref):
        return [ref[:, j : j + width] for j in range(0, ref.shape[1], width)]

    early = Everywhere(at, dp_e, rows_e, e_send, e_recv)
    late = Everywhere(at, dp_l, rows_l, l_send, l_recv)
    row = jnp.full((1, width), count_ref[0].astype(F32), F32)

    @pl.when(tick == 1)
    def _():
        early.begin(lines(bup_ref) + lines(bout_ref) + lines(gain2_ref) + lines(shift2_ref) + [row])

    @pl.when(tick == 4)
    def _():
        early.turn()

    @pl.when(tick == 7)
    def _():
        vec_ref[0] = early.end()

    begin = busy + row_ticks

    @pl.when(tick == begin)
    def _():
        late.begin(lines(gain1) + lines(shift1) + lines(bqkv) + [jnp.zeros((3, width), F32)])

    @pl.when(tick == begin + 2)
    def _():
        late.turn()

    @pl.when(tick == begin + 4)
    def _():
        vec_ref[1] = late.end()


def back(count, segment, mlp, q, k, v, gc, x, base, t2, cosine, sine, g1, gain2, shift2, bup, bout, n2t, glt, n1t, gl, wout, wqkv,
         rows=256):
    length, width = x.shape
    ff = bup.shape[1]
    block = width // 8
    groups = width // PIECE
    n_mlp, pieces = 2 * ff // CHUNK, 4 * groups
    chunks = n_mlp + pieces // 3 + pieces - 2 * (pieces // 3)
    row_ticks = length // rows
    period = row_ticks + 1
    busy = groups * period
    ticks = max(chunks + LAGS["back"], busy + row_ticks + 5)

    def row(cols):
        return pl.BlockSpec((rows, cols), lambda t: (jnp.clip(t - busy, 0, row_ticks - 1), 0))

    def whole(a):
        return pl.BlockSpec(a.shape, lambda t: (0,) * a.ndim, pipeline_mode=pl.Buffered(1))

    def mlp_cols(t):
        return (0, jnp.minimum(row_ticks * (t // period) + jnp.minimum(t % period, row_ticks - 1), n_mlp - 1))

    heads = pl.BlockSpec((GROUP, length, PAIR), lambda t: (jnp.minimum(t // period, groups - 1), 0, 0))
    s = jax.ShapeDtypeStruct
    dma = pltpu.SemaphoreType.DMA
    loaded = (n2t, glt, n1t, gl, wout, wqkv)
    return pl.pallas_call(
        functools.partial(back_body, rows=rows, row_ticks=row_ticks),
        grid=(ticks,),
        in_specs=[pl.BlockSpec(memory_space=pltpu.SMEM), whole(segment), pl.BlockSpec((length, CHUNK), mlp_cols)]
        + [heads] * 4 + [row(width)] * 3
        + [whole(a) for a in (cosine, sine, g1, gain2, shift2, bup, bout)] + [pl.BlockSpec(memory_space=pl.ANY)] * len(loaded),
        out_specs=[row(width), row(width),
                   pl.BlockSpec((chunks, block, CHUNK), lambda t: (0, 0, 0), pipeline_mode=pl.Buffered(1)),
                   pl.BlockSpec((2, 8, width), lambda t: (0, 0, 0), pipeline_mode=pl.Buffered(1))],
        out_shape=[s((length, width), BF16), s((length, width), BF16), s((chunks, block, CHUNK), BF16), s((2, 8, width), F32)],
        scratch_shapes=[
            pltpu.VMEM((2, width, length), BF16),
            pltpu.VMEM((2, width, length), BF16),
            pltpu.VMEM((4 * groups, length, PIECE), BF16),
            pltpu.VMEM(wout.shape, BF16),
            pltpu.VMEM(wqkv.shape, BF16),
            dma((len(loaded),)),
            pltpu.VMEM((groups, length, PIECE), BF16),
            pltpu.VMEM((GROUP, length, PAIR), F32),
            pltpu.VMEM((GROUP, length, PAIR), F32),
            pltpu.VMEM((length, 1), jnp.int32),
            pltpu.VMEM((RING, 2, 2, 2, block, CHUNK), BF16),
            pltpu.VMEM((CORE_RING, 2, 2, block, CHUNK), BF16),
            pltpu.VMEM((LINK_RING, 2, block, CHUNK), BF16),
            pltpu.VMEM((LINK_RING, block, CHUNK), BF16),
            pltpu.VMEM((LINK_RING, block, CHUNK), BF16),
            pltpu.VMEM((LINK_RING, block, CHUNK), BF16),
        ] + [dma((chunks,))] * 10 + [
            pltpu.VMEM((8, 8, width), F32), pltpu.VMEM((4, 8, width), F32),
            pltpu.VMEM((8, 8, width), F32), pltpu.VMEM((4, 8, width), F32),
            dma((12,)), dma((12,)), dma((12,)), dma((12,)),
            pltpu.VMEM((1, width), F32), pltpu.VMEM((1, width), F32), pltpu.VMEM((1, 3 * width), F32),
        ],
        compiler_params=pltpu.CompilerParams(vmem_limit_bytes=60 * 2**20, collective_id=0, has_side_effects=True),
        name="back",
    )(count, segment, mlp, q, k, v, gc, x, base, t2, cosine, sine, g1, gain2, shift2, bup, bout, *loaded)


def finish_body(out_hbm, ig_hbm, total_ref, vec_ref, out_to, ig_to, up_ref, down_ref, low_ref, qkv_ref,
                gain1_ref, shift1_ref, bqkv_ref, bout_ref, gain2_ref, shift2_ref, bup_ref, bdown_ref, held, sem):
    takes = [pltpu.make_async_copy(a, held.at[j], sem.at[j]) for j, a in enumerate((out_hbm, ig_hbm))]
    copies = [pltpu.make_async_copy(held.at[j], a, sem.at[2 + j]) for j, a in enumerate((out_to, ig_to))]
    for take in takes:
        take.start()
    width, ff = gain1_ref.shape[0], bup_ref.shape[0]
    factor = 1.0 / vec_ref[0, 7:8, 0:1]
    groups = width // PIECE
    n_up = ff // CHUNK
    for take, copy in zip(takes, copies):
        take.wait()
        copy.start()
    for i in range(total_ref.shape[0]):
        grad = total_ref[i].astype(F32) * factor
        kind, *what = chunk_columns(i, 2 * n_up, 4 * groups, 2 * n_up // groups)
        if kind == "mlp":
            ref, j = (up_ref, what[0]) if what[0] < n_up else (down_ref, what[0] - n_up)
            ref[:, j * CHUNK : (j + 1) * CHUNK] = grad
            continue
        for e, s in enumerate(what):
            ref, col = (qkv_ref, (s % 3) * width + (s // 3) * PIECE) if s < 3 * groups else (low_ref, (s - 3 * groups) * PIECE)
            ref[:, col : col + PIECE] = grad[:, e * PIECE : (e + 1) * PIECE]
    first, second = vec_ref[0] * factor, vec_ref[1] * factor
    for j in range(ff // width):
        bup_ref[j * width : (j + 1) * width] = first[j]
    j = ff // width
    for ref, line in ((bout_ref, first[j]), (bdown_ref, first[j]), (gain2_ref, first[j + 1]), (shift2_ref, first[j + 2]),
                      (gain1_ref, second[0]), (shift1_ref, second[1])):
        ref[...] = line
    for j in range(3):
        bqkv_ref[j * width : (j + 1) * width] = second[2 + j]
    for copy in copies:
        copy.wait()


def finish(out, ig, total, vec, ff):
    length, width = out.shape
    block = total.shape[1]

    s = jax.ShapeDtypeStruct
    hbm, vmem = pl.BlockSpec(memory_space=pltpu.HBM), pl.BlockSpec(memory_space=pltpu.VMEM)
    vectors = (width, width, 3 * width, width, width, width, ff, width)
    return pl.pallas_call(
        finish_body,
        in_specs=[hbm, hbm, vmem, vmem],
        out_specs=[hbm, hbm] + [vmem] * 12,
        out_shape=[s(out.shape, BF16), s(ig.shape, BF16), s((block, ff), F32), s((block, ff), F32), s((block, width), F32),
                   s((block, 3 * width), F32)] + [s((n,), F32) for n in vectors],
        scratch_shapes=[pltpu.VMEM((2, length, width), BF16), pltpu.SemaphoreType.DMA((4,))],
        compiler_params=pltpu.CompilerParams(vmem_limit_bytes=60 * 2**20),
        name="finish",
    )(out, ig, total, vec)


def by_collectives(count, segment, mlp, q, k, v, gc, x, base, t2, cosine, sine, g1, gain2, shift2, bup, bout, n2t, glt, n1t, gl,
                   wout, wqkv):
    width, ff = x.shape[1], bup.shape[1]
    ctx, ctxt, gu = attention(q, k, v, gc, segment, cosine, sine)
    flat = jnp.concatenate([gu[0], gu[1], gu[2]], axis=1)
    low = jnp.concatenate(list(gl), axis=1)
    out = (base + nn(ctx, wout)).astype(BF16)
    grad_one = nt(flat, wqkv)
    x = x.astype(F32)
    centred = x - jnp.mean(x, axis=1, keepdims=True)
    r = lax.rsqrt(jnp.mean(centred * centred, axis=1, keepdims=True) + EPSILON)
    n = centred * r
    t = grad_one * g1 + t2
    dx = r * (t - jnp.mean(t, axis=1, keepdims=True) - n * jnp.mean(t * n, axis=1, keepdims=True))
    input_grad = (low.astype(F32) + dx).astype(BF16)
    packed = jnp.concatenate([bup[0], bout[0], gain2[0], shift2[0], jnp.full(width, count[0].astype(F32)),
                              jnp.sum(grad_one * n, axis=0), jnp.sum(grad_one, axis=0), jnp.sum(flat, axis=0, dtype=F32),
                              jnp.zeros(3 * width, F32)])
    packed = lax.psum(packed, ("dp", "rows"))
    mlp_part = jnp.concatenate([nn(n2t, mlp[:, :ff]), nn(glt, mlp[:, ff:])], axis=1)
    rest = [nn(n1t, gu[s % 3, :, (s // 3) * PIECE : (s // 3 + 1) * PIECE]) for s in range(3 * width // PIECE)]
    rest = jnp.concatenate(rest + [nn(ctxt, low)], axis=1)
    columns, n_mlp, pieces = [], 2 * ff // CHUNK, 4 * width // PIECE
    for i in range(n_mlp + pieces // 3 + pieces - 2 * (pieces // 3)):
        kind, *what = chunk_columns(i, n_mlp, pieces, n_mlp * PIECE // width)
        held = mlp_part if kind == "mlp" else rest
        begin, size = (what[0] * CHUNK, CHUNK) if kind == "mlp" else (what[0] * PIECE, len(what) * PIECE)
        columns.append(jnp.pad(held[:, begin : begin + size], ((0, 0), (0, CHUNK - size))))
    part = jnp.stack(columns, axis=1).astype(BF16)
    grads = lax.psum(lax.psum_scatter(part, "dp", scatter_dimension=0, tiled=True), "rows")
    return out, input_grad, jnp.swapaxes(grads, 0, 1), packed.reshape(2, 8, width)


def shards(tokens, segment_ids, true_counts, regroup, cotangent, ln1_gain, ln1_bias, qkv_weight, qkv_bias, out_weight,
           out_bias, ln2_gain, ln2_bias, up_weight, up_bias, down_weight, down_bias):
    length, width = cotangent.shape
    ff = up_weight.shape[1]
    cosine, sine = (jnp.asarray(t) for t in rotary_tables(length))
    (arrived, q, k, v, gc, n1t, n2t, glt, gl, mlp, base, t2, gain2, shift2, bias_up, bias_out) = front(
        true_counts, regroup, tokens, cotangent, cosine, sine, ln1_gain, ln1_bias, qkv_weight, qkv_bias, out_weight, out_bias,
        ln2_gain, ln2_bias, up_weight, up_bias, down_weight, down_bias)
    last = back if (lax.axis_size("dp"), lax.axis_size("rows")) == (8, 4) else by_collectives
    out, input_grad, total, vec = last(true_counts, segment_ids, mlp, q, k, v, gc, arrived, base, t2, cosine, sine, ln1_gain, gain2,
                                       shift2, bias_up, bias_out, n2t, glt, n1t, gl, out_weight, qkv_weight)
    (out, input_grad, up, down, low, qkv, gain1, shift1, bias_qkv, bias_out, gain2, shift2, bias_up, bias_down) = finish(
        out, input_grad, total, vec, up_weight.shape[1])
    return (out, input_grad, gain1, shift1, qkv, bias_qkv, low, bias_out, gain2, shift2, up, bias_up, down.T, bias_down)


def solution(mesh):
    both = ("dp", "rows")
    placed = (P(both, None), P(both), P(both), P(both), P(both, None)) + (P(),) * 12
    return jax.shard_map(
        shards, mesh=mesh, in_specs=placed,
        out_specs=(P(both, None), P(both, None), P(), P(), P("dp", None), P(), P("dp", None), P(), P(), P(), P("dp", None), P(),
                   P(None, "dp"), P()),
        check_vma=False)
```

```python
import functools
import numpy as np
import jax
import jax.numpy as jnp
from jax import lax
from jax.experimental import pallas as pl
from jax.experimental.pallas import tpu as pltpu
from jax.sharding import PartitionSpec as P

HEAD_DIM = 64
ROT = 16
PAIR = 128
CHUNK = 512
PIECE = 256
GROUP = 2
SPAN = 256
EPSILON = 1e-05
EXCLUDED = -1e30
F32 = jnp.float32
BF16 = jnp.bfloat16
MESH = pl.DeviceIdType.MESH


def remote(src, dst, send, recv, to):
    return pltpu.make_async_remote_copy(src_ref=src, dst_ref=dst, send_sem=send, recv_sem=recv, device_id=to, device_id_type=MESH)


def nn(a, b):
    return lax.dot_general(a, b, (((1,), (0,)), ((), ())), preferred_element_type=F32)


def nt(a, b):
    return lax.dot_general(a, b, (((1,), (1,)), ((), ())), preferred_element_type=F32)


def tn(a, b):
    return lax.dot_general(a, b, (((0,), (0,)), ((), ())), preferred_element_type=F32)


def rotary_tables(length):
    half = ROT // 2
    placed = np.arange(length, dtype=np.float32)
    rates = np.exp(np.arange(half, dtype=np.float32) * np.float32(-2.0 / ROT) * np.log(np.float32(10000.0)))
    phases = placed[:, None] * rates[None, :].astype(np.float32)
    cosine = np.ones((length, HEAD_DIM), np.float32)
    sine = np.zeros((length, HEAD_DIM), np.float32)
    cosine[:, :half] = np.cos(phases)
    cosine[:, half:ROT] = np.cos(phases)
    sine[:, :half] = -np.sin(phases)
    sine[:, half:ROT] = np.sin(phases)
    return np.tile(cosine, (1, PAIR // HEAD_DIM)), np.tile(sine, (1, PAIR // HEAD_DIM))


def turned(u):
    lane = lax.broadcasted_iota(jnp.int32, u.shape, 1) % HEAD_DIM
    half = ROT // 2
    return jnp.where(lane < half, pltpu.roll(u, PAIR - half, 1), pltpu.roll(u, half, 1))


def gelu_parts(h):
    e = jnp.exp(h * h * -0.5)
    t = 1.0 / (1.0 + 0.2316418882 * jnp.abs(h))
    poly = t * (0.127414796 + t * (-0.142248368 + t * (0.7107068705 + t * (-0.7265760135 + t * 0.5307027145))))
    tail = poly * e
    phi = jnp.where(h >= 0, 1.0 - tail, tail)
    return h * phi, phi + h * (e * 0.3989422804014327)


def attend(q, k, v, gc, begins, t_first):
    each, rows, span = range(len(q)), q[0].shape[0], k[0].shape[0]
    low = lax.broadcasted_iota(jnp.int32, (rows, PAIR), 1) < HEAD_DIM

    def both(t):
        zero = jnp.zeros_like(t)
        return jnp.concatenate([jnp.where(low, t, zero), jnp.where(low, zero, t)], axis=0)

    q2, g2 = [both(t) for t in q], [both(t) for t in gc]
    s_at = lax.broadcasted_iota(jnp.int32, (rows, span), 1)
    t_at = t_first + lax.broadcasted_iota(jnp.int32, (rows, span), 0)
    allowed = (s_at >= begins) & (s_at <= t_at)
    allowed = jnp.concatenate([allowed, allowed], axis=0)
    scores = [jnp.where(allowed, nt(q2[h], k[h]), EXCLUDED) for h in each]
    dp = [nt(g2[h], v[h]) for h in each]
    e = [jnp.exp(scores[h] - jnp.max(scores[h], axis=1, keepdims=True)) for h in each]
    p = [e[h] * (1.0 / jnp.sum(e[h], axis=1, keepdims=True)) for h in each]
    p16 = [p[h].astype(BF16) for h in each]
    c2 = [nn(p16[h], v[h]) for h in each]
    dv = [tn(p16[h], g2[h]) for h in each]
    w = [p[h] * dp[h] for h in each]
    ds16 = [(w[h] - p[h] * jnp.sum(w[h], axis=1, keepdims=True)).astype(BF16) for h in each]
    d2 = [nn(ds16[h], k[h]) for h in each]
    dk = [tn(ds16[h], q2[h]) for h in each]
    context = [jnp.where(low, c2[h][:rows], c2[h][rows:]).astype(BF16) for h in each]
    dq = [jnp.where(low, d2[h][:rows], d2[h][rows:]) * (HEAD_DIM ** -0.5) for h in each]
    return context, dq, dk, dv


def front_body(count_ref, want_ref, seg_ref, cos_ref, sin_ref, g1_vec, b1_vec, bqkv_vec, bout_vec, g2_vec, b2_vec,
               bup_vec, bdown_vec, own_hbm, cot_hbm, wqkv_hbm, wout_hbm, wup_hbm, wdown_hbm,
               x_ref, q_ref, k_ref, v_ref, gc_ref, n1t_ref, n2t_ref, glt_ref, gl_ref, mlp_ref, base_ref, t2_ref,
               gain2_ref, shift2_ref, bup_out, bout_out, begin_ref,
               wqkv_ref, wout_ref, wup_ref, wdown_ref, wants, from_near, from_half, to_inner, to_end,
               g1_ref, b1_ref, bqkv_ref, bout_ref, g2_ref, b2_ref, bup_ref, bdown_ref, own_ref, cot_ref, gl_all, ga_all, gc_all, w_sem, want_send, want_recv, near_send, near_recv, inner_send, end_send, half_recv, *, tile):
    step = pl.program_id(0)
    steps = pl.num_programs(0)
    length, width = cot_ref.shape
    rows = x_ref.shape[0]
    pairs = width // PAIR
    ff = wup_ref.shape[1]
    chunks = length // rows
    part = rows // 2
    parts = length // part
    d, z = lax.axis_index("dp"), lax.axis_index("rows")
    inner = (z + 1) // 2 % 2
    near = z + 1 - 2 * (z % 2)
    other_inner, other_end = 3 - z, 6 - 3 * z
    loads = [pltpu.make_async_copy(src, dst, w_sem.at[j]) for j, (src, dst) in enumerate(
        ((cot_hbm, cot_ref), (own_hbm, own_ref), (wdown_hbm, wdown_ref), (wout_hbm, wout_ref), (wqkv_hbm, wqkv_ref), (wup_hbm, wup_ref)))]

    def span(i):
        return pl.ds(pl.multiple_of(i * rows, rows), rows)

    def bit(i):
        return pl.ds(pl.multiple_of(i * part, part), part)

    def want_copy(j):
        to = lax.rem(z + j, 4)
        return remote(wants.at[0], wants.at[j], want_send.at[j], want_recv.at[j], (d, to))

    def near_copy(i):
        return remote(own_hbm.at[bit(i)], from_near.at[bit(i)], near_send.at[i], near_recv.at[i], (d, near))

    def inner_copy(i):
        return remote(to_inner.at[bit(i)], from_half.at[bit(i)], inner_send.at[i], half_recv.at[i], (d, other_inner))

    def end_copy(i):
        return remote(to_end.at[bit(i)], from_half.at[bit(i)], end_send.at[i], half_recv.at[i], (d, other_end))

    def wanted(by):
        return wants[lax.rem(z - by + 4, 4), 0:1, 0:1]

    def relay(i):
        @pl.when(inner == 1)
        def _():
            near_copy(i).wait_recv()
            mine = own_ref[bit(i), :].astype(F32)
            theirs = from_near[bit(i), :].astype(F32)
            to_end[bit(i), :] = jnp.where(wanted(other_end) == near, theirs, mine).astype(BF16)
            end_copy(i).start()
            to_inner[bit(i), :] = jnp.where(wanted(other_inner) == near, theirs, mine).astype(BF16)
            inner_copy(i).start()

    @pl.when(step == 0)
    def _():
        barrier = pltpu.get_barrier_semaphore()
        for j in (1, 2, 3):
            pl.semaphore_signal(barrier, inc=1, device_id=(d, lax.rem(z + j, 4)), device_id_type=MESH)
        for load in loads:
            load.start()
        wants[0] = jnp.full(wants.shape[1:], want_ref[0] % 4, jnp.int32)
        pl.semaphore_wait(barrier, 3)
        for j in (1, 2, 3):
            want_copy(j).start()

        def hand(i, carry):
            near_copy(i).start()
            return carry

        lax.fori_loop(0, parts, hand, 0)
        for vec, ref in ((g1_vec, g1_ref), (b1_vec, b1_ref), (bqkv_vec, bqkv_ref), (bout_vec, bout_ref), (g2_vec, g2_ref),
                         (b2_vec, b2_ref), (bup_vec, bup_ref), (bdown_vec, bdown_ref)):
            ref[...] = vec[...].reshape(1, -1)
        gain2_ref[...] = jnp.zeros_like(gain2_ref)
        shift2_ref[...] = jnp.zeros_like(shift2_ref)
        bup_out[...] = jnp.zeros_like(bup_out)
        loads[0].wait()
        place = lax.broadcasted_iota(jnp.int32, (length, 1), 0)
        masked = jnp.where(place < count_ref[0], cot_ref[...].astype(F32), 0.0)
        gl_all[...] = masked.astype(BF16)
        bout_out[...] = jnp.sum(masked, axis=0, keepdims=True)

        def active(f):
            ga_all[f] = nt(gl_all[...], wdown_ref[f * tile : (f + 1) * tile, :])

        tiles = ff // tile
        loads[1].wait()
        for j in (1, 2, 3):
            want_copy(j).wait()
        relay(0)
        relay(1)
        loads[2].wait()
        for f in range(tiles - 2):
            active(f)
        relay(2)
        relay(3)
        for f in range(tiles - 2, tiles):
            active(f)
        wide = jnp.broadcast_to(seg_ref[...].reshape(1, -1), (8, length)).astype(F32)
        tall = wide.T[:, :1]
        for b in range(0, length, PAIR):
            earlier = jnp.where(wide[:1] < tall[b : b + PAIR], 1.0, 0.0)
            begin_ref[b : b + PAIR, :] = jnp.sum(earlier, axis=1, keepdims=True).astype(jnp.int32)
        loads[3].wait()
        for p in range(pairs):
            gc_all[p] = nt(gl_all[...], wout_ref[p * PAIR : (p + 1) * PAIR, :]).astype(BF16)
        for load in loads[4:]:
            load.wait()

    @pl.when((step > 0) & (step + 1 < chunks))
    def _():
        relay(2 * step + 2)
        relay(2 * step + 3)

    gl16 = gl_all[span(step), :]
    for j in range(gl_ref.shape[0]):
        gl_ref[j] = gl16[:, j * PIECE : (j + 1) * PIECE]
    glt_ref[...] = gl16.T
    for p in range(pairs):
        gc_ref[p] = gc_all[p, span(step), :]

    @pl.when(inner == 0)
    def _():
        for j in range(2):
            near_copy(2 * step + j).wait_recv()

    for j in range(2):
        inner_copy(2 * step + j).wait_recv()
    source = wanted(z)
    x = jnp.where(source == near, from_near[span(step), :].astype(F32), from_half[span(step), :].astype(F32))
    x = jnp.where(source == z, own_ref[span(step), :].astype(F32), x)
    x_ref[...] = x.astype(BF16)
    centred = x - jnp.mean(x, axis=1, keepdims=True)
    r = lax.rsqrt(jnp.mean(centred * centred, axis=1, keepdims=True) + EPSILON)
    n = centred * r
    n1 = (n * g1_ref[...] + b1_ref[...]).astype(BF16)
    n2 = (n * g2_ref[...] + b2_ref[...]).astype(BF16)
    n1t_ref[...] = n1.T
    n2t_ref[...] = n2.T
    cosine, sine = cos_ref[...], sin_ref[...]
    for p in range(pairs):
        for which, ref in enumerate((q_ref, k_ref, v_ref)):
            wide = slice(which * width + p * PAIR, which * width + (p + 1) * PAIR)
            u = nn(n1, wqkv_ref[:, wide]) + bqkv_ref[:, wide]
            if which < 2:
                u = u * cosine + turned(u) * sine
            if which == 0:
                u = u * (HEAD_DIM ** -0.5)
            ref[p] = u.astype(BF16)
    mlp = x + (bdown_ref[...] + bout_ref[...])
    grad_two = jnp.zeros((rows, width), F32)
    for f in range(0, ff, tile):
        cols = slice(f, f + tile)
        h = nn(n2, wup_ref[:, cols]) + bup_ref[:, cols]
        ga = ga_all[f // tile, span(step), :]
        a, slope = gelu_parts(h)
        a16 = a.astype(BF16)
        gh = ga * slope
        gh16 = gh.astype(BF16)
        mlp_ref[:, cols] = gh16
        mlp_ref[:, ff + f : ff + f + tile] = a16
        bup_out[:, cols] += jnp.sum(gh16.astype(F32), axis=0, keepdims=True)
        mlp = mlp + nn(a16, wdown_ref[cols, :])
        grad_two = grad_two + nt(gh16, wup_ref[:, cols])
    base_ref[...] = mlp
    t2_ref[...] = grad_two * g2_ref[...]
    gain2_ref[...] += jnp.sum(grad_two * n, axis=0, keepdims=True)
    shift2_ref[...] += jnp.sum(grad_two, axis=0, keepdims=True)

    @pl.when(step == steps - 1)
    def _():
        def done(i, carry):
            near_copy(i).wait_send()

            @pl.when(inner == 1)
            def _():
                inner_copy(i).wait_send()
                end_copy(i).wait_send()
            return carry

        lax.fori_loop(0, parts, done, 0)


def front(count, want, segment, own, cot, cosine, sine, g1, b1, wqkv, bqkv, wout, bout, g2, b2, wup, bup, wdown, bdown, rows=128, tile=512):
    length, width = own.shape
    ff = wup.shape[1]
    pairs = width // PAIR
    chunks = length // rows

    def row(cols):
        return pl.BlockSpec((rows, cols), lambda i: (i, 0))

    def whole(a):
        return pl.BlockSpec(a.shape, lambda i: (0,) * a.ndim, pipeline_mode=pl.Buffered(1))

    heads = pl.BlockSpec((pairs, rows, PAIR), lambda i: (0, i, 0))
    down = pl.BlockSpec((width, rows), lambda i: (0, i))

    def vec(cols):
        return pl.BlockSpec((1, cols), lambda i: (0, 0))

    vectors = (g1, b1, bqkv, bout, g2, b2, bup, bdown)
    weights = (wqkv, wout, wup, wdown)
    s = jax.ShapeDtypeStruct
    dma = pltpu.SemaphoreType.DMA
    return pl.pallas_call(
        functools.partial(front_body, tile=tile),
        grid=(chunks,),
        in_specs=[pl.BlockSpec(memory_space=pltpu.SMEM), pl.BlockSpec(memory_space=pltpu.SMEM), whole(segment), row(PAIR), row(PAIR)]
        + [whole(a) for a in vectors] + [pl.BlockSpec(memory_space=pl.ANY)] * 6,
        out_specs=[row(width)] + [heads] * 4 + [down] * 3
        + [pl.BlockSpec((width // PIECE, rows, PIECE), lambda i: (0, i, 0)), row(2 * ff)] + [row(width)] * 2
        + [vec(width), vec(width), vec(ff), vec(width)] + [pl.BlockSpec((length, 1), lambda i: (0, 0))],
        out_shape=[s((length, width), BF16)] + [s((pairs, length, PAIR), BF16)] * 4 + [s((width, length), BF16)] * 3
        + [s((width // PIECE, length, PIECE), BF16), s((length, 2 * ff), BF16)]
        + [s((length, width), F32)] * 2 + [s((1, width), F32), s((1, width), F32), s((1, ff), F32), s((1, width), F32)] + [s((length, 1), jnp.int32)],
        scratch_shapes=[pltpu.VMEM(w.shape, BF16) for w in weights]
        + [pltpu.VMEM((4, 8, 128), jnp.int32)] + [pltpu.VMEM((length, width), BF16)] * 4
        + [pltpu.VMEM((1, v.shape[0]), F32) for v in vectors]
        + [pltpu.VMEM((length, width), BF16)] * 3 + [pltpu.VMEM((ff // tile, length, tile), F32), pltpu.VMEM((pairs, length, PAIR), BF16)]
        + [dma((6,)), dma((4,)), dma((4,))] + [dma((2 * chunks,))] * 5,
        compiler_params=pltpu.CompilerParams(vmem_limit_bytes=60 * 2**20, collective_id=1, has_side_effects=True),
        name="front",
    )(count, want, segment, cosine, sine, *vectors, own, cot, *weights)


def attention_body(q_ref, k_ref, v_ref, gc_ref, seg_ref, cos_ref, sin_ref,
                   ctx_ref, ctxt_ref, gu_ref, dk_acc, dv_acc, segc_ref, segr_ref, first_ref, *, rows):
    group, length, _ = q_ref.shape
    total = length // rows
    each = range(group)

    @pl.when(pl.program_id(0) == 0)
    def _():
        seg = seg_ref[...].reshape(1, -1)
        segr_ref[...] = seg
        segc_ref[...] = jnp.broadcast_to(seg, (8, length)).T[:, :1]
        wide = seg.astype(F32)
        for b in range(total):
            before = jnp.sum(jnp.where(wide < wide[:, b * rows : b * rows + 1], 1.0, 0.0))
            first_ref[b] = before.astype(jnp.int32) // rows

    lane = lax.broadcasted_iota(jnp.int32, (rows, PAIR), 1)
    low = lane < HEAD_DIM
    dk_acc[...] = jnp.zeros_like(dk_acc)
    dv_acc[...] = jnp.zeros_like(dv_acc)

    def both(ref, h, begin):
        t = ref[h, pl.ds(begin, rows), :]
        zero = jnp.zeros_like(t)
        return jnp.concatenate([jnp.where(low, t, zero), jnp.where(low, zero, t)], axis=0)

    def block(b, blocks):
        begin = pl.multiple_of(b * rows, rows)
        start = pl.multiple_of((b + 1 - blocks) * rows, rows)
        span = blocks * rows
        q2 = [both(q_ref, h, begin) for h in each]
        g2 = [both(gc_ref, h, begin) for h in each]
        k = [k_ref[h, pl.ds(start, span), :] for h in each]
        v = [v_ref[h, pl.ds(start, span), :] for h in each]
        segt = segc_ref[pl.ds(begin, rows), :]
        segs = segr_ref[:, pl.ds(start, span)]
        t_at = begin + lax.broadcasted_iota(jnp.int32, (rows, span), 0)
        s_at = start + lax.broadcasted_iota(jnp.int32, (rows, span), 1)
        allowed = (segt == segs) & (s_at <= t_at)
        allowed = jnp.concatenate([allowed, allowed], axis=0)
        scores = [jnp.where(allowed, nt(q2[h], k[h]), EXCLUDED) for h in each]
        dp = [nt(g2[h], v[h]) for h in each]
        e = [jnp.exp(scores[h] - jnp.max(scores[h], axis=1, keepdims=True)) for h in each]
        p = [e[h] * (1.0 / jnp.sum(e[h], axis=1, keepdims=True)) for h in each]
        p16 = [p[h].astype(BF16) for h in each]
        c2 = [nn(p16[h], v[h]) for h in each]
        for h in each:
            dv_acc[h, pl.ds(start, span), :] += tn(p16[h], g2[h])
        w = [p[h] * dp[h] for h in each]
        ds16 = [(w[h] - p[h] * jnp.sum(w[h], axis=1, keepdims=True)).astype(BF16) for h in each]
        d2 = [nn(ds16[h], k[h]) for h in each]
        for h in each:
            dk_acc[h, pl.ds(start, span), :] += tn(ds16[h], q2[h])
        cosine = cos_ref[pl.ds(begin, rows), :]
        sine = sin_ref[pl.ds(begin, rows), :]
        for h in each:
            cols = slice(h * PAIR, (h + 1) * PAIR)
            context = jnp.where(low, c2[h][:rows], c2[h][rows:]).astype(BF16)
            ctx_ref[pl.ds(begin, rows), cols] = context
            ctxt_ref[cols, pl.ds(begin, rows)] = context.T
            dq = jnp.where(low, d2[h][:rows], d2[h][rows:]) * (HEAD_DIM ** -0.5)
            gu_ref[0, pl.ds(begin, rows), cols] = (dq * cosine - turned(dq) * sine).astype(BF16)

    def loop(b, carry):
        count = b + 1 - first_ref[b]
        for blocks in range(1, total + 1):
            @pl.when(count == blocks)
            def _():
                block(b, blocks)
        return carry

    lax.fori_loop(0, total, loop, 0)
    for h in each:
        cols = slice(h * PAIR, (h + 1) * PAIR)
        dk = dk_acc[h]
        gu_ref[1, :, cols] = (dk * cos_ref[...] - turned(dk) * sin_ref[...]).astype(BF16)
        gu_ref[2, :, cols] = dv_acc[h].astype(BF16)


def attention(q, k, v, gc, segment, cosine, sine, rows=256, group=2):
    pairs, length, _ = q.shape
    head = pl.BlockSpec((group, length, PAIR), lambda h: (h, 0, 0))
    cols = pl.BlockSpec((length, group * PAIR), lambda h: (0, h))
    s = jax.ShapeDtypeStruct
    width = pairs * PAIR

    def whole(a):
        return pl.BlockSpec(a.shape, lambda h: (0,) * a.ndim, pipeline_mode=pl.Buffered(1))

    return pl.pallas_call(
        functools.partial(attention_body, rows=rows),
        grid=(pairs // group,),
        in_specs=[head] * 4 + [whole(segment), whole(cosine), whole(sine)],
        out_specs=[cols, pl.BlockSpec((group * PAIR, length), lambda h: (h, 0)),
                   pl.BlockSpec((3, length, group * PAIR), lambda h: (0, 0, h))],
        scratch_shapes=[pltpu.VMEM((group, length, PAIR), F32)] * 2
        + [pltpu.VMEM((length, 1), jnp.int32), pltpu.VMEM((1, length), jnp.int32), pltpu.SMEM((length // rows,), jnp.int32)],
        out_shape=[s((length, width), BF16), s((width, length), BF16), s((3, length, width), BF16)],
        compiler_params=pltpu.CompilerParams(vmem_limit_bytes=56 * 2**20),
        name="attention",
    )(q, k, v, gc, segment, cosine, sine)


class Line:
    def __init__(self):
        self.d = lax.axis_index("dp")
        self.z = lax.axis_index("rows")
        self.core = self.d % 2
        self.x = (self.d // 2) % 2
        self.y = self.d // 4
        self.over_core = (self.d + 1 - 2 * self.core, self.z)
        self.over_x = (self.d + 2 - 4 * self.x, self.z)
        self.over_y = (self.d + 4 - 8 * self.y, self.z)
        self.inner = (self.z + 1) // 2 % 2
        self.near = (self.d, self.z + 1 - 2 * (self.z % 2))
        self.far = (self.d, 3 - self.z)


class Everywhere:
    def __init__(self, at, of_dp, of_rows, send, recv):
        self.at, self.of_dp, self.of_rows, self.send, self.recv = at, of_dp, of_rows, send, recv
        self.devices, self.lines = of_dp.shape[0], of_rows.shape[0]

    def over_dp(self, j):
        at = self.at
        mine = self.of_dp.at[at.d]
        return remote(mine, mine, self.send.at[j], self.recv.at[j], (lax.rem(at.d + j, self.devices), at.z))

    def over_rows(self, j):
        at, sem = self.at, self.devices + j
        mine = self.of_rows.at[at.z]
        return remote(mine, mine, self.send.at[sem], self.recv.at[sem], (at.d, lax.rem(at.z + j, self.lines)))

    def begin(self, rows):
        self.of_dp[self.at.d] = jnp.concatenate(rows, axis=0)
        for j in range(1, self.devices):
            self.over_dp(j).start()

    def turn(self):
        for j in range(1, self.devices):
            self.over_dp(j).wait()
        total = self.of_dp[0]
        for j in range(1, self.devices):
            total = total + self.of_dp[j]
        self.of_rows[self.at.z] = total
        for j in range(1, self.lines):
            self.over_rows(j).start()

    def end(self):
        for j in range(1, self.lines):
            self.over_rows(j).wait()
        total = self.of_rows[0]
        for j in range(1, self.lines):
            total = total + self.of_rows[j]
        return total


LAGS = dict(core=1, first=3, second=5, z=7, mid=9, back=11)
RING, CORE_RING, LINK_RING = 7, 6, 8


def chunk_columns(i, n_mlp, pieces, per_group):
    period = per_group + 1
    busy = n_mlp // per_group * period
    if i < busy and i % period < per_group:
        return "mlp", per_group * (i // period) + i % period
    j = i // period if i < busy else i - n_mlp
    wide = pieces // 3
    return ("rest", 2 * j, 2 * j + 1) if j < wide else ("rest", j + wide)


def back_body(count_ref, begin_ref, mlp_ref, q_ref, k_ref, v_ref, gc_ref, x_ref, base_ref, t2_ref, cos_ref, sin_ref, g1_ref,
              gain2_ref, shift2_ref, bup_ref, bout_ref, n2t_hbm, glt_hbm, n1t_hbm, gl_hbm, wout_hbm, wqkv_hbm,
              out_ref, ig_ref, total_ref, vec_ref,
              left_mlp, left_rest, rhs, wout_ref, wqkv_ref, load_sem, ctx, dk_acc, dv_acc,
              part, from_core, from_first, from_second, from_near, from_far,
              c_send, c_recv, f_send, f_recv, s_send, s_recv, n_send, n_recv, m_send, m_recv,
              dp_e, rows_e, dp_l, rows_l, e_send, e_recv, l_send, l_recv, gain1, shift1, bqkv, *, rows, row_ticks):
    tick = pl.program_id(0)
    at = Line()
    chunks, block = total_ref.shape[0], total_ref.shape[1]
    length, width = begin_ref.shape[0], wout_ref.shape[0]
    groups = width // PIECE
    per_group = length // rows
    n_mlp, pieces = 2 * bup_ref.shape[1] // CHUNK, 4 * groups
    n_wide = n_mlp + pieces // 3
    period = per_group + 1
    busy = groups * period
    g, spot = jnp.minimum(tick // period, groups - 1), tick % period
    attending = (tick < busy) & (spot < per_group)
    first_need = (pltpu.make_async_copy(n2t_hbm, left_mlp.at[0], load_sem.at[0]),)
    later_need = [pltpu.make_async_copy(src, dst, load_sem.at[1 + j]) for j, (src, dst) in enumerate(
        ((glt_hbm, left_mlp.at[1]), (n1t_hbm, left_rest.at[0]), (gl_hbm, rhs.at[pl.ds(3 * groups, groups)]),
         (wout_hbm, wout_ref), (wqkv_hbm, wqkv_ref)))]

    @pl.when(tick == 0)
    def _():
        first_need[0].start()
        barrier = pltpu.get_barrier_semaphore()
        for j in range(1, 8):
            pl.semaphore_signal(barrier, inc=1, device_id=(lax.rem(at.d + j, 8), at.z), device_id_type=MESH)
        for j in range(1, 4):
            pl.semaphore_signal(barrier, inc=1, device_id=(at.d, lax.rem(at.z + j, 4)), device_id_type=MESH)
        pl.semaphore_wait(barrier, 10)
        for load in later_need:
            load.start()
        gain1[...] = jnp.zeros_like(gain1)
        shift1[...] = jnp.zeros_like(shift1)
        bqkv[...] = jnp.zeros_like(bqkv)
        first_need[0].wait()

    @pl.when(tick == 1)
    def _():
        for load in later_need:
            load.wait()

    def places(i):
        even = 1 - i % 2
        f = at.x * even + at.y * (1 - even)
        s = at.y * even + at.x * (1 - even)
        first = (at.d + even * (2 - 4 * at.x) + (1 - even) * (4 - 8 * at.y), at.z)
        second = (at.d + even * (4 - 8 * at.y) + (1 - even) * (2 - 4 * at.x), at.z)
        return f, s, first, second, i % RING

    def core_copy(i, w):
        lanes = pl.ds(0, w)
        return remote(part.at[i % RING, 1 - at.core, :, :, :, lanes], from_core.at[i % CORE_RING, :, :, :, lanes],
                      c_send.at[i], c_recv.at[i], at.over_core)

    def first_copy(i, w):
        f, s, first, second, slot = places(i)
        lanes = pl.ds(0, w)
        return remote(part.at[slot, at.core, 1 - f, :, :, lanes], from_first.at[i % LINK_RING, :, :, lanes],
                      f_send.at[i], f_recv.at[i], first)

    def second_copy(i, w):
        f, s, first, second, slot = places(i)
        lanes = pl.ds(0, w)
        return remote(part.at[slot, at.core, f, 1 - s, :, lanes], from_second.at[i % LINK_RING, :, lanes],
                      s_send.at[i], s_recv.at[i], second)

    def out_copy(i, w):
        lanes = pl.ds(0, w)
        return remote(total_ref.at[i, :, lanes], from_near.at[i % LINK_RING, :, lanes], n_send.at[i], n_recv.at[i], at.near)

    def far_copy(i, w):
        lanes = pl.ds(0, w)
        return remote(total_ref.at[i, :, lanes], from_far.at[i % LINK_RING, :, lanes], m_send.at[i], m_recv.at[i], at.far)

    def plus(a, b):
        return a + b

    def put(h, half, cols, rows_of):
        even = 1 - tick % 2
        for j in range(4):
            d = h * 4 + j
            c, x, y = d % 2, (d // 2) % 2, d // 4
            a = x * even + y * (1 - even)
            b = y * even + x * (1 - even)
            part[tick % RING, c, a, b, :, cols] = rows_of[j * block : (j + 1) * block].astype(BF16)

    half = width // 2

    @pl.when(attending)
    def _():
        left = (per_group * g + spot) // (n_mlp // 2)
        for h in range(2):
            put(h, half, slice(0, CHUNK), nn(left_mlp[left, h * half : (h + 1) * half, :], mlp_ref[...]))
        core_copy(tick, CHUNK).start()

    def rest(s, e):
        for h in range(2):
            put(h, half, slice(e * PIECE, (e + 1) * PIECE),
                nn(left_rest[s // (3 * groups), h * half : (h + 1) * half, :], rhs[s]))

    @pl.when((tick < n_wide) & jnp.logical_not(attending))
    def _():
        late = tick // busy
        j = (tick // period) * (1 - late) + (tick - n_mlp) * late
        for e in range(2):
            rest(2 * j + e, e)
        core_copy(tick, CHUNK).start()

    @pl.when((tick >= n_wide) & (tick < chunks))
    def _():
        rest(tick - n_wide + 2 * (n_wide - n_mlp), 0)
        core_copy(tick, PIECE).start()

    def when(lag, f):
        i = tick - lag

        @pl.when((i >= 0) & (i < n_wide))
        def _():
            f(i, CHUNK)

        @pl.when((i >= n_wide) & (i < chunks))
        def _():
            f(i, PIECE)

    def core_step(i, w):
        f, s, first, second, slot = places(i)
        core_copy(i, w).wait()
        for a in range(2):
            for b in range(2):
                part[slot, at.core, a, b, :, :w] = plus(part[slot, at.core, a, b, :, :w], from_core[i % CORE_RING, a, b, :, :w])
        first_copy(i, w).start()

    def first_step(i, w):
        f, s, first, second, slot = places(i)
        first_copy(i, w).wait()
        for b in range(2):
            part[slot, at.core, f, b, :, :w] = plus(part[slot, at.core, f, b, :, :w], from_first[i % LINK_RING, b, :, :w])
        second_copy(i, w).start()

    def second_step(i, w):
        f, s, first, second, slot = places(i)
        second_copy(i, w).wait()
        total_ref[i, :, :w] = plus(part[slot, at.core, f, s, :, :w], from_second[i % LINK_RING, :, :w])

        @pl.when(at.inner == 0)
        def _():
            out_copy(i, w).start()

    def near_step(i, w):
        @pl.when(at.inner == 1)
        def _():
            out_copy(i, w).wait_recv()
            total_ref[i, :, :w] = plus(total_ref[i, :, :w], from_near[i % LINK_RING, :, :w])
            far_copy(i, w).start()

    def far_step(i, w):
        @pl.when(at.inner == 1)
        def _():
            far_copy(i, w).wait()
            total_ref[i, :, :w] = plus(total_ref[i, :, :w], from_far[i % LINK_RING, :, :w])
            out_copy(i, w).start()

        @pl.when(at.inner == 0)
        def _():
            out_copy(i, w).wait_send()

    def back_step(i, w):
        @pl.when(at.inner == 0)
        def _():
            out_copy(i, w).wait_recv()
            total_ref[i, :, :w] = from_near[i % LINK_RING, :, :w]

        @pl.when(at.inner == 1)
        def _():
            out_copy(i, w).wait_send()

    when(LAGS["core"], core_step)
    when(LAGS["first"], first_step)
    when(LAGS["second"], second_step)
    when(LAGS["z"], near_step)
    when(LAGS["mid"], far_step)
    when(LAGS["back"], back_step)

    each = range(GROUP)

    def unit(b):
        span = (b + 1) * rows
        mine = slice(b * rows, span)
        context, dq, dk, dv = attend([q_ref[h, mine, :] for h in each], [k_ref[h, :span, :] for h in each],
                                     [v_ref[h, :span, :] for h in each], [gc_ref[h, mine, :] for h in each],
                                     begin_ref[mine, :], b * rows)
        for h in each:
            cols = slice(h * PAIR, (h + 1) * PAIR)
            dk_acc[h, :span, :] += dk[h]
            dv_acc[h, :span, :] += dv[h]
            ctx[g, mine, cols] = context[h]
            left_rest[1, pl.ds(pl.multiple_of(g * PIECE + h * PAIR, PAIR), PAIR), mine] = context[h].T
            rhs[3 * g, mine, cols] = (dq[h] * cos_ref[mine, :] - turned(dq[h]) * sin_ref[mine, :]).astype(BF16)

    @pl.when(attending & (spot == 0))
    def _():
        dk_acc[...] = jnp.zeros_like(dk_acc)
        dv_acc[...] = jnp.zeros_like(dv_acc)

    for b in range(per_group):
        @pl.when(attending & (spot == b))
        def _():
            unit(b)

    @pl.when(attending & (spot == per_group - 1))
    def _():
        for h in each:
            cols = slice(h * PAIR, (h + 1) * PAIR)
            dk = dk_acc[h]
            rhs[3 * g + 1, :, cols] = (dk * cos_ref[...] - turned(dk) * sin_ref[...]).astype(BF16)
            rhs[3 * g + 2, :, cols] = dv_acc[h].astype(BF16)

    row_at = chunks - 2

    @pl.when((tick >= row_at) & (tick < row_at + row_ticks))
    def _():
        n_rows = x_ref.shape[0]
        here = pl.ds(pl.multiple_of((tick - row_at) * n_rows, n_rows), n_rows)
        attn = base_ref[...]
        for j in range(groups):
            attn = attn + nn(ctx[j, here, :], wout_ref[j * PIECE : (j + 1) * PIECE, :])
        out_ref[...] = attn.astype(BF16)
        g1 = jnp.zeros(attn.shape, F32)
        for s in range(3 * groups):
            cols = slice((s % 3) * width + (s // 3) * PIECE, (s % 3) * width + (s // 3 + 1) * PIECE)
            grads = rhs[s, here, :]
            g1 = g1 + nt(grads, wqkv_ref[:, cols])
            bqkv[:, cols] += jnp.sum(grads.astype(F32), axis=0, keepdims=True)
        x = x_ref[...].astype(F32)
        centred = x - jnp.mean(x, axis=1, keepdims=True)
        r = lax.rsqrt(jnp.mean(centred * centred, axis=1, keepdims=True) + EPSILON)
        n = centred * r
        gain1[...] += jnp.sum(g1 * n, axis=0, keepdims=True)
        shift1[...] += jnp.sum(g1, axis=0, keepdims=True)
        t = g1 * g1_ref[...].reshape(1, -1) + t2_ref[...]
        dx = r * (t - jnp.mean(t, axis=1, keepdims=True) - n * jnp.mean(t * n, axis=1, keepdims=True))
        gl = jnp.concatenate([rhs[3 * groups + j, here, :] for j in range(groups)], axis=1)
        ig_ref[...] = (gl.astype(F32) + dx).astype(BF16)

    def lines(ref):
        return [ref[:, j : j + width] for j in range(0, ref.shape[1], width)]

    early = Everywhere(at, dp_e, rows_e, e_send, e_recv)
    late = Everywhere(at, dp_l, rows_l, l_send, l_recv)
    row = jnp.full((1, width), count_ref[0].astype(F32), F32)

    @pl.when(tick == 1)
    def _():
        early.begin(lines(bup_ref) + lines(bout_ref) + lines(gain2_ref) + lines(shift2_ref) + [row])

    @pl.when(tick == 4)
    def _():
        early.turn()

    @pl.when(tick == 7)
    def _():
        vec_ref[0] = early.end()

    begin = row_at + row_ticks

    @pl.when(tick == begin)
    def _():
        late.begin(lines(gain1) + lines(shift1) + lines(bqkv) + [jnp.zeros((3, width), F32)])

    @pl.when(tick == begin + 2)
    def _():
        late.turn()

    @pl.when(tick == begin + 4)
    def _():
        vec_ref[1] = late.end()


def back(count, begins, mlp, q, k, v, gc, x, base, t2, cosine, sine, g1, gain2, shift2, bup, bout, n2t, glt, n1t, gl, wout, wqkv,
         rows=256):
    length, width = x.shape
    ff = bup.shape[1]
    block = width // 8
    groups = width // PIECE
    n_mlp, pieces = 2 * ff // CHUNK, 4 * groups
    chunks = n_mlp + pieces // 3 + pieces - 2 * (pieces // 3)
    row_ticks = length // rows
    period = row_ticks + 1
    busy = groups * period
    ticks = max(chunks + LAGS["back"], chunks - 2 + row_ticks + 5)

    def row(cols):
        return pl.BlockSpec((rows, cols), lambda t: (jnp.clip(t - (chunks - 2), 0, row_ticks - 1), 0))

    def whole(a):
        return pl.BlockSpec(a.shape, lambda t: (0,) * a.ndim, pipeline_mode=pl.Buffered(1))

    def mlp_cols(t):
        return (0, jnp.minimum(row_ticks * (t // period) + jnp.minimum(t % period, row_ticks - 1), n_mlp - 1))

    heads = pl.BlockSpec((GROUP, length, PAIR), lambda t: (jnp.minimum(t // period, groups - 1), 0, 0))
    s = jax.ShapeDtypeStruct
    dma = pltpu.SemaphoreType.DMA
    loaded = (n2t, glt, n1t, gl, wout, wqkv)
    return pl.pallas_call(
        functools.partial(back_body, rows=rows, row_ticks=row_ticks),
        grid=(ticks,),
        in_specs=[pl.BlockSpec(memory_space=pltpu.SMEM), whole(begins), pl.BlockSpec((length, CHUNK), mlp_cols)]
        + [heads] * 4 + [row(width)] * 3
        + [whole(a) for a in (cosine, sine, g1, gain2, shift2, bup, bout)] + [pl.BlockSpec(memory_space=pl.ANY)] * len(loaded),
        out_specs=[row(width), row(width),
                   pl.BlockSpec((chunks, block, CHUNK), lambda t: (0, 0, 0), pipeline_mode=pl.Buffered(1)),
                   pl.BlockSpec((2, 8, width), lambda t: (0, 0, 0), pipeline_mode=pl.Buffered(1))],
        out_shape=[s((length, width), BF16), s((length, width), BF16), s((chunks, block, CHUNK), BF16), s((2, 8, width), F32)],
        scratch_shapes=[
            pltpu.VMEM((2, width, length), BF16),
            pltpu.VMEM((2, width, length), BF16),
            pltpu.VMEM((4 * groups, length, PIECE), BF16),
            pltpu.VMEM(wout.shape, BF16),
            pltpu.VMEM(wqkv.shape, BF16),
            dma((len(loaded),)),
            pltpu.VMEM((groups, length, PIECE), BF16),
            pltpu.VMEM((GROUP, length, PAIR), F32),
            pltpu.VMEM((GROUP, length, PAIR), F32),
            pltpu.VMEM((RING, 2, 2, 2, block, CHUNK), BF16),
            pltpu.VMEM((CORE_RING, 2, 2, block, CHUNK), BF16),
            pltpu.VMEM((LINK_RING, 2, block, CHUNK), BF16),
            pltpu.VMEM((LINK_RING, block, CHUNK), BF16),
            pltpu.VMEM((LINK_RING, block, CHUNK), BF16),
            pltpu.VMEM((LINK_RING, block, CHUNK), BF16),
        ] + [dma((chunks,))] * 10 + [
            pltpu.VMEM((8, 8, width), F32), pltpu.VMEM((4, 8, width), F32),
            pltpu.VMEM((8, 8, width), F32), pltpu.VMEM((4, 8, width), F32),
            dma((12,)), dma((12,)), dma((12,)), dma((12,)),
            pltpu.VMEM((1, width), F32), pltpu.VMEM((1, width), F32), pltpu.VMEM((1, 3 * width), F32),
        ],
        compiler_params=pltpu.CompilerParams(vmem_limit_bytes=60 * 2**20, collective_id=0, has_side_effects=True),
        name="back",
    )(count, begins, mlp, q, k, v, gc, x, base, t2, cosine, sine, g1, gain2, shift2, bup, bout, *loaded)


def finish_body(out_hbm, ig_hbm, total_hbm, vec_ref, out_to, ig_to, up_to, down_to, low_to, qkv_to,
                gain1_ref, shift1_ref, bqkv_ref, bout_ref, gain2_ref, shift2_ref, bup_ref, bdown_ref,
                held, total_ref, up_ref, down_ref, low_ref, qkv_ref, sem):
    load = pltpu.make_async_copy(total_hbm, total_ref, sem.at[0])
    load.start()
    takes = [pltpu.make_async_copy(a, held.at[j], sem.at[1 + j]) for j, a in enumerate((out_hbm, ig_hbm))]
    copies = [pltpu.make_async_copy(held.at[j], a, sem.at[3 + j]) for j, a in enumerate((out_to, ig_to))]
    for take in takes:
        take.start()
    width, ff = gain1_ref.shape[0], bup_ref.shape[0]
    factor = 1.0 / vec_ref[0, 7:8, 0:1]
    groups = width // PIECE
    n_up = ff // CHUNK
    load.wait()

    def put(kinds):
        for i in range(total_ref.shape[0]):
            kind, *what = chunk_columns(i, 2 * n_up, 4 * groups, 2 * n_up // groups)
            if kind not in kinds or (kind == "mlp" and what[0] // n_up != kinds[kind]):
                continue
            if kind == "mlp":
                ref, j = (up_ref, down_ref)[kinds[kind]], what[0] % n_up
                ref[:, j * CHUNK : (j + 1) * CHUNK] = total_ref[i].astype(F32) * factor
                continue
            for e, s in enumerate(what):
                ref, col = (qkv_ref, (s % 3) * width + (s // 3) * PIECE) if s < 3 * groups else (low_ref, (s - 3 * groups) * PIECE)
                ref[:, col : col + PIECE] = total_ref[i, :, e * PIECE : (e + 1) * PIECE].astype(F32) * factor

    results = []

    def send(ref, to):
        results.append(pltpu.make_async_copy(ref, to, sem.at[5 + len(results)]))
        results[-1].start()

    put({"mlp": 0})
    send(up_ref, up_to)
    for take, copy in zip(takes, copies):
        take.wait()
        copy.start()
    put({"mlp": 1})
    send(down_ref, down_to)
    put({"rest": 0})
    send(low_ref, low_to)
    send(qkv_ref, qkv_to)
    first, second = vec_ref[0] * factor, vec_ref[1] * factor
    for j in range(ff // width):
        bup_ref[j * width : (j + 1) * width] = first[j]
    j = ff // width
    for ref, line in ((bout_ref, first[j]), (bdown_ref, first[j]), (gain2_ref, first[j + 1]), (shift2_ref, first[j + 2]),
                      (gain1_ref, second[0]), (shift1_ref, second[1])):
        ref[...] = line
    for j in range(3):
        bqkv_ref[j * width : (j + 1) * width] = second[2 + j]
    for copy in copies + results:
        copy.wait()


def finish(out, ig, total, vec, ff):
    length, width = out.shape
    block = total.shape[1]
    s = jax.ShapeDtypeStruct
    hbm, vmem = pl.BlockSpec(memory_space=pltpu.HBM), pl.BlockSpec(memory_space=pltpu.VMEM)
    vectors = (width, width, 3 * width, width, width, width, ff, width)
    grads = [(block, ff), (block, ff), (block, width), (block, 3 * width)]
    return pl.pallas_call(
        finish_body,
        in_specs=[hbm, hbm, hbm, vmem],
        out_specs=[hbm] * 6 + [vmem] * 8,
        out_shape=[s(out.shape, BF16), s(ig.shape, BF16)] + [s(shape, F32) for shape in grads] + [s((n,), F32) for n in vectors],
        scratch_shapes=[pltpu.VMEM((2, length, width), BF16), pltpu.VMEM(total.shape, BF16)]
        + [pltpu.VMEM(shape, F32) for shape in grads] + [pltpu.SemaphoreType.DMA((9,))],
        compiler_params=pltpu.CompilerParams(vmem_limit_bytes=60 * 2**20),
        name="finish",
    )(out, ig, total, vec)


def by_collectives(segment, count, begins, mlp, q, k, v, gc, x, base, t2, cosine, sine, g1, gain2, shift2, bup, bout, n2t, glt, n1t, gl,
                   wout, wqkv):
    width, ff = x.shape[1], bup.shape[1]
    ctx, ctxt, gu = attention(q, k, v, gc, segment, cosine, sine)
    flat = jnp.concatenate([gu[0], gu[1], gu[2]], axis=1)
    low = jnp.concatenate(list(gl), axis=1)
    out = (base + nn(ctx, wout)).astype(BF16)
    grad_one = nt(flat, wqkv)
    x = x.astype(F32)
    centred = x - jnp.mean(x, axis=1, keepdims=True)
    r = lax.rsqrt(jnp.mean(centred * centred, axis=1, keepdims=True) + EPSILON)
    n = centred * r
    t = grad_one * g1 + t2
    dx = r * (t - jnp.mean(t, axis=1, keepdims=True) - n * jnp.mean(t * n, axis=1, keepdims=True))
    input_grad = (low.astype(F32) + dx).astype(BF16)
    packed = jnp.concatenate([bup[0], bout[0], gain2[0], shift2[0], jnp.full(width, count[0].astype(F32)),
                              jnp.sum(grad_one * n, axis=0), jnp.sum(grad_one, axis=0), jnp.sum(flat, axis=0, dtype=F32),
                              jnp.zeros(3 * width, F32)])
    packed = lax.psum(packed, ("dp", "rows"))
    mlp_part = jnp.concatenate([nn(n2t, mlp[:, :ff]), nn(glt, mlp[:, ff:])], axis=1)
    rest = [nn(n1t, gu[s % 3, :, (s // 3) * PIECE : (s // 3 + 1) * PIECE]) for s in range(3 * width // PIECE)]
    rest = jnp.concatenate(rest + [nn(ctxt, low)], axis=1)
    columns, n_mlp, pieces = [], 2 * ff // CHUNK, 4 * width // PIECE
    for i in range(n_mlp + pieces // 3 + pieces - 2 * (pieces // 3)):
        kind, *what = chunk_columns(i, n_mlp, pieces, n_mlp * PIECE // width)
        held = mlp_part if kind == "mlp" else rest
        begin, size = (what[0] * CHUNK, CHUNK) if kind == "mlp" else (what[0] * PIECE, len(what) * PIECE)
        columns.append(jnp.pad(held[:, begin : begin + size], ((0, 0), (0, CHUNK - size))))
    part = jnp.stack(columns, axis=1).astype(BF16)
    grads = lax.psum(lax.psum_scatter(part, "dp", scatter_dimension=0, tiled=True), "rows")
    return out, input_grad, jnp.swapaxes(grads, 0, 1), packed.reshape(2, 8, width)


def shards(tokens, segment_ids, true_counts, regroup, cotangent, ln1_gain, ln1_bias, qkv_weight, qkv_bias, out_weight,
           out_bias, ln2_gain, ln2_bias, up_weight, up_bias, down_weight, down_bias):
    length, width = cotangent.shape
    ff = up_weight.shape[1]
    cosine, sine = (jnp.asarray(t) for t in rotary_tables(length))
    (arrived, q, k, v, gc, n1t, n2t, glt, gl, mlp, base, t2, gain2, shift2, bias_up, bias_out, begins) = front(
        true_counts, regroup, segment_ids, tokens, cotangent, cosine, sine, ln1_gain, ln1_bias, qkv_weight, qkv_bias, out_weight, out_bias,
        ln2_gain, ln2_bias, up_weight, up_bias, down_weight, down_bias)
    last = back if (lax.axis_size("dp"), lax.axis_size("rows")) == (8, 4) else functools.partial(by_collectives, segment_ids)
    out, input_grad, total, vec = last(true_counts, begins, mlp, q, k, v, gc, arrived, base, t2, cosine, sine, ln1_gain, gain2,
                                       shift2, bias_up, bias_out, n2t, glt, n1t, gl, out_weight, qkv_weight)
    (out, input_grad, up, down, low, qkv, gain1, shift1, bias_qkv, bias_out, gain2, shift2, bias_up, bias_down) = finish(
        out, input_grad, total, vec, up_weight.shape[1])
    return (out, input_grad, gain1, shift1, qkv, bias_qkv, low, bias_out, gain2, shift2, up, bias_up, down.T, bias_down)


def solution(mesh):
    both = ("dp", "rows")
    placed = (P(both, None), P(both), P(both), P(both), P(both, None)) + (P(),) * 12
    return jax.shard_map(
        shards, mesh=mesh, in_specs=placed,
        out_specs=(P(both, None), P(both, None), P(), P(), P("dp", None), P(), P("dp", None), P(), P(), P(), P("dp", None), P(),
                   P(None, "dp"), P()),
        check_vma=False)
```

```python
import functools
import numpy as np
import jax
import jax.numpy as jnp
from jax import lax
from jax.experimental import pallas as pl
from jax.experimental.pallas import tpu as pltpu
from jax.sharding import PartitionSpec as P

HEAD_DIM = 64
ROT = 16
PAIR = 128
CHUNK = 512
PIECE = 256
GROUP = 2
SPAN = 256
EPSILON = 1e-05
EXCLUDED = -1e30
F32 = jnp.float32
BF16 = jnp.bfloat16
MESH = pl.DeviceIdType.MESH


def remote(src, dst, send, recv, to):
    return pltpu.make_async_remote_copy(src_ref=src, dst_ref=dst, send_sem=send, recv_sem=recv, device_id=to, device_id_type=MESH)


def nn(a, b):
    return lax.dot_general(a, b, (((1,), (0,)), ((), ())), preferred_element_type=F32)


def nt(a, b):
    return lax.dot_general(a, b, (((1,), (1,)), ((), ())), preferred_element_type=F32)


def tn(a, b):
    return lax.dot_general(a, b, (((0,), (0,)), ((), ())), preferred_element_type=F32)


def rotary_tables(length):
    half = ROT // 2
    placed = np.arange(length, dtype=np.float32)
    rates = np.exp(np.arange(half, dtype=np.float32) * np.float32(-2.0 / ROT) * np.log(np.float32(10000.0)))
    phases = placed[:, None] * rates[None, :].astype(np.float32)
    cosine = np.ones((length, HEAD_DIM), np.float32)
    sine = np.zeros((length, HEAD_DIM), np.float32)
    cosine[:, :half] = np.cos(phases)
    cosine[:, half:ROT] = np.cos(phases)
    sine[:, :half] = -np.sin(phases)
    sine[:, half:ROT] = np.sin(phases)
    return np.tile(cosine, (1, PAIR // HEAD_DIM)), np.tile(sine, (1, PAIR // HEAD_DIM))


def turned(u):
    lane = lax.broadcasted_iota(jnp.int32, u.shape, 1) % HEAD_DIM
    half = ROT // 2
    return jnp.where(lane < half, pltpu.roll(u, PAIR - half, 1), pltpu.roll(u, half, 1))


def gelu_parts(h):
    e = jnp.exp(h * h * -0.5)
    t = 1.0 / (1.0 + 0.2316418882 * jnp.abs(h))
    poly = t * (0.127414796 + t * (-0.142248368 + t * (0.7107068705 + t * (-0.7265760135 + t * 0.5307027145))))
    tail = poly * e
    phi = jnp.where(h >= 0, 1.0 - tail, tail)
    return h * phi, phi + h * (e * 0.3989422804014327)


def attend(q, k, v, gc, begins, t_first):
    each, rows = range(len(q)), q[0].shape[0]
    low = lax.broadcasted_iota(jnp.int32, (rows, PAIR), 1) < HEAD_DIM

    def both(t):
        zero = jnp.zeros_like(t)
        return jnp.concatenate([jnp.where(low, t, zero), jnp.where(low, zero, t)], axis=0)

    def allowed(h):
        span = k[h].shape[0]
        s_at = lax.broadcasted_iota(jnp.int32, (rows, span), 1)
        t_at = t_first[h] + lax.broadcasted_iota(jnp.int32, (rows, span), 0)
        seen = (s_at >= begins[h]) & (s_at <= t_at)
        return jnp.concatenate([seen, seen], axis=0)

    seen = {t_first[h]: allowed(h) for h in each}
    q2, g2 = [both(t) for t in q], [both(t) for t in gc]
    scores = [jnp.where(seen[t_first[h]], nt(q2[h], k[h]), EXCLUDED) for h in each]
    dp = [nt(g2[h], v[h]) for h in each]
    e = [jnp.exp(scores[h] - jnp.max(scores[h], axis=1, keepdims=True)) for h in each]
    p = [e[h] * (1.0 / jnp.sum(e[h], axis=1, keepdims=True)) for h in each]
    p16 = [p[h].astype(BF16) for h in each]
    c2 = [nn(p16[h], v[h]) for h in each]
    dv = [tn(p16[h], g2[h]) for h in each]
    w = [p[h] * dp[h] for h in each]
    ds16 = [(w[h] - p[h] * jnp.sum(w[h], axis=1, keepdims=True)).astype(BF16) for h in each]
    d2 = [nn(ds16[h], k[h]) for h in each]
    dk = [tn(ds16[h], q2[h]) for h in each]
    context = [jnp.where(low, c2[h][:rows], c2[h][rows:]).astype(BF16) for h in each]
    dq = [jnp.where(low, d2[h][:rows], d2[h][rows:]) * (HEAD_DIM ** -0.5) for h in each]
    return context, dq, dk, dv


def front_body(count_ref, want_ref, seg_ref, cos_ref, sin_ref, g1_vec, b1_vec, bqkv_vec, bout_vec, g2_vec, b2_vec,
               bup_vec, bdown_vec, own_hbm, cot_hbm, wqkv_hbm, wout_hbm, wup_hbm, wdown_hbm,
               x_ref, q_ref, k_ref, v_ref, gc_ref, n1t_ref, n2t_ref, glt_ref, gl_ref, mlp_ref, base_ref, t2_ref,
               gain2_ref, shift2_ref, bup_out, bout_out, begin_ref,
               wqkv_ref, wout_ref, wup_ref, wdown_ref, wants, from_near, from_half, to_inner, to_end,
               g1_ref, b1_ref, bqkv_ref, bout_ref, g2_ref, b2_ref, bup_ref, bdown_ref, own_ref, cot_ref, gl_all, ga_all, gc_all, w_sem, want_send, want_recv, near_send, near_recv, inner_send, end_send, half_recv, *, tile):
    step = pl.program_id(0)
    steps = pl.num_programs(0)
    length, width = cot_ref.shape
    rows = x_ref.shape[0]
    pairs = width // PAIR
    ff = wup_ref.shape[1]
    chunks = length // rows
    part = rows // 2
    parts = length // part
    d, z = lax.axis_index("dp"), lax.axis_index("rows")
    inner = (z + 1) // 2 % 2
    near = z + 1 - 2 * (z % 2)
    other_inner, other_end = 3 - z, 6 - 3 * z
    loads = [pltpu.make_async_copy(src, dst, w_sem.at[j]) for j, (src, dst) in enumerate(
        ((cot_hbm, cot_ref), (own_hbm, own_ref), (wdown_hbm, wdown_ref), (wout_hbm, wout_ref), (wqkv_hbm, wqkv_ref), (wup_hbm, wup_ref)))]

    def span(i):
        return pl.ds(pl.multiple_of(i * rows, rows), rows)

    def bit(i):
        return pl.ds(pl.multiple_of(i * part, part), part)

    def want_copy(j):
        to = lax.rem(z + j, 4)
        return remote(wants.at[0], wants.at[j], want_send.at[j], want_recv.at[j], (d, to))

    def near_copy(i):
        return remote(own_hbm.at[bit(i)], from_near.at[bit(i)], near_send.at[i], near_recv.at[i], (d, near))

    def inner_copy(i):
        return remote(to_inner.at[bit(i)], from_half.at[bit(i)], inner_send.at[i], half_recv.at[i], (d, other_inner))

    def end_copy(i):
        return remote(to_end.at[bit(i)], from_half.at[bit(i)], end_send.at[i], half_recv.at[i], (d, other_end))

    def wanted(by):
        return wants[lax.rem(z - by + 4, 4), 0:1, 0:1]

    def relay(i):
        @pl.when(inner == 1)
        def _():
            near_copy(i).wait_recv()
            mine = own_ref[bit(i), :].astype(F32)
            theirs = from_near[bit(i), :].astype(F32)
            to_end[bit(i), :] = jnp.where(wanted(other_end) == near, theirs, mine).astype(BF16)
            end_copy(i).start()
            to_inner[bit(i), :] = jnp.where(wanted(other_inner) == near, theirs, mine).astype(BF16)
            inner_copy(i).start()

    @pl.when(step == 0)
    def _():
        barrier = pltpu.get_barrier_semaphore()
        for j in (1, 2, 3):
            pl.semaphore_signal(barrier, inc=1, device_id=(d, lax.rem(z + j, 4)), device_id_type=MESH)
        for load in loads:
            load.start()
        wants[0] = jnp.full(wants.shape[1:], want_ref[0] % 4, jnp.int32)
        pl.semaphore_wait(barrier, 3)
        for j in (1, 2, 3):
            want_copy(j).start()

        def hand(i, carry):
            near_copy(i).start()
            return carry

        lax.fori_loop(0, parts, hand, 0)
        for vec, ref in ((g1_vec, g1_ref), (b1_vec, b1_ref), (bqkv_vec, bqkv_ref), (bout_vec, bout_ref), (g2_vec, g2_ref),
                         (b2_vec, b2_ref), (bup_vec, bup_ref), (bdown_vec, bdown_ref)):
            ref[...] = vec[...].reshape(1, -1)
        gain2_ref[...] = jnp.zeros_like(gain2_ref)
        shift2_ref[...] = jnp.zeros_like(shift2_ref)
        bup_out[...] = jnp.zeros_like(bup_out)
        loads[0].wait()
        place = lax.broadcasted_iota(jnp.int32, (length, 1), 0)
        masked = jnp.where(place < count_ref[0], cot_ref[...].astype(F32), 0.0)
        gl_all[...] = masked.astype(BF16)
        bout_out[...] = jnp.sum(masked, axis=0, keepdims=True)

        def active(f):
            ga_all[f] = nt(gl_all[...], wdown_ref[f * tile : (f + 1) * tile, :])

        tiles = ff // tile
        loads[1].wait()
        for j in (1, 2, 3):
            want_copy(j).wait()
        relay(0)
        relay(1)
        loads[2].wait()
        for f in range(tiles - 2):
            active(f)
        relay(2)
        relay(3)
        for f in range(tiles - 2, tiles):
            active(f)
        wide = jnp.broadcast_to(seg_ref[...].reshape(1, -1), (8, length)).astype(F32)
        tall = wide.T[:, :1]
        for b in range(0, length, PAIR):
            earlier = jnp.where(wide[:1] < tall[b : b + PAIR], 1.0, 0.0)
            begin_ref[b : b + PAIR, :] = jnp.sum(earlier, axis=1, keepdims=True).astype(jnp.int32)
        loads[3].wait()
        for p in range(pairs):
            gc_all[p] = nt(gl_all[...], wout_ref[p * PAIR : (p + 1) * PAIR, :]).astype(BF16)
        for load in loads[4:]:
            load.wait()

    @pl.when((step > 0) & (step + 1 < chunks))
    def _():
        relay(2 * step + 2)
        relay(2 * step + 3)

    gl16 = gl_all[span(step), :]
    for j in range(gl_ref.shape[0]):
        gl_ref[j] = gl16[:, j * PIECE : (j + 1) * PIECE]
    glt_ref[...] = gl16.T
    for p in range(pairs):
        gc_ref[p] = gc_all[p, span(step), :]

    @pl.when(inner == 0)
    def _():
        for j in range(2):
            near_copy(2 * step + j).wait_recv()

    for j in range(2):
        inner_copy(2 * step + j).wait_recv()
    source = wanted(z)
    x = jnp.where(source == near, from_near[span(step), :].astype(F32), from_half[span(step), :].astype(F32))
    x = jnp.where(source == z, own_ref[span(step), :].astype(F32), x)
    x_ref[...] = x.astype(BF16)
    centred = x - jnp.mean(x, axis=1, keepdims=True)
    r = lax.rsqrt(jnp.mean(centred * centred, axis=1, keepdims=True) + EPSILON)
    n = centred * r
    n1 = (n * g1_ref[...] + b1_ref[...]).astype(BF16)
    n2 = (n * g2_ref[...] + b2_ref[...]).astype(BF16)
    n1t_ref[...] = n1.T
    n2t_ref[...] = n2.T
    cosine, sine = cos_ref[...], sin_ref[...]
    for p in range(pairs):
        for which, ref in enumerate((q_ref, k_ref, v_ref)):
            wide = slice(which * width + p * PAIR, which * width + (p + 1) * PAIR)
            u = nn(n1, wqkv_ref[:, wide]) + bqkv_ref[:, wide]
            if which < 2:
                u = u * cosine + turned(u) * sine
            if which == 0:
                u = u * (HEAD_DIM ** -0.5)
            ref[p] = u.astype(BF16)
    mlp = x + (bdown_ref[...] + bout_ref[...])
    grad_two = jnp.zeros((rows, width), F32)
    for f in range(0, ff, tile):
        cols = slice(f, f + tile)
        h = nn(n2, wup_ref[:, cols]) + bup_ref[:, cols]
        ga = ga_all[f // tile, span(step), :]
        a, slope = gelu_parts(h)
        a16 = a.astype(BF16)
        gh = ga * slope
        gh16 = gh.astype(BF16)
        mlp_ref[:, cols] = gh16
        mlp_ref[:, ff + f : ff + f + tile] = a16
        bup_out[:, cols] += jnp.sum(gh16.astype(F32), axis=0, keepdims=True)
        mlp = mlp + nn(a16, wdown_ref[cols, :])
        grad_two = grad_two + nt(gh16, wup_ref[:, cols])
    base_ref[...] = mlp
    t2_ref[...] = grad_two * g2_ref[...]
    gain2_ref[...] += jnp.sum(grad_two * n, axis=0, keepdims=True)
    shift2_ref[...] += jnp.sum(grad_two, axis=0, keepdims=True)

    @pl.when(step == steps - 1)
    def _():
        def done(i, carry):
            near_copy(i).wait_send()

            @pl.when(inner == 1)
            def _():
                inner_copy(i).wait_send()
                end_copy(i).wait_send()
            return carry

        lax.fori_loop(0, parts, done, 0)


def front(count, want, segment, own, cot, cosine, sine, g1, b1, wqkv, bqkv, wout, bout, g2, b2, wup, bup, wdown, bdown, rows=128, tile=512):
    length, width = own.shape
    ff = wup.shape[1]
    pairs = width // PAIR
    chunks = length // rows

    def row(cols):
        return pl.BlockSpec((rows, cols), lambda i: (i, 0))

    def whole(a):
        return pl.BlockSpec(a.shape, lambda i: (0,) * a.ndim, pipeline_mode=pl.Buffered(1))

    heads = pl.BlockSpec((pairs, rows, PAIR), lambda i: (0, i, 0))
    down = pl.BlockSpec((width, rows), lambda i: (0, i))

    def vec(cols):
        return pl.BlockSpec((1, cols), lambda i: (0, 0))

    vectors = (g1, b1, bqkv, bout, g2, b2, bup, bdown)
    weights = (wqkv, wout, wup, wdown)
    s = jax.ShapeDtypeStruct
    dma = pltpu.SemaphoreType.DMA
    return pl.pallas_call(
        functools.partial(front_body, tile=tile),
        grid=(chunks,),
        in_specs=[pl.BlockSpec(memory_space=pltpu.SMEM), pl.BlockSpec(memory_space=pltpu.SMEM), whole(segment), row(PAIR), row(PAIR)]
        + [whole(a) for a in vectors] + [pl.BlockSpec(memory_space=pl.ANY)] * 6,
        out_specs=[row(width)] + [heads] * 4 + [down] * 3
        + [pl.BlockSpec((width // PIECE, rows, PIECE), lambda i: (0, i, 0)), row(2 * ff)] + [row(width)] * 2
        + [vec(width), vec(width), vec(ff), vec(width)] + [pl.BlockSpec((length, 1), lambda i: (0, 0))],
        out_shape=[s((length, width), BF16)] + [s((pairs, length, PAIR), BF16)] * 4 + [s((width, length), BF16)] * 3
        + [s((width // PIECE, length, PIECE), BF16), s((length, 2 * ff), BF16)]
        + [s((length, width), F32)] * 2 + [s((1, width), F32), s((1, width), F32), s((1, ff), F32), s((1, width), F32)] + [s((length, 1), jnp.int32)],
        scratch_shapes=[pltpu.VMEM(w.shape, BF16) for w in weights]
        + [pltpu.VMEM((4, 8, 128), jnp.int32)] + [pltpu.VMEM((length, width), BF16)] * 4
        + [pltpu.VMEM((1, v.shape[0]), F32) for v in vectors]
        + [pltpu.VMEM((length, width), BF16)] * 3 + [pltpu.VMEM((ff // tile, length, tile), F32), pltpu.VMEM((pairs, length, PAIR), BF16)]
        + [dma((6,)), dma((4,)), dma((4,))] + [dma((2 * chunks,))] * 5,
        compiler_params=pltpu.CompilerParams(vmem_limit_bytes=60 * 2**20, collective_id=1, has_side_effects=True),
        name="front",
    )(count, want, segment, cosine, sine, *vectors, own, cot, *weights)


def attention_body(q_ref, k_ref, v_ref, gc_ref, seg_ref, cos_ref, sin_ref,
                   ctx_ref, ctxt_ref, gu_ref, dk_acc, dv_acc, segc_ref, segr_ref, first_ref, *, rows):
    group, length, _ = q_ref.shape
    total = length // rows
    each = range(group)

    @pl.when(pl.program_id(0) == 0)
    def _():
        seg = seg_ref[...].reshape(1, -1)
        segr_ref[...] = seg
        segc_ref[...] = jnp.broadcast_to(seg, (8, length)).T[:, :1]
        wide = seg.astype(F32)
        for b in range(total):
            before = jnp.sum(jnp.where(wide < wide[:, b * rows : b * rows + 1], 1.0, 0.0))
            first_ref[b] = before.astype(jnp.int32) // rows

    lane = lax.broadcasted_iota(jnp.int32, (rows, PAIR), 1)
    low = lane < HEAD_DIM
    dk_acc[...] = jnp.zeros_like(dk_acc)
    dv_acc[...] = jnp.zeros_like(dv_acc)

    def both(ref, h, begin):
        t = ref[h, pl.ds(begin, rows), :]
        zero = jnp.zeros_like(t)
        return jnp.concatenate([jnp.where(low, t, zero), jnp.where(low, zero, t)], axis=0)

    def block(b, blocks):
        begin = pl.multiple_of(b * rows, rows)
        start = pl.multiple_of((b + 1 - blocks) * rows, rows)
        span = blocks * rows
        q2 = [both(q_ref, h, begin) for h in each]
        g2 = [both(gc_ref, h, begin) for h in each]
        k = [k_ref[h, pl.ds(start, span), :] for h in each]
        v = [v_ref[h, pl.ds(start, span), :] for h in each]
        segt = segc_ref[pl.ds(begin, rows), :]
        segs = segr_ref[:, pl.ds(start, span)]
        t_at = begin + lax.broadcasted_iota(jnp.int32, (rows, span), 0)
        s_at = start + lax.broadcasted_iota(jnp.int32, (rows, span), 1)
        allowed = (segt == segs) & (s_at <= t_at)
        allowed = jnp.concatenate([allowed, allowed], axis=0)
        scores = [jnp.where(allowed, nt(q2[h], k[h]), EXCLUDED) for h in each]
        dp = [nt(g2[h], v[h]) for h in each]
        e = [jnp.exp(scores[h] - jnp.max(scores[h], axis=1, keepdims=True)) for h in each]
        p = [e[h] * (1.0 / jnp.sum(e[h], axis=1, keepdims=True)) for h in each]
        p16 = [p[h].astype(BF16) for h in each]
        c2 = [nn(p16[h], v[h]) for h in each]
        for h in each:
            dv_acc[h, pl.ds(start, span), :] += tn(p16[h], g2[h])
        w = [p[h] * dp[h] for h in each]
        ds16 = [(w[h] - p[h] * jnp.sum(w[h], axis=1, keepdims=True)).astype(BF16) for h in each]
        d2 = [nn(ds16[h], k[h]) for h in each]
        for h in each:
            dk_acc[h, pl.ds(start, span), :] += tn(ds16[h], q2[h])
        cosine = cos_ref[pl.ds(begin, rows), :]
        sine = sin_ref[pl.ds(begin, rows), :]
        for h in each:
            cols = slice(h * PAIR, (h + 1) * PAIR)
            context = jnp.where(low, c2[h][:rows], c2[h][rows:]).astype(BF16)
            ctx_ref[pl.ds(begin, rows), cols] = context
            ctxt_ref[cols, pl.ds(begin, rows)] = context.T
            dq = jnp.where(low, d2[h][:rows], d2[h][rows:]) * (HEAD_DIM ** -0.5)
            gu_ref[0, pl.ds(begin, rows), cols] = (dq * cosine - turned(dq) * sine).astype(BF16)

    def loop(b, carry):
        count = b + 1 - first_ref[b]
        for blocks in range(1, total + 1):
            @pl.when(count == blocks)
            def _():
                block(b, blocks)
        return carry

    lax.fori_loop(0, total, loop, 0)
    for h in each:
        cols = slice(h * PAIR, (h + 1) * PAIR)
        dk = dk_acc[h]
        gu_ref[1, :, cols] = (dk * cos_ref[...] - turned(dk) * sin_ref[...]).astype(BF16)
        gu_ref[2, :, cols] = dv_acc[h].astype(BF16)


def attention(q, k, v, gc, segment, cosine, sine, rows=256, group=2):
    pairs, length, _ = q.shape
    head = pl.BlockSpec((group, length, PAIR), lambda h: (h, 0, 0))
    cols = pl.BlockSpec((length, group * PAIR), lambda h: (0, h))
    s = jax.ShapeDtypeStruct
    width = pairs * PAIR

    def whole(a):
        return pl.BlockSpec(a.shape, lambda h: (0,) * a.ndim, pipeline_mode=pl.Buffered(1))

    return pl.pallas_call(
        functools.partial(attention_body, rows=rows),
        grid=(pairs // group,),
        in_specs=[head] * 4 + [whole(segment), whole(cosine), whole(sine)],
        out_specs=[cols, pl.BlockSpec((group * PAIR, length), lambda h: (h, 0)),
                   pl.BlockSpec((3, length, group * PAIR), lambda h: (0, 0, h))],
        scratch_shapes=[pltpu.VMEM((group, length, PAIR), F32)] * 2
        + [pltpu.VMEM((length, 1), jnp.int32), pltpu.VMEM((1, length), jnp.int32), pltpu.SMEM((length // rows,), jnp.int32)],
        out_shape=[s((length, width), BF16), s((width, length), BF16), s((3, length, width), BF16)],
        compiler_params=pltpu.CompilerParams(vmem_limit_bytes=56 * 2**20),
        name="attention",
    )(q, k, v, gc, segment, cosine, sine)


class Line:
    def __init__(self):
        self.d = lax.axis_index("dp")
        self.z = lax.axis_index("rows")
        self.core = self.d % 2
        self.x = (self.d // 2) % 2
        self.y = self.d // 4
        self.over_core = (self.d + 1 - 2 * self.core, self.z)
        self.over_x = (self.d + 2 - 4 * self.x, self.z)
        self.over_y = (self.d + 4 - 8 * self.y, self.z)
        self.inner = (self.z + 1) // 2 % 2
        self.near = (self.d, self.z + 1 - 2 * (self.z % 2))
        self.far = (self.d, 3 - self.z)


class Everywhere:
    def __init__(self, at, of_dp, of_rows, send, recv):
        self.at, self.of_dp, self.of_rows, self.send, self.recv = at, of_dp, of_rows, send, recv
        self.devices, self.lines = of_dp.shape[0], of_rows.shape[0]

    def over_dp(self, j):
        at = self.at
        mine = self.of_dp.at[at.d]
        return remote(mine, mine, self.send.at[j], self.recv.at[j], (lax.rem(at.d + j, self.devices), at.z))

    def over_rows(self, j):
        at, sem = self.at, self.devices + j
        mine = self.of_rows.at[at.z]
        return remote(mine, mine, self.send.at[sem], self.recv.at[sem], (at.d, lax.rem(at.z + j, self.lines)))

    def begin(self, rows):
        self.of_dp[self.at.d] = jnp.concatenate(rows, axis=0)
        for j in range(1, self.devices):
            self.over_dp(j).start()

    def turn(self):
        for j in range(1, self.devices):
            self.over_dp(j).wait()
        total = self.of_dp[0]
        for j in range(1, self.devices):
            total = total + self.of_dp[j]
        self.of_rows[self.at.z] = total
        for j in range(1, self.lines):
            self.over_rows(j).start()

    def end(self):
        for j in range(1, self.lines):
            self.over_rows(j).wait()
        total = self.of_rows[0]
        for j in range(1, self.lines):
            total = total + self.of_rows[j]
        return total


LAGS = dict(core=1, first=3, second=5, z=7, mid=9, back=11)
RING, CORE_RING, LINK_RING = 7, 6, 8


def chunk_columns(i, n_mlp, pieces, per_group):
    period = per_group + 1
    busy = n_mlp // per_group * period
    if i < busy and i % period < per_group:
        return "mlp", per_group * (i // period) + i % period
    j = i // period if i < busy else i - n_mlp
    wide = pieces // 3
    return ("rest", 2 * j, 2 * j + 1) if j < wide else ("rest", j + wide)


def back_body(count_ref, begin_ref, mlp_ref, q_ref, k_ref, v_ref, gc_ref, x_ref, base_ref, t2_ref, cos_ref, sin_ref, g1_ref,
              gain2_ref, shift2_ref, bup_ref, bout_ref, n2t_hbm, glt_hbm, n1t_hbm, gl_hbm, wout_hbm, wqkv_hbm,
              out_ref, ig_ref, total_ref, vec_ref,
              left_mlp, left_rest, rhs, wout_ref, wqkv_ref, load_sem, ctx, dk_acc, dv_acc,
              part, from_core, from_first, from_second, from_near, from_far,
              c_send, c_recv, f_send, f_recv, s_send, s_recv, n_send, n_recv, m_send, m_recv,
              dp_e, rows_e, dp_l, rows_l, e_send, e_recv, l_send, l_recv, gain1, shift1, bqkv, *, rows, row_ticks):
    tick = pl.program_id(0)
    at = Line()
    chunks, block = total_ref.shape[0], total_ref.shape[1]
    length, width = begin_ref.shape[0], wout_ref.shape[0]
    groups = width // PIECE
    per_group = length // rows
    n_mlp, pieces = 2 * bup_ref.shape[1] // CHUNK, 4 * groups
    n_wide = n_mlp + pieces // 3
    period = per_group + 1
    busy = groups * period
    g, spot = jnp.minimum(tick // period, groups - 1), tick % period
    attending = (tick < busy) & (spot < per_group)
    first_need = (pltpu.make_async_copy(n2t_hbm, left_mlp.at[0], load_sem.at[0]),)
    later_need = [pltpu.make_async_copy(src, dst, load_sem.at[1 + j]) for j, (src, dst) in enumerate(
        ((glt_hbm, left_mlp.at[1]), (n1t_hbm, left_rest.at[0]), (gl_hbm, rhs.at[pl.ds(3 * groups, groups)]),
         (wout_hbm, wout_ref), (wqkv_hbm, wqkv_ref)))]

    @pl.when(tick == 0)
    def _():
        first_need[0].start()
        barrier = pltpu.get_barrier_semaphore()
        for j in range(1, 8):
            pl.semaphore_signal(barrier, inc=1, device_id=(lax.rem(at.d + j, 8), at.z), device_id_type=MESH)
        for j in range(1, 4):
            pl.semaphore_signal(barrier, inc=1, device_id=(at.d, lax.rem(at.z + j, 4)), device_id_type=MESH)
        pl.semaphore_wait(barrier, 10)
        for load in later_need:
            load.start()
        gain1[...] = jnp.zeros_like(gain1)
        shift1[...] = jnp.zeros_like(shift1)
        bqkv[...] = jnp.zeros_like(bqkv)
        first_need[0].wait()

    @pl.when(tick == 1)
    def _():
        for load in later_need:
            load.wait()

    def places(i):
        even = 1 - i % 2
        f = at.x * even + at.y * (1 - even)
        s = at.y * even + at.x * (1 - even)
        first = (at.d + even * (2 - 4 * at.x) + (1 - even) * (4 - 8 * at.y), at.z)
        second = (at.d + even * (4 - 8 * at.y) + (1 - even) * (2 - 4 * at.x), at.z)
        return f, s, first, second, i % RING

    def core_copy(i, w):
        lanes = pl.ds(0, w)
        return remote(part.at[i % RING, 1 - at.core, :, :, :, lanes], from_core.at[i % CORE_RING, :, :, :, lanes],
                      c_send.at[i], c_recv.at[i], at.over_core)

    def first_copy(i, w):
        f, s, first, second, slot = places(i)
        lanes = pl.ds(0, w)
        return remote(part.at[slot, at.core, 1 - f, :, :, lanes], from_first.at[i % LINK_RING, :, :, lanes],
                      f_send.at[i], f_recv.at[i], first)

    def second_copy(i, w):
        f, s, first, second, slot = places(i)
        lanes = pl.ds(0, w)
        return remote(part.at[slot, at.core, f, 1 - s, :, lanes], from_second.at[i % LINK_RING, :, lanes],
                      s_send.at[i], s_recv.at[i], second)

    def out_copy(i, w):
        lanes = pl.ds(0, w)
        return remote(total_ref.at[i, :, lanes], from_near.at[i % LINK_RING, :, lanes], n_send.at[i], n_recv.at[i], at.near)

    def far_copy(i, w):
        lanes = pl.ds(0, w)
        return remote(total_ref.at[i, :, lanes], from_far.at[i % LINK_RING, :, lanes], m_send.at[i], m_recv.at[i], at.far)

    def plus(a, b):
        return a + b

    def put(h, half, cols, rows_of):
        even = 1 - tick % 2
        for j in range(4):
            d = h * 4 + j
            c, x, y = d % 2, (d // 2) % 2, d // 4
            a = x * even + y * (1 - even)
            b = y * even + x * (1 - even)
            part[tick % RING, c, a, b, :, cols] = rows_of[j * block : (j + 1) * block].astype(BF16)

    half = width // 2

    @pl.when(attending)
    def _():
        left = (per_group * g + spot) // (n_mlp // 2)
        for h in range(2):
            put(h, half, slice(0, CHUNK), nn(left_mlp[left, h * half : (h + 1) * half, :], mlp_ref[...]))
        core_copy(tick, CHUNK).start()

    def rest(s, e):
        for h in range(2):
            put(h, half, slice(e * PIECE, (e + 1) * PIECE),
                nn(left_rest[s // (3 * groups), h * half : (h + 1) * half, :], rhs[s]))

    @pl.when((tick < n_wide) & jnp.logical_not(attending))
    def _():
        late = tick // busy
        j = (tick // period) * (1 - late) + (tick - n_mlp) * late
        for e in range(2):
            rest(2 * j + e, e)
        core_copy(tick, CHUNK).start()

    @pl.when((tick >= n_wide) & (tick < chunks))
    def _():
        rest(tick - n_wide + 2 * (n_wide - n_mlp), 0)
        core_copy(tick, PIECE).start()

    def when(lag, f):
        i = tick - lag

        @pl.when((i >= 0) & (i < n_wide))
        def _():
            f(i, CHUNK)

        @pl.when((i >= n_wide) & (i < chunks))
        def _():
            f(i, PIECE)

    def core_step(i, w):
        f, s, first, second, slot = places(i)
        core_copy(i, w).wait()
        for a in range(2):
            for b in range(2):
                part[slot, at.core, a, b, :, :w] = plus(part[slot, at.core, a, b, :, :w], from_core[i % CORE_RING, a, b, :, :w])
        first_copy(i, w).start()

    def first_step(i, w):
        f, s, first, second, slot = places(i)
        first_copy(i, w).wait()
        for b in range(2):
            part[slot, at.core, f, b, :, :w] = plus(part[slot, at.core, f, b, :, :w], from_first[i % LINK_RING, b, :, :w])
        second_copy(i, w).start()

    def second_step(i, w):
        f, s, first, second, slot = places(i)
        second_copy(i, w).wait()
        total_ref[i, :, :w] = plus(part[slot, at.core, f, s, :, :w], from_second[i % LINK_RING, :, :w])

        @pl.when(at.inner == 0)
        def _():
            out_copy(i, w).start()

    def near_step(i, w):
        @pl.when(at.inner == 1)
        def _():
            out_copy(i, w).wait_recv()
            total_ref[i, :, :w] = plus(total_ref[i, :, :w], from_near[i % LINK_RING, :, :w])
            far_copy(i, w).start()

    def far_step(i, w):
        @pl.when(at.inner == 1)
        def _():
            far_copy(i, w).wait()
            total_ref[i, :, :w] = plus(total_ref[i, :, :w], from_far[i % LINK_RING, :, :w])
            out_copy(i, w).start()

        @pl.when(at.inner == 0)
        def _():
            out_copy(i, w).wait_send()

    def back_step(i, w):
        @pl.when(at.inner == 0)
        def _():
            out_copy(i, w).wait_recv()
            total_ref[i, :, :w] = from_near[i % LINK_RING, :, :w]

        @pl.when(at.inner == 1)
        def _():
            out_copy(i, w).wait_send()

    when(LAGS["core"], core_step)
    when(LAGS["first"], first_step)
    when(LAGS["second"], second_step)
    when(LAGS["z"], near_step)
    when(LAGS["mid"], far_step)
    when(LAGS["back"], back_step)

    each = range(GROUP)

    def unit(b):
        part = rows // 2
        blocks = [(h, b * rows + j * part) for j in range(2) for h in each]
        context, dq, dk, dv = attend([q_ref[h, t : t + part, :] for h, t in blocks], [k_ref[h, : t + part, :] for h, t in blocks],
                                     [v_ref[h, : t + part, :] for h, t in blocks], [gc_ref[h, t : t + part, :] for h, t in blocks],
                                     [begin_ref[t : t + part, :] for h, t in blocks], [t for h, t in blocks])
        for i, (h, t) in enumerate(blocks):
            cols, mine = slice(h * PAIR, (h + 1) * PAIR), slice(t, t + part)
            dk_acc[h, : t + part, :] += dk[i]
            dv_acc[h, : t + part, :] += dv[i]
            ctx[g, mine, cols] = context[i]
            left_rest[1, pl.ds(pl.multiple_of(g * PIECE + h * PAIR, PAIR), PAIR), mine] = context[i].T
            rhs[3 * g, mine, cols] = (dq[i] * cos_ref[mine, :] - turned(dq[i]) * sin_ref[mine, :]).astype(BF16)

    @pl.when(attending & (spot == 0))
    def _():
        dk_acc[...] = jnp.zeros_like(dk_acc)
        dv_acc[...] = jnp.zeros_like(dv_acc)

    for b in range(per_group):
        @pl.when(attending & (spot == b))
        def _():
            unit(b)

    @pl.when(attending & (spot == per_group - 1))
    def _():
        for h in each:
            cols = slice(h * PAIR, (h + 1) * PAIR)
            dk = dk_acc[h]
            rhs[3 * g + 1, :, cols] = (dk * cos_ref[...] - turned(dk) * sin_ref[...]).astype(BF16)
            rhs[3 * g + 2, :, cols] = dv_acc[h].astype(BF16)

    row_at = chunks - 2

    @pl.when((tick >= row_at) & (tick < row_at + row_ticks))
    def _():
        n_rows = x_ref.shape[0]
        here = pl.ds(pl.multiple_of((tick - row_at) * n_rows, n_rows), n_rows)
        attn = base_ref[...]
        for j in range(groups):
            attn = attn + nn(ctx[j, here, :], wout_ref[j * PIECE : (j + 1) * PIECE, :])
        out_ref[...] = attn.astype(BF16)
        g1 = jnp.zeros(attn.shape, F32)
        for s in range(3 * groups):
            cols = slice((s % 3) * width + (s // 3) * PIECE, (s % 3) * width + (s // 3 + 1) * PIECE)
            grads = rhs[s, here, :]
            g1 = g1 + nt(grads, wqkv_ref[:, cols])
            bqkv[:, cols] += jnp.sum(grads.astype(F32), axis=0, keepdims=True)
        x = x_ref[...].astype(F32)
        centred = x - jnp.mean(x, axis=1, keepdims=True)
        r = lax.rsqrt(jnp.mean(centred * centred, axis=1, keepdims=True) + EPSILON)
        n = centred * r
        gain1[...] += jnp.sum(g1 * n, axis=0, keepdims=True)
        shift1[...] += jnp.sum(g1, axis=0, keepdims=True)
        t = g1 * g1_ref[...].reshape(1, -1) + t2_ref[...]
        dx = r * (t - jnp.mean(t, axis=1, keepdims=True) - n * jnp.mean(t * n, axis=1, keepdims=True))
        gl = jnp.concatenate([rhs[3 * groups + j, here, :] for j in range(groups)], axis=1)
        ig_ref[...] = (gl.astype(F32) + dx).astype(BF16)

    def lines(ref):
        return [ref[:, j : j + width] for j in range(0, ref.shape[1], width)]

    early = Everywhere(at, dp_e, rows_e, e_send, e_recv)
    late = Everywhere(at, dp_l, rows_l, l_send, l_recv)
    row = jnp.full((1, width), count_ref[0].astype(F32), F32)

    @pl.when(tick == 1)
    def _():
        early.begin(lines(bup_ref) + lines(bout_ref) + lines(gain2_ref) + lines(shift2_ref) + [row])

    @pl.when(tick == 4)
    def _():
        early.turn()

    @pl.when(tick == 7)
    def _():
        vec_ref[0] = early.end()

    begin = row_at + row_ticks

    @pl.when(tick == begin)
    def _():
        late.begin(lines(gain1) + lines(shift1) + lines(bqkv) + [jnp.zeros((3, width), F32)])

    @pl.when(tick == begin + 2)
    def _():
        late.turn()

    @pl.when(tick == begin + 4)
    def _():
        vec_ref[1] = late.end()


def back(count, begins, mlp, q, k, v, gc, x, base, t2, cosine, sine, g1, gain2, shift2, bup, bout, n2t, glt, n1t, gl, wout, wqkv,
         rows=256):
    length, width = x.shape
    ff = bup.shape[1]
    block = width // 8
    groups = width // PIECE
    n_mlp, pieces = 2 * ff // CHUNK, 4 * groups
    chunks = n_mlp + pieces // 3 + pieces - 2 * (pieces // 3)
    row_ticks = length // rows
    period = row_ticks + 1
    busy = groups * period
    ticks = max(chunks + LAGS["back"], chunks - 2 + row_ticks + 5)

    def row(cols):
        return pl.BlockSpec((rows, cols), lambda t: (jnp.clip(t - (chunks - 2), 0, row_ticks - 1), 0))

    def whole(a):
        return pl.BlockSpec(a.shape, lambda t: (0,) * a.ndim, pipeline_mode=pl.Buffered(1))

    def mlp_cols(t):
        return (0, jnp.minimum(row_ticks * (t // period) + jnp.minimum(t % period, row_ticks - 1), n_mlp - 1))

    heads = pl.BlockSpec((GROUP, length, PAIR), lambda t: (jnp.minimum(t // period, groups - 1), 0, 0))
    s = jax.ShapeDtypeStruct
    dma = pltpu.SemaphoreType.DMA
    loaded = (n2t, glt, n1t, gl, wout, wqkv)
    return pl.pallas_call(
        functools.partial(back_body, rows=rows, row_ticks=row_ticks),
        grid=(ticks,),
        in_specs=[pl.BlockSpec(memory_space=pltpu.SMEM), whole(begins), pl.BlockSpec((length, CHUNK), mlp_cols)]
        + [heads] * 4 + [row(width)] * 3
        + [whole(a) for a in (cosine, sine, g1, gain2, shift2, bup, bout)] + [pl.BlockSpec(memory_space=pl.ANY)] * len(loaded),
        out_specs=[row(width), row(width),
                   pl.BlockSpec((chunks, block, CHUNK), lambda t: (0, 0, 0), pipeline_mode=pl.Buffered(1)),
                   pl.BlockSpec((2, 8, width), lambda t: (0, 0, 0), pipeline_mode=pl.Buffered(1))],
        out_shape=[s((length, width), BF16), s((length, width), BF16), s((chunks, block, CHUNK), BF16), s((2, 8, width), F32)],
        scratch_shapes=[
            pltpu.VMEM((2, width, length), BF16),
            pltpu.VMEM((2, width, length), BF16),
            pltpu.VMEM((4 * groups, length, PIECE), BF16),
            pltpu.VMEM(wout.shape, BF16),
            pltpu.VMEM(wqkv.shape, BF16),
            dma((len(loaded),)),
            pltpu.VMEM((groups, length, PIECE), BF16),
            pltpu.VMEM((GROUP, length, PAIR), F32),
            pltpu.VMEM((GROUP, length, PAIR), F32),
            pltpu.VMEM((RING, 2, 2, 2, block, CHUNK), BF16),
            pltpu.VMEM((CORE_RING, 2, 2, block, CHUNK), BF16),
            pltpu.VMEM((LINK_RING, 2, block, CHUNK), BF16),
            pltpu.VMEM((LINK_RING, block, CHUNK), BF16),
            pltpu.VMEM((LINK_RING, block, CHUNK), BF16),
            pltpu.VMEM((LINK_RING, block, CHUNK), BF16),
        ] + [dma((chunks,))] * 10 + [
            pltpu.VMEM((8, 8, width), F32), pltpu.VMEM((4, 8, width), F32),
            pltpu.VMEM((8, 8, width), F32), pltpu.VMEM((4, 8, width), F32),
            dma((12,)), dma((12,)), dma((12,)), dma((12,)),
            pltpu.VMEM((1, width), F32), pltpu.VMEM((1, width), F32), pltpu.VMEM((1, 3 * width), F32),
        ],
        compiler_params=pltpu.CompilerParams(vmem_limit_bytes=60 * 2**20, collective_id=0, has_side_effects=True),
        name="back",
    )(count, begins, mlp, q, k, v, gc, x, base, t2, cosine, sine, g1, gain2, shift2, bup, bout, *loaded)


def finish_body(out_hbm, ig_hbm, total_hbm, vec_ref, out_to, ig_to, up_to, down_to, low_to, qkv_to,
                gain1_ref, shift1_ref, bqkv_ref, bout_ref, gain2_ref, shift2_ref, bup_ref, bdown_ref,
                held, total_ref, up_ref, down_ref, low_ref, qkv_ref, sem):
    load = pltpu.make_async_copy(total_hbm, total_ref, sem.at[0])
    load.start()
    takes = [pltpu.make_async_copy(a, held.at[j], sem.at[1 + j]) for j, a in enumerate((out_hbm, ig_hbm))]
    copies = [pltpu.make_async_copy(held.at[j], a, sem.at[3 + j]) for j, a in enumerate((out_to, ig_to))]
    for take in takes:
        take.start()
    width, ff = gain1_ref.shape[0], bup_ref.shape[0]
    factor = 1.0 / vec_ref[0, 7:8, 0:1]
    groups = width // PIECE
    n_up = ff // CHUNK
    load.wait()

    def put(kinds):
        for i in range(total_ref.shape[0]):
            kind, *what = chunk_columns(i, 2 * n_up, 4 * groups, 2 * n_up // groups)
            if kind not in kinds or (kind == "mlp" and what[0] // n_up != kinds[kind]):
                continue
            if kind == "mlp":
                ref, j = (up_ref, down_ref)[kinds[kind]], what[0] % n_up
                ref[:, j * CHUNK : (j + 1) * CHUNK] = total_ref[i].astype(F32) * factor
                continue
            for e, s in enumerate(what):
                ref, col = (qkv_ref, (s % 3) * width + (s // 3) * PIECE) if s < 3 * groups else (low_ref, (s - 3 * groups) * PIECE)
                ref[:, col : col + PIECE] = total_ref[i, :, e * PIECE : (e + 1) * PIECE].astype(F32) * factor

    results = []

    def send(ref, to):
        results.append(pltpu.make_async_copy(ref, to, sem.at[5 + len(results)]))
        results[-1].start()

    put({"mlp": 0})
    send(up_ref, up_to)
    for take, copy in zip(takes, copies):
        take.wait()
        copy.start()
    put({"mlp": 1})
    send(down_ref, down_to)
    put({"rest": 0})
    send(low_ref, low_to)
    send(qkv_ref, qkv_to)
    first, second = vec_ref[0] * factor, vec_ref[1] * factor
    for j in range(ff // width):
        bup_ref[j * width : (j + 1) * width] = first[j]
    j = ff // width
    for ref, line in ((bout_ref, first[j]), (bdown_ref, first[j]), (gain2_ref, first[j + 1]), (shift2_ref, first[j + 2]),
                      (gain1_ref, second[0]), (shift1_ref, second[1])):
        ref[...] = line
    for j in range(3):
        bqkv_ref[j * width : (j + 1) * width] = second[2 + j]
    for copy in copies + results:
        copy.wait()


def finish(out, ig, total, vec, ff):
    length, width = out.shape
    block = total.shape[1]
    s = jax.ShapeDtypeStruct
    hbm, vmem = pl.BlockSpec(memory_space=pltpu.HBM), pl.BlockSpec(memory_space=pltpu.VMEM)
    vectors = (width, width, 3 * width, width, width, width, ff, width)
    grads = [(block, ff), (block, ff), (block, width), (block, 3 * width)]
    return pl.pallas_call(
        finish_body,
        in_specs=[hbm, hbm, hbm, vmem],
        out_specs=[hbm] * 6 + [vmem] * 8,
        out_shape=[s(out.shape, BF16), s(ig.shape, BF16)] + [s(shape, F32) for shape in grads] + [s((n,), F32) for n in vectors],
        scratch_shapes=[pltpu.VMEM((2, length, width), BF16), pltpu.VMEM(total.shape, BF16)]
        + [pltpu.VMEM(shape, F32) for shape in grads] + [pltpu.SemaphoreType.DMA((9,))],
        compiler_params=pltpu.CompilerParams(vmem_limit_bytes=60 * 2**20),
        name="finish",
    )(out, ig, total, vec)


def by_collectives(segment, count, begins, mlp, q, k, v, gc, x, base, t2, cosine, sine, g1, gain2, shift2, bup, bout, n2t, glt, n1t, gl,
                   wout, wqkv):
    width, ff = x.shape[1], bup.shape[1]
    ctx, ctxt, gu = attention(q, k, v, gc, segment, cosine, sine)
    flat = jnp.concatenate([gu[0], gu[1], gu[2]], axis=1)
    low = jnp.concatenate(list(gl), axis=1)
    out = (base + nn(ctx, wout)).astype(BF16)
    grad_one = nt(flat, wqkv)
    x = x.astype(F32)
    centred = x - jnp.mean(x, axis=1, keepdims=True)
    r = lax.rsqrt(jnp.mean(centred * centred, axis=1, keepdims=True) + EPSILON)
    n = centred * r
    t = grad_one * g1 + t2
    dx = r * (t - jnp.mean(t, axis=1, keepdims=True) - n * jnp.mean(t * n, axis=1, keepdims=True))
    input_grad = (low.astype(F32) + dx).astype(BF16)
    packed = jnp.concatenate([bup[0], bout[0], gain2[0], shift2[0], jnp.full(width, count[0].astype(F32)),
                              jnp.sum(grad_one * n, axis=0), jnp.sum(grad_one, axis=0), jnp.sum(flat, axis=0, dtype=F32),
                              jnp.zeros(3 * width, F32)])
    packed = lax.psum(packed, ("dp", "rows"))
    mlp_part = jnp.concatenate([nn(n2t, mlp[:, :ff]), nn(glt, mlp[:, ff:])], axis=1)
    rest = [nn(n1t, gu[s % 3, :, (s // 3) * PIECE : (s // 3 + 1) * PIECE]) for s in range(3 * width // PIECE)]
    rest = jnp.concatenate(rest + [nn(ctxt, low)], axis=1)
    columns, n_mlp, pieces = [], 2 * ff // CHUNK, 4 * width // PIECE
    for i in range(n_mlp + pieces // 3 + pieces - 2 * (pieces // 3)):
        kind, *what = chunk_columns(i, n_mlp, pieces, n_mlp * PIECE // width)
        held = mlp_part if kind == "mlp" else rest
        begin, size = (what[0] * CHUNK, CHUNK) if kind == "mlp" else (what[0] * PIECE, len(what) * PIECE)
        columns.append(jnp.pad(held[:, begin : begin + size], ((0, 0), (0, CHUNK - size))))
    part = jnp.stack(columns, axis=1).astype(BF16)
    grads = lax.psum(lax.psum_scatter(part, "dp", scatter_dimension=0, tiled=True), "rows")
    return out, input_grad, jnp.swapaxes(grads, 0, 1), packed.reshape(2, 8, width)


def shards(tokens, segment_ids, true_counts, regroup, cotangent, ln1_gain, ln1_bias, qkv_weight, qkv_bias, out_weight,
           out_bias, ln2_gain, ln2_bias, up_weight, up_bias, down_weight, down_bias):
    length, width = cotangent.shape
    ff = up_weight.shape[1]
    cosine, sine = (jnp.asarray(t) for t in rotary_tables(length))
    (arrived, q, k, v, gc, n1t, n2t, glt, gl, mlp, base, t2, gain2, shift2, bias_up, bias_out, begins) = front(
        true_counts, regroup, segment_ids, tokens, cotangent, cosine, sine, ln1_gain, ln1_bias, qkv_weight, qkv_bias, out_weight, out_bias,
        ln2_gain, ln2_bias, up_weight, up_bias, down_weight, down_bias)
    last = back if (lax.axis_size("dp"), lax.axis_size("rows")) == (8, 4) else functools.partial(by_collectives, segment_ids)
    out, input_grad, total, vec = last(true_counts, begins, mlp, q, k, v, gc, arrived, base, t2, cosine, sine, ln1_gain, gain2,
                                       shift2, bias_up, bias_out, n2t, glt, n1t, gl, out_weight, qkv_weight)
    (out, input_grad, up, down, low, qkv, gain1, shift1, bias_qkv, bias_out, gain2, shift2, bias_up, bias_down) = finish(
        out, input_grad, total, vec, up_weight.shape[1])
    return (out, input_grad, gain1, shift1, qkv, bias_qkv, low, bias_out, gain2, shift2, up, bias_up, down.T, bias_down)


def solution(mesh):
    both = ("dp", "rows")
    placed = (P(both, None), P(both), P(both), P(both), P(both, None)) + (P(),) * 12
    return jax.shard_map(
        shards, mesh=mesh, in_specs=placed,
        out_specs=(P(both, None), P(both, None), P(), P(), P("dp", None), P(), P("dp", None), P(), P(), P(), P("dp", None), P(),
                   P(None, "dp"), P()),
        check_vma=False)
```

```python
import functools
import numpy as np
import jax
import jax.numpy as jnp
from jax import lax
from jax.experimental import pallas as pl
from jax.experimental.pallas import tpu as pltpu
from jax.sharding import PartitionSpec as P

HEAD_DIM = 64
ROT = 16
PAIR = 128
CHUNK = 512
PIECE = 256
GROUP = 2
SPAN = 256
EPSILON = 1e-05
EXCLUDED = -1e30
F32 = jnp.float32
BF16 = jnp.bfloat16
MESH = pl.DeviceIdType.MESH


def remote(src, dst, send, recv, to):
    return pltpu.make_async_remote_copy(src_ref=src, dst_ref=dst, send_sem=send, recv_sem=recv, device_id=to, device_id_type=MESH)


def nn(a, b):
    return lax.dot_general(a, b, (((1,), (0,)), ((), ())), preferred_element_type=F32)


def nt(a, b):
    return lax.dot_general(a, b, (((1,), (1,)), ((), ())), preferred_element_type=F32)


def tn(a, b):
    return lax.dot_general(a, b, (((0,), (0,)), ((), ())), preferred_element_type=F32)


def rotary_tables(length):
    half = ROT // 2
    placed = np.arange(length, dtype=np.float32)
    rates = np.exp(np.arange(half, dtype=np.float32) * np.float32(-2.0 / ROT) * np.log(np.float32(10000.0)))
    phases = placed[:, None] * rates[None, :].astype(np.float32)
    cosine = np.ones((length, HEAD_DIM), np.float32)
    sine = np.zeros((length, HEAD_DIM), np.float32)
    cosine[:, :half] = np.cos(phases)
    cosine[:, half:ROT] = np.cos(phases)
    sine[:, :half] = -np.sin(phases)
    sine[:, half:ROT] = np.sin(phases)
    return np.tile(cosine, (1, PAIR // HEAD_DIM)), np.tile(sine, (1, PAIR // HEAD_DIM))


def turned(u):
    lane = lax.broadcasted_iota(jnp.int32, u.shape, 1) % HEAD_DIM
    half = ROT // 2
    return jnp.where(lane < half, pltpu.roll(u, PAIR - half, 1), pltpu.roll(u, half, 1))


def gelu_parts(h):
    e = jnp.exp(h * h * -0.5)
    t = 1.0 / (1.0 + 0.2316418882 * jnp.abs(h))
    poly = t * (0.127414796 + t * (-0.142248368 + t * (0.7107068705 + t * (-0.7265760135 + t * 0.5307027145))))
    tail = poly * e
    phi = jnp.where(h >= 0, 1.0 - tail, tail)
    return h * phi, phi + h * (e * 0.3989422804014327)


def attend(q, k, v, gc, begins, t_first):
    each, rows = range(len(q)), q[0].shape[0]
    low = lax.broadcasted_iota(jnp.int32, (rows, PAIR), 1) < HEAD_DIM

    def both(t):
        zero = jnp.zeros_like(t)
        return jnp.concatenate([jnp.where(low, t, zero), jnp.where(low, zero, t)], axis=0)

    def allowed(h):
        span = k[h].shape[0]
        s_at = lax.broadcasted_iota(jnp.int32, (rows, span), 1)
        t_at = t_first[h] + lax.broadcasted_iota(jnp.int32, (rows, span), 0)
        seen = (s_at >= begins[h]) & (s_at <= t_at)
        return jnp.concatenate([seen, seen], axis=0)

    seen = {t_first[h]: allowed(h) for h in each}
    q2, g2 = [both(t) for t in q], [both(t) for t in gc]
    scores = [jnp.where(seen[t_first[h]], nt(q2[h], k[h]), EXCLUDED) for h in each]
    dp = [nt(g2[h], v[h]) for h in each]
    e = [jnp.exp(scores[h] - jnp.max(scores[h], axis=1, keepdims=True)) for h in each]
    p = [e[h] * (1.0 / jnp.sum(e[h], axis=1, keepdims=True)) for h in each]
    p16 = [p[h].astype(BF16) for h in each]
    c2 = [nn(p16[h], v[h]) for h in each]
    dv = [tn(p16[h], g2[h]) for h in each]
    w = [p[h] * dp[h] for h in each]
    ds16 = [(w[h] - p[h] * jnp.sum(w[h], axis=1, keepdims=True)).astype(BF16) for h in each]
    d2 = [nn(ds16[h], k[h]) for h in each]
    dk = [tn(ds16[h], q2[h]) for h in each]
    context = [jnp.where(low, c2[h][:rows], c2[h][rows:]).astype(BF16) for h in each]
    dq = [jnp.where(low, d2[h][:rows], d2[h][rows:]) * (HEAD_DIM ** -0.5) for h in each]
    return context, dq, dk, dv


def front_body(count_ref, want_ref, seg_ref, cos_ref, sin_ref, g1_vec, b1_vec, bqkv_vec, bout_vec, g2_vec, b2_vec,
               bup_vec, bdown_vec, own_hbm, cot_hbm, wqkv_hbm, wout_hbm, wup_hbm, wdown_hbm,
               x_ref, q_ref, k_ref, v_ref, gc_ref, n1t_ref, n2t_ref, glt_ref, gl_ref, mlp_ref, base_ref, t2_ref,
               gain2_ref, shift2_ref, bup_out, bout_out, begin_ref,
               wqkv_ref, wout_ref, wup_ref, wdown_ref, wants, from_near, from_half, to_inner, to_end,
               g1_ref, b1_ref, bqkv_ref, bout_ref, g2_ref, b2_ref, bup_ref, bdown_ref, own_ref, cot_ref, gl_all, ga_all, gc_all, w_sem, want_send, want_recv, near_send, near_recv, inner_send, end_send, half_recv, *, tile):
    step = pl.program_id(0)
    steps = pl.num_programs(0)
    length, width = cot_ref.shape
    rows = x_ref.shape[0]
    pairs = width // PAIR
    ff = wup_ref.shape[1]
    chunks = length // rows
    part = rows // 2
    parts = length // part
    d, z = lax.axis_index("dp"), lax.axis_index("rows")
    inner = (z + 1) // 2 % 2
    near = z + 1 - 2 * (z % 2)
    other_inner, other_end = 3 - z, 6 - 3 * z
    loads = [pltpu.make_async_copy(src, dst, w_sem.at[j]) for j, (src, dst) in enumerate(
        ((cot_hbm, cot_ref), (own_hbm, own_ref), (wdown_hbm, wdown_ref), (wout_hbm, wout_ref), (wqkv_hbm, wqkv_ref), (wup_hbm, wup_ref)))]

    def span(i):
        return pl.ds(pl.multiple_of(i * rows, rows), rows)

    def bit(i):
        return pl.ds(pl.multiple_of(i * part, part), part)

    def want_copy(j):
        to = lax.rem(z + j, 4)
        return remote(wants.at[0], wants.at[j], want_send.at[j], want_recv.at[j], (d, to))

    def near_copy(i):
        return remote(own_hbm.at[bit(i)], from_near.at[bit(i)], near_send.at[i], near_recv.at[i], (d, near))

    def inner_copy(i):
        return remote(to_inner.at[bit(i)], from_half.at[bit(i)], inner_send.at[i], half_recv.at[i], (d, other_inner))

    def end_copy(i):
        return remote(to_end.at[bit(i)], from_half.at[bit(i)], end_send.at[i], half_recv.at[i], (d, other_end))

    def wanted(by):
        return wants[lax.rem(z - by + 4, 4), 0:1, 0:1]

    def relay(i):
        @pl.when(inner == 1)
        def _():
            near_copy(i).wait_recv()
            mine = own_ref[bit(i), :].astype(F32)
            theirs = from_near[bit(i), :].astype(F32)
            to_end[bit(i), :] = jnp.where(wanted(other_end) == near, theirs, mine).astype(BF16)
            end_copy(i).start()
            to_inner[bit(i), :] = jnp.where(wanted(other_inner) == near, theirs, mine).astype(BF16)
            inner_copy(i).start()

    @pl.when(step == 0)
    def _():
        barrier = pltpu.get_barrier_semaphore()
        for j in (1, 2, 3):
            pl.semaphore_signal(barrier, inc=1, device_id=(d, lax.rem(z + j, 4)), device_id_type=MESH)
        for load in loads:
            load.start()
        wants[0] = jnp.full(wants.shape[1:], want_ref[0] % 4, jnp.int32)
        pl.semaphore_wait(barrier, 3)
        for j in (1, 2, 3):
            want_copy(j).start()

        def hand(i, carry):
            near_copy(i).start()
            return carry

        lax.fori_loop(0, parts, hand, 0)
        for vec, ref in ((g1_vec, g1_ref), (b1_vec, b1_ref), (bqkv_vec, bqkv_ref), (bout_vec, bout_ref), (g2_vec, g2_ref),
                         (b2_vec, b2_ref), (bup_vec, bup_ref), (bdown_vec, bdown_ref)):
            ref[...] = vec[...].reshape(1, -1)
        gain2_ref[...] = jnp.zeros_like(gain2_ref)
        shift2_ref[...] = jnp.zeros_like(shift2_ref)
        bup_out[...] = jnp.zeros_like(bup_out)
        loads[0].wait()
        place = lax.broadcasted_iota(jnp.int32, (length, 1), 0)
        masked = jnp.where(place < count_ref[0], cot_ref[...].astype(F32), 0.0)
        gl_all[...] = masked.astype(BF16)
        bout_out[...] = jnp.sum(masked, axis=0, keepdims=True)

        def active(f):
            ga_all[f] = nt(gl_all[...], wdown_ref[f * tile : (f + 1) * tile, :])

        tiles = ff // tile
        loads[1].wait()
        for j in (1, 2, 3):
            want_copy(j).wait()
        relay(0)
        relay(1)
        loads[2].wait()
        for f in range(tiles - 2):
            active(f)
        relay(2)
        relay(3)
        for f in range(tiles - 2, tiles):
            active(f)
        wide = jnp.broadcast_to(seg_ref[...].reshape(1, -1), (8, length)).astype(F32)
        tall = wide.T[:, :1]
        for b in range(0, length, PAIR):
            earlier = jnp.where(wide[:1] < tall[b : b + PAIR], 1.0, 0.0)
            begin_ref[b : b + PAIR, :] = jnp.sum(earlier, axis=1, keepdims=True).astype(jnp.int32)
        loads[3].wait()
        for p in range(pairs):
            gc_all[p] = nt(gl_all[...], wout_ref[p * PAIR : (p + 1) * PAIR, :]).astype(BF16)
        for load in loads[4:]:
            load.wait()

    @pl.when((step > 0) & (step + 1 < chunks))
    def _():
        relay(2 * step + 2)
        relay(2 * step + 3)

    gl16 = gl_all[span(step), :]
    for j in range(gl_ref.shape[0]):
        gl_ref[j] = gl16[:, j * PIECE : (j + 1) * PIECE]
    glt_ref[...] = gl16.T
    for p in range(pairs):
        gc_ref[p] = gc_all[p, span(step), :]

    @pl.when(inner == 0)
    def _():
        for j in range(2):
            near_copy(2 * step + j).wait_recv()

    for j in range(2):
        inner_copy(2 * step + j).wait_recv()
    source = wanted(z)
    x = jnp.where(source == near, from_near[span(step), :].astype(F32), from_half[span(step), :].astype(F32))
    x = jnp.where(source == z, own_ref[span(step), :].astype(F32), x)
    x_ref[...] = x.astype(BF16)
    centred = x - jnp.mean(x, axis=1, keepdims=True)
    r = lax.rsqrt(jnp.mean(centred * centred, axis=1, keepdims=True) + EPSILON)
    n = centred * r
    n1 = (n * g1_ref[...] + b1_ref[...]).astype(BF16)
    n2 = (n * g2_ref[...] + b2_ref[...]).astype(BF16)
    n1t_ref[...] = n1.T
    n2t_ref[...] = n2.T
    cosine, sine = cos_ref[...], sin_ref[...]
    for p in range(pairs):
        for which, ref in enumerate((q_ref, k_ref, v_ref)):
            wide = slice(which * width + p * PAIR, which * width + (p + 1) * PAIR)
            u = nn(n1, wqkv_ref[:, wide]) + bqkv_ref[:, wide]
            if which < 2:
                u = u * cosine + turned(u) * sine
            if which == 0:
                u = u * (HEAD_DIM ** -0.5)
            ref[p] = u.astype(BF16)
    mlp = x + (bdown_ref[...] + bout_ref[...])
    grad_two = jnp.zeros((rows, width), F32)
    for f in range(0, ff, tile):
        cols = slice(f, f + tile)
        h = nn(n2, wup_ref[:, cols]) + bup_ref[:, cols]
        ga = ga_all[f // tile, span(step), :]
        a, slope = gelu_parts(h)
        a16 = a.astype(BF16)
        gh = ga * slope
        gh16 = gh.astype(BF16)
        mlp_ref[:, cols] = gh16
        mlp_ref[:, ff + f : ff + f + tile] = a16
        bup_out[:, cols] += jnp.sum(gh16.astype(F32), axis=0, keepdims=True)
        mlp = mlp + nn(a16, wdown_ref[cols, :])
        grad_two = grad_two + nt(gh16, wup_ref[:, cols])
    base_ref[...] = mlp
    t2_ref[...] = grad_two * g2_ref[...]
    gain2_ref[...] += jnp.sum(grad_two * n, axis=0, keepdims=True)
    shift2_ref[...] += jnp.sum(grad_two, axis=0, keepdims=True)

    @pl.when(step == steps - 1)
    def _():
        def done(i, carry):
            near_copy(i).wait_send()

            @pl.when(inner == 1)
            def _():
                inner_copy(i).wait_send()
                end_copy(i).wait_send()
            return carry

        lax.fori_loop(0, parts, done, 0)


def front(count, want, segment, own, cot, cosine, sine, g1, b1, wqkv, bqkv, wout, bout, g2, b2, wup, bup, wdown, bdown, rows=128, tile=768):
    length, width = own.shape
    ff = wup.shape[1]
    pairs = width // PAIR
    chunks = length // rows

    def row(cols):
        return pl.BlockSpec((rows, cols), lambda i: (i, 0))

    def whole(a):
        return pl.BlockSpec(a.shape, lambda i: (0,) * a.ndim, pipeline_mode=pl.Buffered(1))

    heads = pl.BlockSpec((pairs, rows, PAIR), lambda i: (0, i, 0))
    down = pl.BlockSpec((width, rows), lambda i: (0, i))

    def vec(cols):
        return pl.BlockSpec((1, cols), lambda i: (0, 0))

    vectors = (g1, b1, bqkv, bout, g2, b2, bup, bdown)
    weights = (wqkv, wout, wup, wdown)
    s = jax.ShapeDtypeStruct
    dma = pltpu.SemaphoreType.DMA
    return pl.pallas_call(
        functools.partial(front_body, tile=tile),
        grid=(chunks,),
        in_specs=[pl.BlockSpec(memory_space=pltpu.SMEM), pl.BlockSpec(memory_space=pltpu.SMEM), whole(segment), row(PAIR), row(PAIR)]
        + [whole(a) for a in vectors] + [pl.BlockSpec(memory_space=pl.ANY)] * 6,
        out_specs=[row(width)] + [heads] * 4 + [down] * 3
        + [pl.BlockSpec((width // PIECE, rows, PIECE), lambda i: (0, i, 0)), row(2 * ff)] + [row(width)] * 2
        + [vec(width), vec(width), vec(ff), vec(width)] + [pl.BlockSpec((length, 1), lambda i: (0, 0))],
        out_shape=[s((length, width), BF16)] + [s((pairs, length, PAIR), BF16)] * 4 + [s((width, length), BF16)] * 3
        + [s((width // PIECE, length, PIECE), BF16), s((length, 2 * ff), BF16)]
        + [s((length, width), F32)] * 2 + [s((1, width), F32), s((1, width), F32), s((1, ff), F32), s((1, width), F32)] + [s((length, 1), jnp.int32)],
        scratch_shapes=[pltpu.VMEM(w.shape, BF16) for w in weights]
        + [pltpu.VMEM((4, 8, 128), jnp.int32)] + [pltpu.VMEM((length, width), BF16)] * 4
        + [pltpu.VMEM((1, v.shape[0]), F32) for v in vectors]
        + [pltpu.VMEM((length, width), BF16)] * 3 + [pltpu.VMEM((ff // tile, length, tile), F32), pltpu.VMEM((pairs, length, PAIR), BF16)]
        + [dma((6,)), dma((4,)), dma((4,))] + [dma((2 * chunks,))] * 5,
        compiler_params=pltpu.CompilerParams(vmem_limit_bytes=60 * 2**20, collective_id=1, has_side_effects=True),
        name="front",
    )(count, want, segment, cosine, sine, *vectors, own, cot, *weights)


def attention_body(q_ref, k_ref, v_ref, gc_ref, seg_ref, cos_ref, sin_ref,
                   ctx_ref, ctxt_ref, gu_ref, dk_acc, dv_acc, segc_ref, segr_ref, first_ref, *, rows):
    group, length, _ = q_ref.shape
    total = length // rows
    each = range(group)

    @pl.when(pl.program_id(0) == 0)
    def _():
        seg = seg_ref[...].reshape(1, -1)
        segr_ref[...] = seg
        segc_ref[...] = jnp.broadcast_to(seg, (8, length)).T[:, :1]
        wide = seg.astype(F32)
        for b in range(total):
            before = jnp.sum(jnp.where(wide < wide[:, b * rows : b * rows + 1], 1.0, 0.0))
            first_ref[b] = before.astype(jnp.int32) // rows

    lane = lax.broadcasted_iota(jnp.int32, (rows, PAIR), 1)
    low = lane < HEAD_DIM
    dk_acc[...] = jnp.zeros_like(dk_acc)
    dv_acc[...] = jnp.zeros_like(dv_acc)

    def both(ref, h, begin):
        t = ref[h, pl.ds(begin, rows), :]
        zero = jnp.zeros_like(t)
        return jnp.concatenate([jnp.where(low, t, zero), jnp.where(low, zero, t)], axis=0)

    def block(b, blocks):
        begin = pl.multiple_of(b * rows, rows)
        start = pl.multiple_of((b + 1 - blocks) * rows, rows)
        span = blocks * rows
        q2 = [both(q_ref, h, begin) for h in each]
        g2 = [both(gc_ref, h, begin) for h in each]
        k = [k_ref[h, pl.ds(start, span), :] for h in each]
        v = [v_ref[h, pl.ds(start, span), :] for h in each]
        segt = segc_ref[pl.ds(begin, rows), :]
        segs = segr_ref[:, pl.ds(start, span)]
        t_at = begin + lax.broadcasted_iota(jnp.int32, (rows, span), 0)
        s_at = start + lax.broadcasted_iota(jnp.int32, (rows, span), 1)
        allowed = (segt == segs) & (s_at <= t_at)
        allowed = jnp.concatenate([allowed, allowed], axis=0)
        scores = [jnp.where(allowed, nt(q2[h], k[h]), EXCLUDED) for h in each]
        dp = [nt(g2[h], v[h]) for h in each]
        e = [jnp.exp(scores[h] - jnp.max(scores[h], axis=1, keepdims=True)) for h in each]
        p = [e[h] * (1.0 / jnp.sum(e[h], axis=1, keepdims=True)) for h in each]
        p16 = [p[h].astype(BF16) for h in each]
        c2 = [nn(p16[h], v[h]) for h in each]
        for h in each:
            dv_acc[h, pl.ds(start, span), :] += tn(p16[h], g2[h])
        w = [p[h] * dp[h] for h in each]
        ds16 = [(w[h] - p[h] * jnp.sum(w[h], axis=1, keepdims=True)).astype(BF16) for h in each]
        d2 = [nn(ds16[h], k[h]) for h in each]
        for h in each:
            dk_acc[h, pl.ds(start, span), :] += tn(ds16[h], q2[h])
        cosine = cos_ref[pl.ds(begin, rows), :]
        sine = sin_ref[pl.ds(begin, rows), :]
        for h in each:
            cols = slice(h * PAIR, (h + 1) * PAIR)
            context = jnp.where(low, c2[h][:rows], c2[h][rows:]).astype(BF16)
            ctx_ref[pl.ds(begin, rows), cols] = context
            ctxt_ref[cols, pl.ds(begin, rows)] = context.T
            dq = jnp.where(low, d2[h][:rows], d2[h][rows:]) * (HEAD_DIM ** -0.5)
            gu_ref[0, pl.ds(begin, rows), cols] = (dq * cosine - turned(dq) * sine).astype(BF16)

    def loop(b, carry):
        count = b + 1 - first_ref[b]
        for blocks in range(1, total + 1):
            @pl.when(count == blocks)
            def _():
                block(b, blocks)
        return carry

    lax.fori_loop(0, total, loop, 0)
    for h in each:
        cols = slice(h * PAIR, (h + 1) * PAIR)
        dk = dk_acc[h]
        gu_ref[1, :, cols] = (dk * cos_ref[...] - turned(dk) * sin_ref[...]).astype(BF16)
        gu_ref[2, :, cols] = dv_acc[h].astype(BF16)


def attention(q, k, v, gc, segment, cosine, sine, rows=256, group=2):
    pairs, length, _ = q.shape
    head = pl.BlockSpec((group, length, PAIR), lambda h: (h, 0, 0))
    cols = pl.BlockSpec((length, group * PAIR), lambda h: (0, h))
    s = jax.ShapeDtypeStruct
    width = pairs * PAIR

    def whole(a):
        return pl.BlockSpec(a.shape, lambda h: (0,) * a.ndim, pipeline_mode=pl.Buffered(1))

    return pl.pallas_call(
        functools.partial(attention_body, rows=rows),
        grid=(pairs // group,),
        in_specs=[head] * 4 + [whole(segment), whole(cosine), whole(sine)],
        out_specs=[cols, pl.BlockSpec((group * PAIR, length), lambda h: (h, 0)),
                   pl.BlockSpec((3, length, group * PAIR), lambda h: (0, 0, h))],
        scratch_shapes=[pltpu.VMEM((group, length, PAIR), F32)] * 2
        + [pltpu.VMEM((length, 1), jnp.int32), pltpu.VMEM((1, length), jnp.int32), pltpu.SMEM((length // rows,), jnp.int32)],
        out_shape=[s((length, width), BF16), s((width, length), BF16), s((3, length, width), BF16)],
        compiler_params=pltpu.CompilerParams(vmem_limit_bytes=56 * 2**20),
        name="attention",
    )(q, k, v, gc, segment, cosine, sine)


class Line:
    def __init__(self):
        self.d = lax.axis_index("dp")
        self.z = lax.axis_index("rows")
        self.core = self.d % 2
        self.x = (self.d // 2) % 2
        self.y = self.d // 4
        self.over_core = (self.d + 1 - 2 * self.core, self.z)
        self.over_x = (self.d + 2 - 4 * self.x, self.z)
        self.over_y = (self.d + 4 - 8 * self.y, self.z)
        self.inner = (self.z + 1) // 2 % 2
        self.near = (self.d, self.z + 1 - 2 * (self.z % 2))
        self.far = (self.d, 3 - self.z)


class Everywhere:
    def __init__(self, at, of_dp, of_rows, send, recv):
        self.at, self.of_dp, self.of_rows, self.send, self.recv = at, of_dp, of_rows, send, recv
        self.devices, self.lines = of_dp.shape[0], of_rows.shape[0]

    def over_dp(self, j):
        at = self.at
        mine = self.of_dp.at[at.d]
        return remote(mine, mine, self.send.at[j], self.recv.at[j], (lax.rem(at.d + j, self.devices), at.z))

    def over_rows(self, j):
        at, sem = self.at, self.devices + j
        mine = self.of_rows.at[at.z]
        return remote(mine, mine, self.send.at[sem], self.recv.at[sem], (at.d, lax.rem(at.z + j, self.lines)))

    def begin(self, rows):
        self.of_dp[self.at.d] = jnp.concatenate(rows, axis=0)
        for j in range(1, self.devices):
            self.over_dp(j).start()

    def turn(self):
        for j in range(1, self.devices):
            self.over_dp(j).wait()
        total = self.of_dp[0]
        for j in range(1, self.devices):
            total = total + self.of_dp[j]
        self.of_rows[self.at.z] = total
        for j in range(1, self.lines):
            self.over_rows(j).start()

    def end(self):
        for j in range(1, self.lines):
            self.over_rows(j).wait()
        total = self.of_rows[0]
        for j in range(1, self.lines):
            total = total + self.of_rows[j]
        return total


LAGS = dict(core=1, first=3, second=5, z=7, mid=9, back=11)
RING, CORE_RING, LINK_RING = 7, 6, 8


def chunk_columns(i, n_mlp, pieces, per_group):
    period = per_group + 1
    busy = n_mlp // per_group * period
    if i < busy and i % period < per_group:
        return "mlp", per_group * (i // period) + i % period
    j = i // period if i < busy else i - n_mlp
    wide = pieces // 3
    return ("rest", 2 * j, 2 * j + 1) if j < wide else ("rest", j + wide)


def back_body(count_ref, begin_ref, mlp_ref, q_ref, k_ref, v_ref, gc_ref, x_ref, base_ref, t2_ref, cos_ref, sin_ref, g1_ref,
              gain2_ref, shift2_ref, bup_ref, bout_ref, n2t_hbm, glt_hbm, n1t_hbm, gl_hbm, wout_hbm, wqkv_hbm,
              out_ref, ig_ref, total_ref, vec_ref,
              left_mlp, left_rest, rhs, wout_ref, wqkv_ref, load_sem, ctx, dk_acc, dv_acc,
              part, from_core, from_first, from_second, from_near, from_far,
              c_send, c_recv, f_send, f_recv, s_send, s_recv, n_send, n_recv, m_send, m_recv,
              dp_e, rows_e, dp_l, rows_l, e_send, e_recv, l_send, l_recv, gain1, shift1, bqkv, *, rows, row_ticks):
    tick = pl.program_id(0)
    at = Line()
    chunks, block = total_ref.shape[0], total_ref.shape[1]
    length, width = begin_ref.shape[0], wout_ref.shape[0]
    groups = width // PIECE
    per_group = length // rows
    n_mlp, pieces = 2 * bup_ref.shape[1] // CHUNK, 4 * groups
    n_wide = n_mlp + pieces // 3
    period = per_group + 1
    busy = groups * period
    g, spot = jnp.minimum(tick // period, groups - 1), tick % period
    attending = (tick < busy) & (spot < per_group)
    first_need = (pltpu.make_async_copy(n2t_hbm, left_mlp.at[0], load_sem.at[0]),)
    later_need = [pltpu.make_async_copy(src, dst, load_sem.at[1 + j]) for j, (src, dst) in enumerate(
        ((glt_hbm, left_mlp.at[1]), (n1t_hbm, left_rest.at[0]), (gl_hbm, rhs.at[pl.ds(3 * groups, groups)]),
         (wout_hbm, wout_ref), (wqkv_hbm, wqkv_ref)))]

    @pl.when(tick == 0)
    def _():
        first_need[0].start()
        barrier = pltpu.get_barrier_semaphore()
        for j in range(1, 8):
            pl.semaphore_signal(barrier, inc=1, device_id=(lax.rem(at.d + j, 8), at.z), device_id_type=MESH)
        for j in range(1, 4):
            pl.semaphore_signal(barrier, inc=1, device_id=(at.d, lax.rem(at.z + j, 4)), device_id_type=MESH)
        pl.semaphore_wait(barrier, 10)
        for load in later_need:
            load.start()
        gain1[...] = jnp.zeros_like(gain1)
        shift1[...] = jnp.zeros_like(shift1)
        bqkv[...] = jnp.zeros_like(bqkv)
        first_need[0].wait()

    @pl.when(tick == 1)
    def _():
        for load in later_need:
            load.wait()

    def places(i):
        even = 1 - i % 2
        f = at.x * even + at.y * (1 - even)
        s = at.y * even + at.x * (1 - even)
        first = (at.d + even * (2 - 4 * at.x) + (1 - even) * (4 - 8 * at.y), at.z)
        second = (at.d + even * (4 - 8 * at.y) + (1 - even) * (2 - 4 * at.x), at.z)
        return f, s, first, second, i % RING

    def core_copy(i, w):
        lanes = pl.ds(0, w)
        return remote(part.at[i % RING, 1 - at.core, :, :, :, lanes], from_core.at[i % CORE_RING, :, :, :, lanes],
                      c_send.at[i], c_recv.at[i], at.over_core)

    def first_copy(i, w):
        f, s, first, second, slot = places(i)
        lanes = pl.ds(0, w)
        return remote(part.at[slot, at.core, 1 - f, :, :, lanes], from_first.at[i % LINK_RING, :, :, lanes],
                      f_send.at[i], f_recv.at[i], first)

    def second_copy(i, w):
        f, s, first, second, slot = places(i)
        lanes = pl.ds(0, w)
        return remote(part.at[slot, at.core, f, 1 - s, :, lanes], from_second.at[i % LINK_RING, :, lanes],
                      s_send.at[i], s_recv.at[i], second)

    def out_copy(i, w):
        lanes = pl.ds(0, w)
        return remote(total_ref.at[i, :, lanes], from_near.at[i % LINK_RING, :, lanes], n_send.at[i], n_recv.at[i], at.near)

    def far_copy(i, w):
        lanes = pl.ds(0, w)
        return remote(total_ref.at[i, :, lanes], from_far.at[i % LINK_RING, :, lanes], m_send.at[i], m_recv.at[i], at.far)

    def plus(a, b):
        return a + b

    def put(cols, rows_of):
        even = 1 - tick % 2
        for j in range(8):
            c, x, y = j % 2, (j // 2) % 2, j // 4
            a = x * even + y * (1 - even)
            b = y * even + x * (1 - even)
            part[tick % RING, c, a, b, :, cols] = rows_of[j * block : (j + 1) * block].astype(BF16)

    @pl.when(attending)
    def _():
        left = (per_group * g + spot) // (n_mlp // 2)
        put(slice(0, CHUNK), nn(left_mlp[left], mlp_ref[...]))
        core_copy(tick, CHUNK).start()

    def rest(s, e):
        put(slice(e * PIECE, (e + 1) * PIECE), nn(left_rest[s // (3 * groups)], rhs[s]))

    @pl.when((tick < n_wide) & jnp.logical_not(attending))
    def _():
        late = tick // busy
        j = (tick // period) * (1 - late) + (tick - n_mlp) * late
        for e in range(2):
            rest(2 * j + e, e)
        core_copy(tick, CHUNK).start()

    @pl.when((tick >= n_wide) & (tick < chunks))
    def _():
        rest(tick - n_wide + 2 * (n_wide - n_mlp), 0)
        core_copy(tick, PIECE).start()

    def when(lag, f):
        i = tick - lag

        @pl.when((i >= 0) & (i < n_wide))
        def _():
            f(i, CHUNK)

        @pl.when((i >= n_wide) & (i < chunks))
        def _():
            f(i, PIECE)

    def core_step(i, w):
        f, s, first, second, slot = places(i)
        core_copy(i, w).wait()
        for a in range(2):
            for b in range(2):
                part[slot, at.core, a, b, :, :w] = plus(part[slot, at.core, a, b, :, :w], from_core[i % CORE_RING, a, b, :, :w])
        first_copy(i, w).start()

    def first_step(i, w):
        f, s, first, second, slot = places(i)
        first_copy(i, w).wait()
        for b in range(2):
            part[slot, at.core, f, b, :, :w] = plus(part[slot, at.core, f, b, :, :w], from_first[i % LINK_RING, b, :, :w])
        second_copy(i, w).start()

    def second_step(i, w):
        f, s, first, second, slot = places(i)
        second_copy(i, w).wait()
        total_ref[i, :, :w] = plus(part[slot, at.core, f, s, :, :w], from_second[i % LINK_RING, :, :w])

        @pl.when(at.inner == 0)
        def _():
            out_copy(i, w).start()

    def near_step(i, w):
        @pl.when(at.inner == 1)
        def _():
            out_copy(i, w).wait_recv()
            total_ref[i, :, :w] = plus(total_ref[i, :, :w], from_near[i % LINK_RING, :, :w])
            far_copy(i, w).start()

    def far_step(i, w):
        @pl.when(at.inner == 1)
        def _():
            far_copy(i, w).wait()
            total_ref[i, :, :w] = plus(total_ref[i, :, :w], from_far[i % LINK_RING, :, :w])
            out_copy(i, w).start()

        @pl.when(at.inner == 0)
        def _():
            out_copy(i, w).wait_send()

    def back_step(i, w):
        @pl.when(at.inner == 0)
        def _():
            out_copy(i, w).wait_recv()
            total_ref[i, :, :w] = from_near[i % LINK_RING, :, :w]

        @pl.when(at.inner == 1)
        def _():
            out_copy(i, w).wait_send()

    when(LAGS["core"], core_step)
    when(LAGS["first"], first_step)
    when(LAGS["second"], second_step)
    when(LAGS["z"], near_step)
    when(LAGS["mid"], far_step)
    when(LAGS["back"], back_step)

    each = range(GROUP)

    def unit(b):
        part = rows // 2
        blocks = [(h, b * rows + j * part) for j in range(2) for h in each]
        context, dq, dk, dv = attend([q_ref[h, t : t + part, :] for h, t in blocks], [k_ref[h, : t + part, :] for h, t in blocks],
                                     [v_ref[h, : t + part, :] for h, t in blocks], [gc_ref[h, t : t + part, :] for h, t in blocks],
                                     [begin_ref[t : t + part, :] for h, t in blocks], [t for h, t in blocks])
        for i, (h, t) in enumerate(blocks):
            cols, mine = slice(h * PAIR, (h + 1) * PAIR), slice(t, t + part)
            dk_acc[h, : t + part, :] += dk[i]
            dv_acc[h, : t + part, :] += dv[i]
            ctx[g, mine, cols] = context[i]
            left_rest[1, pl.ds(pl.multiple_of(g * PIECE + h * PAIR, PAIR), PAIR), mine] = context[i].T
            rhs[3 * g, mine, cols] = (dq[i] * cos_ref[mine, :] - turned(dq[i]) * sin_ref[mine, :]).astype(BF16)

    @pl.when(attending & (spot == 0))
    def _():
        dk_acc[...] = jnp.zeros_like(dk_acc)
        dv_acc[...] = jnp.zeros_like(dv_acc)

    for b in range(per_group):
        @pl.when(attending & (spot == b))
        def _():
            unit(b)

    @pl.when(attending & (spot == per_group - 1))
    def _():
        for h in each:
            cols = slice(h * PAIR, (h + 1) * PAIR)
            dk = dk_acc[h]
            rhs[3 * g + 1, :, cols] = (dk * cos_ref[...] - turned(dk) * sin_ref[...]).astype(BF16)
            rhs[3 * g + 2, :, cols] = dv_acc[h].astype(BF16)

    row_at = chunks - 2

    @pl.when((tick >= row_at) & (tick < row_at + row_ticks))
    def _():
        n_rows = x_ref.shape[0]
        here = pl.ds(pl.multiple_of((tick - row_at) * n_rows, n_rows), n_rows)
        attn = base_ref[...]
        for j in range(groups):
            attn = attn + nn(ctx[j, here, :], wout_ref[j * PIECE : (j + 1) * PIECE, :])
        out_ref[...] = attn.astype(BF16)
        g1 = jnp.zeros(attn.shape, F32)
        for s in range(3 * groups):
            cols = slice((s % 3) * width + (s // 3) * PIECE, (s % 3) * width + (s // 3 + 1) * PIECE)
            grads = rhs[s, here, :]
            g1 = g1 + nt(grads, wqkv_ref[:, cols])
            bqkv[:, cols] += jnp.sum(grads.astype(F32), axis=0, keepdims=True)
        x = x_ref[...].astype(F32)
        centred = x - jnp.mean(x, axis=1, keepdims=True)
        r = lax.rsqrt(jnp.mean(centred * centred, axis=1, keepdims=True) + EPSILON)
        n = centred * r
        gain1[...] += jnp.sum(g1 * n, axis=0, keepdims=True)
        shift1[...] += jnp.sum(g1, axis=0, keepdims=True)
        t = g1 * g1_ref[...].reshape(1, -1) + t2_ref[...]
        dx = r * (t - jnp.mean(t, axis=1, keepdims=True) - n * jnp.mean(t * n, axis=1, keepdims=True))
        gl = jnp.concatenate([rhs[3 * groups + j, here, :] for j in range(groups)], axis=1)
        ig_ref[...] = (gl.astype(F32) + dx).astype(BF16)

    def lines(ref):
        return [ref[:, j : j + width] for j in range(0, ref.shape[1], width)]

    early = Everywhere(at, dp_e, rows_e, e_send, e_recv)
    late = Everywhere(at, dp_l, rows_l, l_send, l_recv)
    row = jnp.full((1, width), count_ref[0].astype(F32), F32)

    @pl.when(tick == 1)
    def _():
        early.begin(lines(bup_ref) + lines(bout_ref) + lines(gain2_ref) + lines(shift2_ref) + [row])

    @pl.when(tick == 4)
    def _():
        early.turn()

    @pl.when(tick == 7)
    def _():
        vec_ref[0] = early.end()

    begin = row_at + row_ticks

    @pl.when(tick == begin)
    def _():
        late.begin(lines(gain1) + lines(shift1) + lines(bqkv) + [jnp.zeros((3, width), F32)])

    @pl.when(tick == begin + 2)
    def _():
        late.turn()

    @pl.when(tick == begin + 4)
    def _():
        vec_ref[1] = late.end()


def back(count, begins, mlp, q, k, v, gc, x, base, t2, cosine, sine, g1, gain2, shift2, bup, bout, n2t, glt, n1t, gl, wout, wqkv,
         rows=256):
    length, width = x.shape
    ff = bup.shape[1]
    block = width // 8
    groups = width // PIECE
    n_mlp, pieces = 2 * ff // CHUNK, 4 * groups
    chunks = n_mlp + pieces // 3 + pieces - 2 * (pieces // 3)
    row_ticks = length // rows
    period = row_ticks + 1
    busy = groups * period
    ticks = max(chunks + LAGS["back"], chunks - 2 + row_ticks + 5)

    def row(cols):
        return pl.BlockSpec((rows, cols), lambda t: (jnp.clip(t - (chunks - 2), 0, row_ticks - 1), 0))

    def whole(a):
        return pl.BlockSpec(a.shape, lambda t: (0,) * a.ndim, pipeline_mode=pl.Buffered(1))

    def mlp_cols(t):
        return (0, jnp.minimum(row_ticks * (t // period) + jnp.minimum(t % period, row_ticks - 1), n_mlp - 1))

    heads = pl.BlockSpec((GROUP, length, PAIR), lambda t: (jnp.minimum(t // period, groups - 1), 0, 0))
    s = jax.ShapeDtypeStruct
    dma = pltpu.SemaphoreType.DMA
    loaded = (n2t, glt, n1t, gl, wout, wqkv)
    return pl.pallas_call(
        functools.partial(back_body, rows=rows, row_ticks=row_ticks),
        grid=(ticks,),
        in_specs=[pl.BlockSpec(memory_space=pltpu.SMEM), whole(begins), pl.BlockSpec((length, CHUNK), mlp_cols)]
        + [heads] * 4 + [row(width)] * 3
        + [whole(a) for a in (cosine, sine, g1, gain2, shift2, bup, bout)] + [pl.BlockSpec(memory_space=pl.ANY)] * len(loaded),
        out_specs=[row(width), row(width),
                   pl.BlockSpec((chunks, block, CHUNK), lambda t: (0, 0, 0), pipeline_mode=pl.Buffered(1)),
                   pl.BlockSpec((2, 8, width), lambda t: (0, 0, 0), pipeline_mode=pl.Buffered(1))],
        out_shape=[s((length, width), BF16), s((length, width), BF16), s((chunks, block, CHUNK), BF16), s((2, 8, width), F32)],
        scratch_shapes=[
            pltpu.VMEM((2, width, length), BF16),
            pltpu.VMEM((2, width, length), BF16),
            pltpu.VMEM((4 * groups, length, PIECE), BF16),
            pltpu.VMEM(wout.shape, BF16),
            pltpu.VMEM(wqkv.shape, BF16),
            dma((len(loaded),)),
            pltpu.VMEM((groups, length, PIECE), BF16),
            pltpu.VMEM((GROUP, length, PAIR), F32),
            pltpu.VMEM((GROUP, length, PAIR), F32),
            pltpu.VMEM((RING, 2, 2, 2, block, CHUNK), BF16),
            pltpu.VMEM((CORE_RING, 2, 2, block, CHUNK), BF16),
            pltpu.VMEM((LINK_RING, 2, block, CHUNK), BF16),
            pltpu.VMEM((LINK_RING, block, CHUNK), BF16),
            pltpu.VMEM((LINK_RING, block, CHUNK), BF16),
            pltpu.VMEM((LINK_RING, block, CHUNK), BF16),
        ] + [dma((chunks,))] * 10 + [
            pltpu.VMEM((8, 8, width), F32), pltpu.VMEM((4, 8, width), F32),
            pltpu.VMEM((8, 8, width), F32), pltpu.VMEM((4, 8, width), F32),
            dma((12,)), dma((12,)), dma((12,)), dma((12,)),
            pltpu.VMEM((1, width), F32), pltpu.VMEM((1, width), F32), pltpu.VMEM((1, 3 * width), F32),
        ],
        compiler_params=pltpu.CompilerParams(vmem_limit_bytes=60 * 2**20, collective_id=0, has_side_effects=True),
        name="back",
    )(count, begins, mlp, q, k, v, gc, x, base, t2, cosine, sine, g1, gain2, shift2, bup, bout, *loaded)


def finish_body(out_hbm, ig_hbm, total_hbm, vec_ref, out_to, ig_to, up_to, down_to, low_to, qkv_to,
                gain1_ref, shift1_ref, bqkv_ref, bout_ref, gain2_ref, shift2_ref, bup_ref, bdown_ref,
                held, total_ref, up_ref, down_ref, low_ref, qkv_ref, sem):
    load = pltpu.make_async_copy(total_hbm, total_ref, sem.at[0])
    load.start()
    takes = [pltpu.make_async_copy(a, held.at[j], sem.at[1 + j]) for j, a in enumerate((out_hbm, ig_hbm))]
    copies = [pltpu.make_async_copy(held.at[j], a, sem.at[3 + j]) for j, a in enumerate((out_to, ig_to))]
    for take in takes:
        take.start()
    width, ff = gain1_ref.shape[0], bup_ref.shape[0]
    factor = 1.0 / vec_ref[0, 7:8, 0:1]
    groups = width // PIECE
    n_up = ff // CHUNK
    load.wait()

    def put(kinds):
        for i in range(total_ref.shape[0]):
            kind, *what = chunk_columns(i, 2 * n_up, 4 * groups, 2 * n_up // groups)
            if kind not in kinds or (kind == "mlp" and what[0] // n_up != kinds[kind]):
                continue
            if kind == "mlp":
                ref, j = (up_ref, down_ref)[kinds[kind]], what[0] % n_up
                ref[:, j * CHUNK : (j + 1) * CHUNK] = total_ref[i].astype(F32) * factor
                continue
            for e, s in enumerate(what):
                ref, col = (qkv_ref, (s % 3) * width + (s // 3) * PIECE) if s < 3 * groups else (low_ref, (s - 3 * groups) * PIECE)
                ref[:, col : col + PIECE] = total_ref[i, :, e * PIECE : (e + 1) * PIECE].astype(F32) * factor

    results = []

    def send(ref, to):
        results.append(pltpu.make_async_copy(ref, to, sem.at[5 + len(results)]))
        results[-1].start()

    put({"mlp": 0})
    send(up_ref, up_to)
    for take, copy in zip(takes, copies):
        take.wait()
        copy.start()
    put({"mlp": 1})
    send(down_ref, down_to)
    put({"rest": 0})
    send(low_ref, low_to)
    send(qkv_ref, qkv_to)
    first, second = vec_ref[0] * factor, vec_ref[1] * factor
    for j in range(ff // width):
        bup_ref[j * width : (j + 1) * width] = first[j]
    j = ff // width
    for ref, line in ((bout_ref, first[j]), (bdown_ref, first[j]), (gain2_ref, first[j + 1]), (shift2_ref, first[j + 2]),
                      (gain1_ref, second[0]), (shift1_ref, second[1])):
        ref[...] = line
    for j in range(3):
        bqkv_ref[j * width : (j + 1) * width] = second[2 + j]
    for copy in copies + results:
        copy.wait()


def finish(out, ig, total, vec, ff):
    length, width = out.shape
    block = total.shape[1]
    s = jax.ShapeDtypeStruct
    hbm, vmem = pl.BlockSpec(memory_space=pltpu.HBM), pl.BlockSpec(memory_space=pltpu.VMEM)
    vectors = (width, width, 3 * width, width, width, width, ff, width)
    grads = [(block, ff), (block, ff), (block, width), (block, 3 * width)]
    return pl.pallas_call(
        finish_body,
        in_specs=[hbm, hbm, hbm, vmem],
        out_specs=[hbm] * 6 + [vmem] * 8,
        out_shape=[s(out.shape, BF16), s(ig.shape, BF16)] + [s(shape, F32) for shape in grads] + [s((n,), F32) for n in vectors],
        scratch_shapes=[pltpu.VMEM((2, length, width), BF16), pltpu.VMEM(total.shape, BF16)]
        + [pltpu.VMEM(shape, F32) for shape in grads] + [pltpu.SemaphoreType.DMA((9,))],
        compiler_params=pltpu.CompilerParams(vmem_limit_bytes=60 * 2**20),
        name="finish",
    )(out, ig, total, vec)


def by_collectives(segment, count, begins, mlp, q, k, v, gc, x, base, t2, cosine, sine, g1, gain2, shift2, bup, bout, n2t, glt, n1t, gl,
                   wout, wqkv):
    width, ff = x.shape[1], bup.shape[1]
    ctx, ctxt, gu = attention(q, k, v, gc, segment, cosine, sine)
    flat = jnp.concatenate([gu[0], gu[1], gu[2]], axis=1)
    low = jnp.concatenate(list(gl), axis=1)
    out = (base + nn(ctx, wout)).astype(BF16)
    grad_one = nt(flat, wqkv)
    x = x.astype(F32)
    centred = x - jnp.mean(x, axis=1, keepdims=True)
    r = lax.rsqrt(jnp.mean(centred * centred, axis=1, keepdims=True) + EPSILON)
    n = centred * r
    t = grad_one * g1 + t2
    dx = r * (t - jnp.mean(t, axis=1, keepdims=True) - n * jnp.mean(t * n, axis=1, keepdims=True))
    input_grad = (low.astype(F32) + dx).astype(BF16)
    packed = jnp.concatenate([bup[0], bout[0], gain2[0], shift2[0], jnp.full(width, count[0].astype(F32)),
                              jnp.sum(grad_one * n, axis=0), jnp.sum(grad_one, axis=0), jnp.sum(flat, axis=0, dtype=F32),
                              jnp.zeros(3 * width, F32)])
    packed = lax.psum(packed, ("dp", "rows"))
    mlp_part = jnp.concatenate([nn(n2t, mlp[:, :ff]), nn(glt, mlp[:, ff:])], axis=1)
    rest = [nn(n1t, gu[s % 3, :, (s // 3) * PIECE : (s // 3 + 1) * PIECE]) for s in range(3 * width // PIECE)]
    rest = jnp.concatenate(rest + [nn(ctxt, low)], axis=1)
    columns, n_mlp, pieces = [], 2 * ff // CHUNK, 4 * width // PIECE
    for i in range(n_mlp + pieces // 3 + pieces - 2 * (pieces // 3)):
        kind, *what = chunk_columns(i, n_mlp, pieces, n_mlp * PIECE // width)
        held = mlp_part if kind == "mlp" else rest
        begin, size = (what[0] * CHUNK, CHUNK) if kind == "mlp" else (what[0] * PIECE, len(what) * PIECE)
        columns.append(jnp.pad(held[:, begin : begin + size], ((0, 0), (0, CHUNK - size))))
    part = jnp.stack(columns, axis=1).astype(BF16)
    grads = lax.psum(lax.psum_scatter(part, "dp", scatter_dimension=0, tiled=True), "rows")
    return out, input_grad, jnp.swapaxes(grads, 0, 1), packed.reshape(2, 8, width)


def shards(tokens, segment_ids, true_counts, regroup, cotangent, ln1_gain, ln1_bias, qkv_weight, qkv_bias, out_weight,
           out_bias, ln2_gain, ln2_bias, up_weight, up_bias, down_weight, down_bias):
    length, width = cotangent.shape
    ff = up_weight.shape[1]
    cosine, sine = (jnp.asarray(t) for t in rotary_tables(length))
    (arrived, q, k, v, gc, n1t, n2t, glt, gl, mlp, base, t2, gain2, shift2, bias_up, bias_out, begins) = front(
        true_counts, regroup, segment_ids, tokens, cotangent, cosine, sine, ln1_gain, ln1_bias, qkv_weight, qkv_bias, out_weight, out_bias,
        ln2_gain, ln2_bias, up_weight, up_bias, down_weight, down_bias)
    last = back if (lax.axis_size("dp"), lax.axis_size("rows")) == (8, 4) else functools.partial(by_collectives, segment_ids)
    out, input_grad, total, vec = last(true_counts, begins, mlp, q, k, v, gc, arrived, base, t2, cosine, sine, ln1_gain, gain2,
                                       shift2, bias_up, bias_out, n2t, glt, n1t, gl, out_weight, qkv_weight)
    (out, input_grad, up, down, low, qkv, gain1, shift1, bias_qkv, bias_out, gain2, shift2, bias_up, bias_down) = finish(
        out, input_grad, total, vec, up_weight.shape[1])
    return (out, input_grad, gain1, shift1, qkv, bias_qkv, low, bias_out, gain2, shift2, up, bias_up, down.T, bias_down)


def solution(mesh):
    both = ("dp", "rows")
    placed = (P(both, None), P(both), P(both), P(both), P(both, None)) + (P(),) * 12
    return jax.shard_map(
        shards, mesh=mesh, in_specs=placed,
        out_specs=(P(both, None), P(both, None), P(), P(), P("dp", None), P(), P("dp", None), P(), P(), P(), P("dp", None), P(),
                   P(None, "dp"), P()),
        check_vma=False)
```
